32 devices in a mesh: replica: 2 (over x), section: 16 (over z, y, core).
Axes of the slice: x: 2, y: 2, z: 4, core: 2. Of those that a mesh axis runs over, the one named last changes fastest.
Arguments:
- prompt_states: bfloat16 [16384, 8192], P(('replica', 'section')), parts along dimension 0, may hold values from -60 to 60
- kv_weight: bfloat16 [8192, 1024], P('section'), may hold values from -0.0625 to 0.0625
- image_owner: int32 [256], P(('replica', 'section')), parts along dimension 0, may hold values from 0 to 15, as said below
- image_row: int32 [256], P(('replica', 'section')), parts along dimension 0, may hold values from 0 to 7
- queries: bfloat16 [256, 4096], P(('replica', 'section')), parts along dimension 0, may hold values from -100 to 100
- cache: bfloat16 [256, 256, 1024], P(('replica', 'section')), parts along dimension 0, may hold values from -6 to 6
- context_length: int32 [256], P(('replica', 'section')), parts along dimension 0, may hold values from 2 to 256, as said below
Outputs:
- attended: bfloat16 [256, 4096], P(('replica', 'section')), parts along dimension 0
The draws below stay inside these ranges and needn't reach their ends.
There are 2 independent parts, one for each index of `replica`. The reference program is written for one: setup_inputs(seed, part) draws one part's arguments, and reference() takes and returns one part's arrays. A program takes and returns all parts, laid end to end along the dimension named above; an argument that names none is the same for every part. Nothing has to cross between parts.
Inputs may be any that keep to these rules, and one draw needn't show every extreme that they name: `image_owner`: the images of one device go to distinct owners; some owner receives one image from every device. `context_length`: every device holds a row with all 256 positions live.
All inputs are finite; a program needn't handle non-finite values.
Results may differ from the reference program's by a relative error of at most 0.005.
Values may be sent and summed in bfloat16 or wider, within the bound.
No kernel may reach another device: no remote copies, remote signals or barrier semaphores. Data moves between devices by JAX's collectives and lax.ppermute only.
A program may use at most 128 MiB of HBM per device.

```python
import math
import jax
import jax.numpy as jnp
from jax import lax

D = 8192
HD = 128
KVH = 4
QH = 32
IMG_TOK = 64
IMG_DEV = 8
RD = 8
CTX = 256
KVW = 1024
QW = 4096
ROWS = 128
IMAGES = 128
PTOK = 8192
N_SECTION = 16


def lead_keys(key):
    values = jax.random.normal(jax.random.fold_in(key, 77), (ROWS, KVH * HD), jnp.float32)
    return jnp.clip(values, -5.0, 5.0)


def draw_prompt_states(key, part):
    key = jax.random.fold_in(key, 11)
    first, second = jax.random.split(key)
    base = jnp.clip(jax.random.normal(first, (PTOK, D), jnp.float32), -6.0, 6.0)
    spread = jnp.exp(jax.random.uniform(second, (PTOK, 1), jnp.float32, 0.0, 2.3))
    return (base * spread).astype(jnp.bfloat16)


def draw_image_owner(key, part):
    key = jax.random.fold_in(key, 21)
    first, second, third = jax.random.split(key, 3)
    favored = jax.random.randint(first, (), 0, N_SECTION)
    owner_ids = jnp.arange(N_SECTION, dtype=jnp.int32)
    bias = jax.random.randint(second, (N_SECTION,), 0, 4)
    bias = jnp.where(owner_ids == favored, 8, bias)
    noise = jax.random.randint(third, (N_SECTION, N_SECTION), 0, 1024)
    scores = (bias[None, :] * 1024 + noise) * N_SECTION + owner_ids[None, :]
    top_scores, picked = lax.top_k(scores, IMG_DEV)
    return picked.reshape(IMAGES).astype(jnp.int32)


def draw_queries(key, part):
    key = jax.random.fold_in(key, 5)
    values = jnp.clip(jax.random.normal(key, (ROWS, QW), jnp.float32) * 1.5, -9.0, 9.0)
    return values.astype(jnp.bfloat16)


def draw_cache(key, part):
    leading = lead_keys(key)
    key = jax.random.fold_in(key, 3)
    values = jnp.clip(jax.random.normal(key, (ROWS, CTX, KVW), jnp.float32), -6.0, 6.0)
    values = values.at[:, 0, :KVH * HD].set(leading)
    return values.astype(jnp.bfloat16)


def draw_context_length(key, part):
    key = jax.random.fold_in(key, 9)
    first, second = jax.random.split(key)
    lengths = jax.random.randint(first, (ROWS,), 2, CTX + 1)
    full_at = jax.random.randint(second, (ROWS // RD,), 0, RD)
    is_full = (jnp.arange(RD)[None, :] == full_at[:, None]).reshape(ROWS)
    return jnp.where(is_full, CTX, lengths).astype(jnp.int32)


def with_ends(drawn, key, smallest, top_value):
    place = [jax.random.randint(jax.random.fold_in(key, axis), (), 0, length) for axis, length in enumerate(drawn.shape)]
    widest = drawn.shape.index(max(drawn.shape))
    neighbour = place[:widest] + [(place[widest] + 1) % drawn.shape[widest]] + place[widest + 1:]
    return drawn.at[tuple(place)].set(smallest).at[tuple(neighbour)].set(top_value)


def level_of(stream_key, dims, shards, smallest, top_value):
    gain = 1.0
    for dim, parts in shards:
        steps = jax.random.uniform(jax.random.fold_in(jax.random.fold_in(stream_key, 6), dim), (parts,), jnp.float32, smallest / len(shards), top_value / len(shards))
        gain = gain * jnp.repeat(jnp.exp(steps), dims[dim] // parts).reshape((-1,) + (1,) * (len(dims) - 1 - dim))
    return gain


def centred(rng, dims, scale, limit, shards=(), kind=jnp.bfloat16):
    values = scale * jax.random.normal(rng, dims, jnp.float32)
    if shards:
        values = values * level_of(rng, dims, shards, -0.22, 0.18)
    return jnp.clip(values, -limit, limit).astype(kind)


def setup_inputs(seed: int = 0, part: int = 0) -> dict:
    streams_of = jax.random.split(jax.random.key(seed), 8)
    own_keys = jax.random.split(jax.random.fold_in(streams_of[7], part), 8)
    return {
        "prompt_states": draw_prompt_states(jax.random.fold_in(jax.random.fold_in(streams_of[7], part), 71), part),
        "kv_weight": centred(streams_of[1], (D, KVW), D ** -0.5, 0.0625, ((0, 16),)),
        "image_owner": draw_image_owner(jax.random.fold_in(jax.random.fold_in(streams_of[7], part), 71), part),
        "image_row": with_ends(jax.random.randint(own_keys[3], (IMAGES,), 0, RD), jax.random.fold_in(own_keys[3], 1), 0, RD - 1).astype(jnp.int32),
        "queries": draw_queries(jax.random.fold_in(jax.random.fold_in(streams_of[7], part), 71), part),
        "cache": draw_cache(jax.random.fold_in(jax.random.fold_in(streams_of[7], part), 71), part),
        "context_length": draw_context_length(jax.random.fold_in(jax.random.fold_in(streams_of[7], part), 71), part),
    }


def normalize_rows(states):
    values = states.astype(jnp.float32)
    return values * lax.rsqrt(lax.optimization_barrier(jnp.mean(values * values, axis=-1, keepdims=True)) + 1e-05)

def settle(values):
    return lax.optimization_barrier(values.astype(jnp.bfloat16)).astype(jnp.float32)

def reference(prompt_states, kv_weight, image_owner, image_row, queries, cache, context_length):
    group_size = QH // KVH
    key_width = KVH * HD
    score_scale = 1.0 / math.sqrt(HD)
    normed = normalize_rows(prompt_states).astype(jnp.bfloat16)
    new_kv = settle(jnp.dot(normed, kv_weight, preferred_element_type=jnp.float32))
    new_keys = new_kv[:, :key_width].reshape(IMAGES, IMG_TOK, KVH, HD)
    new_vals = new_kv[:, key_width:].reshape(IMAGES, IMG_TOK, KVH, HD)
    image_target = (image_owner * RD + image_row).astype(jnp.int32)
    image_queries = queries[image_target].astype(jnp.float32).reshape(IMAGES, KVH, group_size, HD)
    image_scores = jnp.einsum('ikgd,imkd->ikgm', image_queries, new_keys) * score_scale
    image_max = lax.optimization_barrier(jnp.max(image_scores, axis=-1))

    def one_row(row_index):
        query_row = lax.dynamic_index_in_dim(queries, row_index, 0, keepdims=False)
        query_row = query_row.astype(jnp.float32).reshape(KVH, group_size, HD)
        cache_row = lax.dynamic_index_in_dim(cache, row_index, 0, keepdims=False).astype(jnp.float32)
        res_keys = cache_row[:, :key_width].reshape(CTX, KVH, HD)
        res_vals = cache_row[:, key_width:].reshape(CTX, KVH, HD)
        row_length = lax.dynamic_index_in_dim(context_length, row_index, 0, keepdims=False)
        res_live = (jnp.arange(CTX, dtype=jnp.int32) < row_length)[None, None, :]
        res_scores = jnp.einsum('kgd,tkd->kgt', query_row, res_keys) * score_scale
        res_scores = jnp.where(res_live, res_scores, -1e+30)
        mine = (image_target == row_index)[:, None, None]
        new_top = lax.optimization_barrier(jnp.max(jnp.where(mine, image_max, -1e+30), axis=0))
        row_top = jnp.maximum(lax.optimization_barrier(jnp.max(res_scores, axis=-1)), new_top)
        res_w = jnp.where(res_live, jnp.exp(res_scores - row_top[..., None]), 0.0)
        res_den = lax.optimization_barrier(jnp.sum(res_w, axis=-1))
        res_sum = jnp.einsum('kgt,tkd->kgd', settle(res_w), res_vals)
        return (row_top, res_sum, res_den)
    row_top, res_sum, res_den = lax.map(one_row, jnp.arange(ROWS, dtype=jnp.int32))
    image_w = jnp.exp(image_scores - row_top[image_target][..., None])
    image_den = lax.optimization_barrier(jnp.sum(image_w, axis=-1))
    image_sum = jnp.einsum('ikgm,imkd->ikgd', settle(image_w), new_vals)
    new_den = jax.ops.segment_sum(image_den, image_target, num_segments=ROWS)
    new_sum = jax.ops.segment_sum(image_sum, image_target, num_segments=ROWS)
    out = (res_sum + new_sum) / (res_den + new_den)[..., None]
    return out.reshape(ROWS, QH * HD).astype(jnp.bfloat16)
```

```python
import functools
import math

import jax
import jax.numpy as jnp
from jax import lax
from jax.experimental import pallas as pl
from jax.experimental.pallas import tpu as pltpu
from jax.sharding import PartitionSpec as P

HD = 128
KVH = 4
QH = 32
IMG_TOK = 64
GROUP = QH // KVH
HALF_KVH = KVH // 2
HALF_QH = QH // 2
SCALE = 1.0 / math.sqrt(HD)

masked_score = -1e30


def normalize_rows(states):
    values = states.astype(jnp.float32)
    return values * lax.rsqrt(jnp.mean(values * values, axis=-1, keepdims=True) + 1e-05)


def swap_core(x, n):
    return lax.ppermute(x, "section", [(i, i ^ 1) for i in range(n)])


def swap_replica(x):
    count = lax.axis_size("replica")
    return lax.ppermute(x, "replica", [(i, i ^ 1) for i in range(count)])


def same_core_groups(n):
    return [list(range(core, n, 2)) for core in range(2)]


def gather_plain(chunk, n):
    chip_rows = chunk.shape[0]
    whole = lax.all_gather(chunk, "section", axis=0, tiled=True, axis_index_groups=same_core_groups(n))
    return [(whole, chip * chip_rows, chip_rows, chip, 0) for chip in range(n // 2)]


def gather_grid(chunk, span, z, y, rep):
    rows = chunk.shape[0]
    rest = rows - span
    order = [0, 1, 3, 2]
    ring = [
        (order[p] * 4 + low, order[(p + 1) % 4] * 4 + low) for p in range(4) for low in range(4)
    ]
    swap_y = [(i, i ^ 2) for i in range(16)]
    places = jnp.array([0, 1, 3, 2], jnp.int32)
    place = places[z]
    mine = lax.dynamic_slice_in_dim(chunk, rep * rest, span, 0)
    along_z = [mine]
    along_y = []
    for step in range(4):
        if step < 3:
            along_z.append(lax.ppermute(along_z[-1], "section", ring))
        along_y.append(lax.ppermute(along_z[step], "section", swap_y))
    pieces = [(chunk, 0, rows, z * 2 + y, 0)]
    for step in range(4):
        from_z = places[(place - step) % 4]
        for piece, chip in ((along_z[step], from_z * 2 + y), (along_y[step], from_z * 2 + 1 - y)):
            if piece is mine:
                continue
            if rest == span:
                extra = swap_replica(piece)
            else:
                extra = swap_replica(lax.dynamic_slice_in_dim(piece, rep * (span - rest), rest, 0))
            pieces.append((piece, 0, span, chip, rep * rest))
            pieces.append((extra, 0, rest, chip, (1 - rep) * span))
    return pieces


def granules(pieces, rows_dev, core, size):
    arrays, layout, offsets = [], [], []
    for array, start, rows, chip, first in pieces:
        at = [i for i, known in enumerate(arrays) if known is array]
        if not at:
            arrays.append(array)
            at = [len(arrays) - 1]
        for part in range(rows // size):
            row = first + part * size
            half = row // rows_dev
            place = (half + core) % 2 * rows_dev + row % rows_dev
            layout.append((at[0], start + part * size))
            offsets.append(jnp.asarray(chip * 2 * rows_dev + place, jnp.int32))
    return arrays, layout, jnp.stack(offsets)


def project(layout, size, offsets_ref, own_ref, other_ref, piece_refs, weight, total, sems):
    step = pl.program_id(0)
    tokens, depth = own_ref.shape

    @pl.when(step == 0)
    def _():
        copies = [
            pltpu.make_async_copy(
                piece_refs[which].at[pl.ds(start, size)],
                weight.at[pl.ds(pl.multiple_of(offsets_ref[i], size), size)],
                sems.at[i],
            )
            for i, (which, start) in enumerate(layout)
        ]
        for copy in copies:
            copy.start()
        total[...] = jnp.zeros_like(total)
        for copy in copies:
            copy.wait()

    block = weight[pl.ds(pl.multiple_of(step * depth, depth), depth), :]
    total[:tokens, :] += jnp.dot(own_ref[...], block, preferred_element_type=jnp.float32)
    total[tokens:, :] += jnp.dot(other_ref[...], block, preferred_element_type=jnp.float32)


def key_kernel(layout, size, n_pieces, offsets_ref, own_ref, other_ref, query_ref, *refs):
    piece_refs = refs[:n_pieces]
    weights_ref, max_ref, sum_ref, weight, total, sems = refs[n_pieces:]
    project(layout, size, offsets_ref, own_ref, other_ref, piece_refs, weight, total, sems)

    @pl.when(pl.program_id(0) == pl.num_programs(0) - 1)
    def _():
        tokens = total.shape[0]
        queries = query_ref.shape[1]
        image_of_query = lax.broadcasted_iota(jnp.int32, (queries, tokens), 0) // GROUP
        image_of_token = lax.broadcasted_iota(jnp.int32, (queries, tokens), 1) // IMG_TOK
        live = image_of_query == image_of_token
        for head in range(HALF_KVH):
            keys = total[:, head * HD : (head + 1) * HD].astype(jnp.bfloat16)
            scores = (
                lax.dot_general(
                    query_ref[head], keys, (((1,), (1,)), ((), ())), preferred_element_type=jnp.float32
                )
                * SCALE
            )
            scores = jnp.where(live, scores, masked_score)
            top = jnp.max(scores, axis=1, keepdims=True)
            weights = jnp.where(live, jnp.exp(scores - top), 0.0)
            weights_ref[head] = weights.astype(jnp.bfloat16)
            max_ref[head] = jnp.broadcast_to(top, (queries, HD))
            sum_ref[head] = jnp.broadcast_to(jnp.sum(weights, axis=1, keepdims=True), (queries, HD))


def value_kernel(layout, size, n_pieces, offsets_ref, slot_ref, own_ref, other_ref, weights_ref, *refs):
    piece_refs = refs[:n_pieces]
    slots_ref, weight, total, summed, sems = refs[n_pieces:]
    project(layout, size, offsets_ref, own_ref, other_ref, piece_refs, weight, total, sems)

    @pl.when(pl.program_id(0) == pl.num_programs(0) - 1)
    def _():
        slots_ref[...] = jnp.zeros_like(slots_ref)
        images = weights_ref.shape[1] // GROUP
        for head in range(HALF_KVH):
            values = total[:, head * HD : (head + 1) * HD].astype(jnp.bfloat16)
            out = jnp.dot(weights_ref[head], values, preferred_element_type=jnp.float32)
            summed[:, head * GROUP : (head + 1) * GROUP, :] = out.reshape(images, GROUP, HD)
        for image in range(images):
            slots_ref[slot_ref[image]] = summed[image].astype(jnp.bfloat16)


def combine_kernel(row_ref, got_ref, factor_ref, base_ref, out_ref, acc):
    acc[...] = base_ref[...]
    images = factor_ref.shape[0]

    def add(image, carry):
        row = row_ref[image]
        chip, which = image // 2, image % 2
        for core in range(2):
            part = pl.ds(core * HALF_QH, HALF_QH)
            acc[row, part, :] += factor_ref[image, part, :] * got_ref[
                (chip * 2 + core) * 2 + which
            ].astype(jnp.float32)
        return carry

    lax.fori_loop(0, images, add, 0, unroll=4)
    for head in range(QH):
        out_ref[:, head * HD : (head + 1) * HD] = acc[:, head, :].astype(jnp.bfloat16)


def resident(queries, cache, context_length):
    rows, context = cache.shape[:2]
    local_queries = queries.reshape(rows, KVH, GROUP, HD)
    keys = cache[:, :, : KVH * HD].reshape(rows, context, KVH, HD)
    vals = cache[:, :, KVH * HD :].reshape(rows, context, KVH, HD)
    scores = jnp.einsum("rkgd,rtkd->rkgt", local_queries, keys, preferred_element_type=jnp.float32) * SCALE
    live = (jnp.arange(context)[None, :] < context_length[:, None])[:, None, None, :]
    scores = jnp.where(live, scores, masked_score)
    top = jnp.max(scores, axis=-1)
    weights = jnp.where(live, jnp.exp(scores - top[..., None]), 0.0)
    total = jnp.einsum("rkgt,rtkd->rkgd", weights.astype(jnp.bfloat16), vals, preferred_element_type=jnp.float32)
    return (
        top.reshape(rows, QH),
        jnp.sum(weights, axis=-1).reshape(rows, QH),
        total.reshape(rows, QH, HD),
    )


def per_device(prompt_states, kv_weight, image_owner, image_row, queries, cache, context_length):
    n = lax.axis_size("section")
    section = lax.axis_index("section")
    rep = lax.axis_index("replica")
    core = section % 2
    tokens, width = prompt_states.shape
    rows_dev, kv_width = kv_weight.shape
    half = kv_width // 4
    images = image_owner.shape[0]
    decode_rows = queries.shape[0]
    grid_form = n == 16 and lax.axis_size("replica") == 2

    columns = kv_weight.reshape(rows_dev, 2, 2, half)
    keep = jnp.where(core == 0, columns[:, :, 0], columns[:, :, 1])
    give = jnp.where(core == 0, columns[:, :, 1], columns[:, :, 0])
    phases = []
    for kind in range(2):
        got = swap_core(give[:, kind], n)
        chunk = jnp.concatenate([keep[:, kind], got], axis=0)
        if grid_form:
            span = chunk.shape[0] * (2 + kind) // 4
            phases.append(gather_grid(chunk, span, section // 4, section // 2 % 2, rep))
        else:
            phases.append(gather_plain(chunk, n))

    normed = normalize_rows(prompt_states).astype(jnp.bfloat16)
    other = swap_core(normed, n)

    target = image_owner * decode_rows + image_row
    all_target = lax.all_gather(target, "section", axis=0, tiled=False)
    chip_target = jnp.concatenate([target, jnp.take(all_target, section ^ 1, axis=0)])
    query_halves = queries.reshape(decode_rows, 2, HALF_QH * HD)
    keep_q = jnp.where(core == 0, query_halves[:, 0], query_halves[:, 1])
    give_q = jnp.where(core == 0, query_halves[:, 1], query_halves[:, 0])
    chip_q = jnp.concatenate([keep_q, swap_core(give_q, n)], axis=0)
    all_q = lax.all_gather(chip_q, "section", axis=0, tiled=True, axis_index_groups=same_core_groups(n))
    place = jnp.where(core == 0, chip_target, chip_target ^ decode_rows)
    pick = (place[:, None] == jnp.arange(n * decode_rows)[None, :]).astype(jnp.bfloat16)
    image_q = jnp.dot(pick, all_q, preferred_element_type=jnp.float32).astype(jnp.bfloat16)
    image_q = image_q.reshape(2 * images, HALF_KVH, GROUP, HD).transpose(1, 0, 2, 3)
    image_q = image_q.reshape(HALF_KVH, 2 * images * GROUP, HD)

    res_top, res_sum, res_out = resident(queries, cache, context_length)

    size = min(rows_dev, 256)
    depth = 1024
    steps = width // depth
    n_queries = 2 * images * GROUP
    token_spec = pl.BlockSpec((tokens, depth), lambda i, *_: (0, i))
    flops = 2 * 2 * tokens * width * 2 * HD

    arrays, layout, offsets = granules(phases[0], rows_dev, core, size)
    weights, maxes, sums = pl.pallas_call(
        functools.partial(key_kernel, layout, size, len(arrays)),
        grid_spec=pltpu.PrefetchScalarGridSpec(
            num_scalar_prefetch=1,
            grid=(steps,),
            in_specs=[token_spec, token_spec, pl.BlockSpec((HALF_KVH, n_queries, HD), lambda i, *_: (0, 0, 0))]
            + [pl.BlockSpec(memory_space=pl.ANY)] * len(arrays),
            out_specs=[
                pl.BlockSpec((HALF_KVH, n_queries, 2 * tokens), lambda i, *_: (0, 0, 0)),
                pl.BlockSpec((HALF_KVH, n_queries, HD), lambda i, *_: (0, 0, 0)),
                pl.BlockSpec((HALF_KVH, n_queries, HD), lambda i, *_: (0, 0, 0)),
            ],
            scratch_shapes=[
                pltpu.VMEM((width, 2 * HD), jnp.bfloat16),
                pltpu.VMEM((2 * tokens, 2 * HD), jnp.float32),
                pltpu.SemaphoreType.DMA((len(layout),)),
            ],
        ),
        out_shape=[
            jax.ShapeDtypeStruct((HALF_KVH, n_queries, 2 * tokens), jnp.bfloat16),
            jax.ShapeDtypeStruct((HALF_KVH, n_queries, HD), jnp.float32),
            jax.ShapeDtypeStruct((HALF_KVH, n_queries, HD), jnp.float32),
        ],
        compiler_params=pltpu.CompilerParams(vmem_limit_bytes=32 * 2**20),
        cost_estimate=pl.CostEstimate(flops=flops, bytes_accessed=22 * 2**20, transcendentals=0),
        name="keys",
    )(offsets, normed, other, image_q, *arrays)

    stats = jnp.stack([maxes[:, :, 0], sums[:, :, 0]]).reshape(2, HALF_KVH, 2, images, GROUP)
    all_stats = lax.all_gather(stats, "section", axis=0, tiled=False)
    all_stats = all_stats.reshape(n // 2, 2, 2, HALF_KVH, 2, images, GROUP)
    flipped = jnp.stack([all_stats[:, 0], all_stats[:, 1, :, :, ::-1]], axis=1)
    by_image = flipped.transpose(0, 4, 5, 2, 1, 3, 6).reshape(n, images, 2, QH)
    mine = (all_target // decode_rows) == section
    slot_stats = jnp.sum(jnp.where(mine[:, :, None, None], by_image, 0.0), axis=1)
    slot_has = jnp.any(mine, axis=1)
    slot_row = jnp.sum(jnp.where(mine, all_target % decode_rows, 0), axis=1)
    joins = slot_has[None, :] & (slot_row[None, :] == jnp.arange(decode_rows)[:, None])
    slot_max = jnp.where(joins[:, :, None], slot_stats[None, :, 0], masked_score)
    row_top = jnp.maximum(res_top, jnp.max(slot_max, axis=1))
    res_factor = jnp.exp(res_top - row_top)
    slot_factor = jnp.where(joins[:, :, None], jnp.exp(slot_max - row_top[:, None]), 0.0)
    denominator = res_sum * res_factor + jnp.sum(slot_factor * slot_stats[None, :, 1], axis=1)
    slot_factor = jnp.sum(slot_factor / denominator[:, None], axis=0)
    base = res_out * (res_factor / denominator)[..., None]
    factor = jnp.broadcast_to(slot_factor[..., None], (n, QH, HD))

    arrays, layout, offsets = granules(phases[1], rows_dev, core, size)
    slot = jnp.concatenate([image_owner * 2 + core, chip_target[images:] // decode_rows * 2 + 1 - core])
    slots = pl.pallas_call(
        functools.partial(value_kernel, layout, size, len(arrays)),
        grid_spec=pltpu.PrefetchScalarGridSpec(
            num_scalar_prefetch=2,
            grid=(steps,),
            in_specs=[
                token_spec,
                token_spec,
                pl.BlockSpec((HALF_KVH, n_queries, 2 * tokens), lambda i, *_: (0, 0, 0)),
            ]
            + [pl.BlockSpec(memory_space=pl.ANY)] * len(arrays),
            out_specs=pl.BlockSpec((2 * n, HALF_QH, HD), lambda i, *_: (0, 0, 0)),
            scratch_shapes=[
                pltpu.VMEM((width, 2 * HD), jnp.bfloat16),
                pltpu.VMEM((2 * tokens, 2 * HD), jnp.float32),
                pltpu.VMEM((2 * images, HALF_QH, HD), jnp.float32),
                pltpu.SemaphoreType.DMA((len(layout),)),
            ],
        ),
        out_shape=jax.ShapeDtypeStruct((2 * n, HALF_QH, HD), jnp.bfloat16),
        compiler_params=pltpu.CompilerParams(vmem_limit_bytes=32 * 2**20),
        cost_estimate=pl.CostEstimate(flops=flops, bytes_accessed=22 * 2**20, transcendentals=0),
        name="values",
    )(offsets, slot, normed, other, weights, *arrays)
    got = lax.all_to_all(
        slots.reshape(n, 2, HALF_QH, HD), "section", split_axis=0, concat_axis=0, tiled=True
    ).reshape(2 * n, HALF_QH, HD)

    return pl.pallas_call(
        combine_kernel,
        grid_spec=pltpu.PrefetchScalarGridSpec(
            num_scalar_prefetch=1,
            grid=(1,),
            in_specs=[
                pl.BlockSpec((2 * n, HALF_QH, HD), lambda i, *_: (0, 0, 0)),
                pl.BlockSpec((n, QH, HD), lambda i, *_: (0, 0, 0)),
                pl.BlockSpec((decode_rows, QH, HD), lambda i, *_: (0, 0, 0)),
            ],
            out_specs=pl.BlockSpec((decode_rows, QH * HD), lambda i, *_: (0, 0)),
            scratch_shapes=[pltpu.VMEM((decode_rows, QH, HD), jnp.float32)],
        ),
        out_shape=jax.ShapeDtypeStruct((decode_rows, QH * HD), jnp.bfloat16),
        compiler_params=pltpu.CompilerParams(vmem_limit_bytes=32 * 2**20),
        name="combine",
    )(slot_row, got, factor, base)


def solution(mesh):
    placed = (
        P(("replica", "section"), None),
        P("section", None),
        P(("replica", "section")),
        P(("replica", "section")),
        P(("replica", "section"), None),
        P(("replica", "section"), None, None),
        P(("replica", "section")),
    )
    return jax.shard_map(
        per_device,
        mesh=mesh,
        in_specs=placed,
        out_specs=P(("replica", "section"), None),
        check_vma=False,
    )
```

```python
import math

import jax
import jax.numpy as jnp
from jax import lax
from jax.sharding import PartitionSpec as P

HD = 128
KVH = 4
QH = 32
IMG_TOK = 64


masked_score = -1e30


def normalize_rows(states):
    values = states.astype(jnp.float32)
    return values * lax.rsqrt(jnp.mean(values * values, axis=-1, keepdims=True) + 1e-05)


def per_device(prompt_states, kv_weight, image_owner, image_row, queries, cache, context_length):
    peer_count = lax.axis_size("section")
    image_count = image_owner.shape[0]
    kv_width = kv_weight.shape[1]
    rows_dev = queries.shape[0]
    context = cache.shape[1]
    key_width = kv_width // 2
    group_size = QH // KVH
    score_scale = 1.0 / math.sqrt(HD)
    copies = lax.axis_size("replica")
    part = kv_weight.shape[0] // copies
    share = lax.dynamic_slice_in_dim(kv_weight, lax.axis_index("replica") * part, part, 0)
    normed = normalize_rows(prompt_states).astype(jnp.bfloat16)
    normed = normed.reshape(-1, peer_count, copies, part).transpose(0, 2, 1, 3).reshape(normed.shape)
    new_kv = jnp.dot(
        normed,
        lax.all_gather(share, ("replica", "section"), axis=0, tiled=True),
        preferred_element_type=jnp.float32,
    ).astype(jnp.bfloat16)
    image_kv = new_kv.reshape(image_count, IMG_TOK, kv_width)
    local_queries = queries.reshape(rows_dev, KVH, group_size, HD)
    res_keys = cache[:, :, :key_width].reshape(rows_dev, context, KVH, HD)
    res_vals = cache[:, :, key_width:].reshape(rows_dev, context, KVH, HD)
    res_scores = (
        jnp.einsum("rkgd,rtkd->rkgt", local_queries, res_keys, preferred_element_type=jnp.float32)
        * score_scale
    )
    res_live = (jnp.arange(context)[None, :] < context_length[:, None])[:, None, None, :]
    res_scores = jnp.where(res_live, res_scores, masked_score)
    res_max = jnp.max(res_scores, axis=-1)
    placement = jnp.arange(peer_count)[:, None] == image_owner[None, :]
    kv_slots = jnp.dot(
        placement.astype(jnp.bfloat16),
        image_kv.reshape(image_count, IMG_TOK * kv_width),
        preferred_element_type=jnp.float32,
    ).astype(jnp.bfloat16)
    row_slots = jnp.where(
        jnp.any(placement, axis=1),
        jnp.sum(jnp.where(placement, image_row[None, :], 0), axis=1),
        rows_dev,
    )
    got_kv, got_rows = (
        lax.all_to_all(
            kv_slots.reshape(peer_count, IMG_TOK, kv_width),
            "section",
            split_axis=0,
            concat_axis=0,
            tiled=True,
        ),
        lax.all_to_all(
            row_slots.reshape(peer_count, 1), "section", split_axis=0, concat_axis=0, tiled=True
        ),
    )
    got_keys = got_kv[:, :, :key_width].reshape(peer_count, IMG_TOK, KVH, HD)
    got_vals = got_kv[:, :, key_width:].reshape(peer_count, IMG_TOK, KVH, HD)
    new_scores = (
        jnp.einsum("rkgd,smkd->rkgsm", local_queries, got_keys, preferred_element_type=jnp.float32)
        * score_scale
    )
    new_live = (got_rows[:, 0][None, :] == jnp.arange(rows_dev)[:, None])[:, None, None, :, None]
    new_scores = jnp.where(new_live, new_scores, masked_score)
    row_top = jnp.maximum(res_max, jnp.max(new_scores, axis=(-2, -1)))
    res_w = jnp.where(res_live, jnp.exp(res_scores - row_top[..., None]), 0.0)
    new_w = jnp.where(new_live, jnp.exp(new_scores - row_top[..., None, None]), 0.0)
    denominator = jnp.sum(res_w, axis=-1) + jnp.sum(new_w, axis=(-2, -1))
    weighted = jnp.einsum(
        "rkgt,rtkd->rkgd", res_w.astype(jnp.bfloat16), res_vals, preferred_element_type=jnp.float32
    )
    weighted = weighted + jnp.einsum(
        "rkgsm,smkd->rkgd", new_w.astype(jnp.bfloat16), got_vals, preferred_element_type=jnp.float32
    )
    return (weighted / denominator[..., None]).reshape(rows_dev, QH * HD).astype(jnp.bfloat16)


def solution(mesh):
    placed = (
        P(("replica", "section"), None),
        P("section", None),
        P(("replica", "section")),
        P(("replica", "section")),
        P(("replica", "section"), None),
        P(("replica", "section"), None, None),
        P(("replica", "section")),
    )
    return jax.shard_map(
        per_device,
        mesh=mesh,
        in_specs=placed,
        out_specs=P(("replica", "section"), None),
        check_vma=False,
    )
```

```python
import functools
import math

import jax
import jax.numpy as jnp
from jax import lax
from jax.experimental import pallas as pl
from jax.experimental.pallas import tpu as pltpu
from jax.sharding import PartitionSpec as P

HD = 128
KVH = 4
QH = 32
IMG_TOK = 64
GROUP = QH // KVH
HALF_KVH = KVH // 2
HALF_QH = QH // 2
SCALE = 1.0 / math.sqrt(HD)
EPS = 1e-05

LANES = 64
N_KINDS = 7

masked_score = -1e30


def swap_core(x):
    n = lax.axis_size("section")
    return lax.ppermute(x, "section", [(i, i ^ 1) for i in range(n)])


def gather_plain(chunk):
    n = lax.axis_size("section")
    rows = chunk.shape[0]
    groups = [list(range(core, n, 2)) for core in range(2)]
    whole = lax.all_gather(chunk, "section", axis=0, tiled=True, axis_index_groups=groups)
    return [(chip, [(whole, chip * rows, rows, 0)]) for chip in range(n // 2)]


def gather_grid(chunk, span):
    section = lax.axis_index("section")
    rep = lax.axis_index("replica")
    z, y = section // 4, section // 2 % 2
    rows = chunk.shape[0]
    rest = rows - span
    order = [0, 1, 3, 2]
    ring = [(order[p] * 4 + low, order[(p + 1) % 4] * 4 + low) for p in range(4) for low in range(4)]
    swap_y = [(i, i ^ 2) for i in range(16)]
    places = jnp.array([0, 1, 3, 2], jnp.int32)
    place = places[z]
    along_z = [lax.dynamic_slice_in_dim(chunk, rep * rest, span, 0)]
    along_y = []
    for step in range(4):
        if step < 3:
            along_z.append(lax.ppermute(along_z[-1], "section", ring))
        along_y.append(lax.ppermute(along_z[step], "section", swap_y))
    groups = [(z * 2 + y, [(chunk, 0, rows, 0)])]
    for step in range(4):
        from_z = places[(place - step) % 4]
        for piece, chip in ((along_z[step], from_z * 2 + y), (along_y[step], from_z * 2 + 1 - y)):
            if piece is along_z[0]:
                continue
            part = piece if rest == span else lax.dynamic_slice_in_dim(piece, rep * (span - rest), rest, 0)
            extra = lax.ppermute(part, "replica", [(0, 1), (1, 0)])
            groups.append((chip, [(piece, 0, span, rep * rest), (extra, 0, rest, (1 - rep) * span)]))
    return groups


def flatten(groups):
    arrays, layout, numbers = [], [], []
    for index, (chip, parts) in enumerate(groups):
        for array, start, rows, place in parts:
            at = [i for i, known in enumerate(arrays) if known is array]
            if not at:
                arrays.append(array)
                at = [len(arrays) - 1]
            layout.append((at[0], start, rows, index))
            numbers.append(jnp.asarray(place, jnp.int32))
    chips = [jnp.asarray(chip, jnp.int32) for chip, _ in groups]
    return arrays, layout, jnp.stack(chips), jnp.stack(numbers)


def split_kernel(core_ref, keep_in, give_in, keep_ref, give_ref):
    keep_ref[...] = keep_in[...]
    give_ref[...] = give_in[...]


def accumulate(layout, place_ref, own_ref, other_ref, piece_refs, weight, total, squares, sems):
    step = pl.program_id(0)
    tokens, depth = own_ref.shape
    copies = [
        pltpu.make_async_copy(
            piece_refs[which].at[pl.ds(start, rows)],
            weight.at[group, pl.ds(pl.multiple_of(place_ref[i], 32), rows)],
            sems.at[i],
        )
        for i, (which, start, rows, group) in enumerate(layout)
    ]

    @pl.when(step == 0)
    def _():
        for copy in copies:
            copy.start()

    for group in range(weight.shape[0]):

        @pl.when(step == group)
        def _():
            for copy, (_, _, _, owner) in zip(copies, layout):
                if owner == group:
                    copy.wait()

    states = jnp.concatenate([own_ref[...], other_ref[...]], axis=0)
    total[...] += jnp.dot(states, weight[step], preferred_element_type=jnp.float32)
    values = states.astype(jnp.float32)
    values = values * values
    squares[...] += sum(values[:, i : i + HD] for i in range(0, depth, HD))


def first_kernel(layout, n_pieces, block_ref, place_ref, own_ref, other_ref, *refs):
    piece_refs = refs[:n_pieces]
    total, squares, weight, sems = refs[n_pieces:]

    @pl.when(pl.program_id(0) == 0)
    def _():
        total[...] = jnp.zeros_like(total)
        squares[...] = jnp.zeros_like(squares)

    accumulate(layout, place_ref, own_ref, other_ref, piece_refs, weight, total, squares, sems)


def parts_of(values, count):
    out = []
    for _ in range(count):
        part = values.astype(jnp.bfloat16).astype(jnp.float32)
        out.append(part)
        values = values - part
    return out


def last_kernel(
    layout, n_pieces, width, block_ref, place_ref, slot_ref, own_ref, other_ref, query_ref, row_lane_ref, in_total, in_squares, *refs
):
    piece_refs = refs[:n_pieces]
    slots_ref, weight, total, squares, summed, stats, sems = refs[n_pieces:]
    images = query_ref.shape[1] // GROUP

    @pl.when(pl.program_id(0) == 0)
    def _():
        total[...] = in_total[...]
        squares[...] = in_squares[...]
        slots_ref[...] = jnp.zeros_like(slots_ref)

    accumulate(layout, place_ref, own_ref, other_ref, piece_refs, weight, total, squares, sems)

    @pl.when(pl.program_id(0) == pl.num_programs(0) - 1)
    def _():
        tokens = total.shape[0]
        queries = query_ref.shape[1]
        factor = lax.rsqrt(jnp.sum(squares[...], axis=1, keepdims=True) / width + EPS)
        image_of_query = lax.broadcasted_iota(jnp.int32, (queries, tokens), 0) // GROUP
        image_of_token = lax.broadcasted_iota(jnp.int32, (queries, tokens), 1) // IMG_TOK
        live = image_of_query == image_of_token
        lane = lax.broadcasted_iota(jnp.int32, (queries, HD), 1)
        first_lane = row_lane_ref[:, :1]
        for head in range(HALF_KVH):
            part = slice(head * GROUP, (head + 1) * GROUP)
            keys = (total[:, head * HD : (head + 1) * HD] * factor).astype(jnp.bfloat16)
            at = (HALF_KVH + head) * HD
            values = (total[:, at : at + HD] * factor).astype(jnp.bfloat16)
            scores = (
                lax.dot_general(
                    query_ref[head], keys, (((1,), (1,)), ((), ())), preferred_element_type=jnp.float32
                )
                * SCALE
            )
            scores = jnp.where(live, scores, masked_score)
            top = jnp.max(scores, axis=1, keepdims=True)
            weights = jnp.where(live, jnp.exp(scores - top), 0.0)
            total_weight = jnp.sum(weights, axis=1, keepdims=True)
            out = jnp.dot(weights.astype(jnp.bfloat16), values, preferred_element_type=jnp.float32)
            summed[:, part, :] = out.reshape(images, GROUP, HD)
            kinds = parts_of(top, 3) + parts_of(total_weight, 3) + [jnp.ones_like(top)]
            tile = jnp.zeros((queries, HD), jnp.float32)
            for kind, column in enumerate(kinds):
                tile = jnp.where(lane == first_lane + kind * 8, column, tile)
            stats[:, part, :] = tile.reshape(images, GROUP, HD)
        for image in range(images):
            owner, which = slot_ref[0, image], slot_ref[1, image]
            slots_ref[owner, which] = summed[image].astype(jnp.bfloat16)
            slots_ref[owner, 2] = slots_ref[owner, 2] + stats[image].astype(jnp.bfloat16)


def resident_kernel(length_ref, query_ref, cache_ref, out_ref, top_ref, sum_ref):
    row = pl.program_id(0)
    context = cache_ref.shape[1]
    live = lax.broadcasted_iota(jnp.int32, (GROUP, context), 1) < length_ref[row]
    lane = lax.broadcasted_iota(jnp.int32, (GROUP, HD), 1)

    @pl.when(row == 0)
    def _():
        top_ref[...] = jnp.zeros_like(top_ref)
        sum_ref[...] = jnp.zeros_like(sum_ref)

    for head in range(KVH):
        part = slice(head * GROUP, (head + 1) * GROUP)
        keys = cache_ref[0, :, head * HD : (head + 1) * HD]
        values = cache_ref[0, :, (KVH + head) * HD : (KVH + head + 1) * HD]
        scores = (
            lax.dot_general(
                query_ref[0, part, :], keys, (((1,), (1,)), ((), ())), preferred_element_type=jnp.float32
            )
            * SCALE
        )
        scores = jnp.where(live, scores, masked_score)
        top = jnp.max(scores, axis=1, keepdims=True)
        weights = jnp.where(live, jnp.exp(scores - top), 0.0)
        out_ref[0, part, :] = jnp.dot(weights.astype(jnp.bfloat16), values, preferred_element_type=jnp.float32)
        top_ref[part, :] = jnp.where(lane == row, top, top_ref[part, :])
        sum_ref[part, :] = jnp.where(lane == row, jnp.sum(weights, axis=1, keepdims=True), sum_ref[part, :])


def combine_kernel(got_ref, res_out_ref, res_top_ref, res_sum_ref, out_ref, acc, shares):
    chips = got_ref.shape[0] // 2
    rows = res_out_ref.shape[0]
    lane = lax.broadcasted_iota(jnp.int32, (HALF_QH, HD), 1)
    head_lane = (lane % LANES) < 8

    def moved(tile, by):
        return pltpu.roll(tile, HD - by, 1)

    for core in range(2):
        part = slice(core * HALF_QH, (core + 1) * HALF_QH)
        tops, sums, here = [], [], []
        for chip in range(chips):
            tile = got_ref[chip * 2 + core, 2].astype(jnp.float32)
            present = (moved(tile, 48) > 0.5) & head_lane
            tops.append(jnp.where(present, tile + moved(tile, 8) + moved(tile, 16), masked_score))
            sums.append(moved(tile, 24) + moved(tile, 32) + moved(tile, 40))
            here.append(present)
        row_top = functools.reduce(jnp.maximum, tops)
        row_top = jnp.maximum(row_top, pltpu.roll(row_top, LANES, 1))
        res_top = jnp.where(lane < 8, res_top_ref[part, :], masked_score)
        res_top = jnp.maximum(res_top, pltpu.roll(res_top, LANES, 1))
        row_top = jnp.maximum(row_top, res_top)
        weights = [jnp.where(a, jnp.exp(t - row_top), 0.0) for a, t in zip(here, tops)]
        joined = sum(w * s for w, s in zip(weights, sums))
        res_weight = jnp.exp(res_top - row_top)
        denominator = joined + pltpu.roll(joined, LANES, 1) + res_weight * res_sum_ref[part, :]
        scale = jnp.where(lane < 8, 1.0 / denominator, 0.0)
        scale = scale + pltpu.roll(scale, LANES, 1)
        res_share = res_weight * scale
        weights = [w * scale for w in weights]
        for row in range(rows):
            value = res_out_ref[row, part, :] * res_share[:, row : row + 1]
            for chip in range(chips):
                for which in range(2):
                    at = which * LANES + row
                    value += weights[chip][:, at : at + 1] * got_ref[chip * 2 + core, which].astype(jnp.float32)
            acc[row, part, :] = value
    for head in range(QH):
        out_ref[:, head * HD : (head + 1) * HD] = acc[:, head, :].astype(jnp.bfloat16)


def whole(shape):
    return pl.BlockSpec(shape, lambda i, *_: (0,) * len(shape))


def per_device(prompt_states, kv_weight, image_owner, image_row, queries, cache, context_length):
    n = lax.axis_size("section")
    section = lax.axis_index("section")
    core = section % 2
    tokens, width = prompt_states.shape
    rows_dev, kv_width = kv_weight.shape
    columns_dev = kv_width // 2
    images = image_owner.shape[0]
    decode_rows = queries.shape[0]
    context = cache.shape[1]
    grid_form = n == 16 and lax.axis_size("replica") == 2

    cut = columns_dev // 2
    keep, give = pl.pallas_call(
        split_kernel,
        grid_spec=pltpu.PrefetchScalarGridSpec(
            num_scalar_prefetch=1,
            grid=(2,),
            in_specs=[
                pl.BlockSpec((rows_dev, cut), lambda i, core_ref: (0, 2 * i + core_ref[0])),
                pl.BlockSpec((rows_dev, cut), lambda i, core_ref: (0, 2 * i + 1 - core_ref[0])),
            ],
            out_specs=[pl.BlockSpec((rows_dev, cut), lambda i, core_ref: (0, i))] * 2,
        ),
        out_shape=[jax.ShapeDtypeStruct((rows_dev, columns_dev), jnp.bfloat16)] * 2,
        cost_estimate=pl.CostEstimate(flops=0, bytes_accessed=2 * 2**20, transcendentals=0),
        name="split",
    )(core.reshape(1), kv_weight, kv_weight)
    taken = swap_core(give)
    if grid_form:
        phases = [gather_grid(keep, rows_dev // 2), gather_grid(taken, rows_dev * 13 // 16)]
    else:
        phases = [gather_plain(keep), gather_plain(taken)]

    states, taken = lax.optimization_barrier((prompt_states, taken))
    other = swap_core(states)

    owner_and_row = jnp.stack([image_owner, image_row])
    chip_images = jnp.concatenate([owner_and_row, swap_core(owner_and_row)], axis=1)
    send_q = queries.reshape(decode_rows, 2, HALF_QH * HD).transpose(1, 0, 2)
    send_q = jnp.broadcast_to(send_q[None], (n // 2, 2, decode_rows, HALF_QH * HD)).reshape(
        n, decode_rows, HALF_QH * HD
    )
    all_q = lax.all_to_all(send_q, "section", split_axis=0, concat_axis=0, tiled=True)
    all_q = all_q.reshape(n * decode_rows, HALF_QH * HD)
    target = chip_images[0] * decode_rows + chip_images[1]
    pick = (target[:, None] == jnp.arange(n * decode_rows)[None, :]).astype(jnp.bfloat16)
    image_q = jnp.dot(pick, all_q, preferred_element_type=jnp.float32).astype(jnp.bfloat16)
    image_q = image_q.reshape(2 * images, HALF_KVH, GROUP, HD).transpose(1, 0, 2, 3)
    image_q = image_q.reshape(HALF_KVH, 2 * images * GROUP, HD)
    n_queries = 2 * images * GROUP

    which = jnp.concatenate([jnp.full((images,), core), jnp.full((images,), 1 - core)]).astype(jnp.int32)
    slot = jnp.stack([chip_images[0], which])
    row_lane = jnp.broadcast_to(jnp.repeat(which * LANES + chip_images[1], GROUP)[:, None], (n_queries, HD))

    res_out, res_top, res_sum = pl.pallas_call(
        resident_kernel,
        grid_spec=pltpu.PrefetchScalarGridSpec(
            num_scalar_prefetch=1,
            grid=(decode_rows,),
            in_specs=[
                pl.BlockSpec((1, QH, HD), lambda i, *_: (i, 0, 0)),
                pl.BlockSpec((1, context, kv_width), lambda i, *_: (i, 0, 0)),
            ],
            out_specs=[pl.BlockSpec((1, QH, HD), lambda i, *_: (i, 0, 0)), whole((QH, HD)), whole((QH, HD))],
        ),
        out_shape=[
            jax.ShapeDtypeStruct((decode_rows, QH, HD), jnp.float32),
            jax.ShapeDtypeStruct((QH, HD), jnp.float32),
            jax.ShapeDtypeStruct((QH, HD), jnp.float32),
        ],
        compiler_params=pltpu.CompilerParams(vmem_limit_bytes=16 * 2**20),
        cost_estimate=pl.CostEstimate(flops=2**28, bytes_accessed=4 * 2**20, transcendentals=0),
        name="resident",
    )(context_length, queries.reshape(decode_rows, QH, HD), cache)

    flops = 2 * 2 * tokens * width // 2 * columns_dev
    cost = pl.CostEstimate(flops=flops, bytes_accessed=16 * 2**20, transcendentals=0)
    params = pltpu.CompilerParams(vmem_limit_bytes=56 * 2**20)
    token_spec = pl.BlockSpec((tokens, rows_dev), lambda i, block_ref, *_: (0, block_ref[i]))
    anywhere = pl.BlockSpec(memory_space=pl.ANY)

    arrays, layout, chips, places = flatten(phases[0])
    total, squares = pl.pallas_call(
        functools.partial(first_kernel, layout, len(arrays)),
        grid_spec=pltpu.PrefetchScalarGridSpec(
            num_scalar_prefetch=2,
            grid=(n // 2,),
            in_specs=[token_spec, token_spec] + [anywhere] * len(arrays),
            out_specs=[whole((2 * tokens, columns_dev)), whole((2 * tokens, HD))],
            scratch_shapes=[
                pltpu.VMEM((n // 2, rows_dev, columns_dev), jnp.bfloat16),
                pltpu.SemaphoreType.DMA((len(layout),)),
            ],
        ),
        out_shape=[
            jax.ShapeDtypeStruct((2 * tokens, columns_dev), jnp.float32),
            jax.ShapeDtypeStruct((2 * tokens, HD), jnp.float32),
        ],
        compiler_params=params,
        cost_estimate=cost,
        name="first_rows",
    )(chips * 2 + core, places, prompt_states, other, *arrays)

    arrays, layout, chips, places = flatten(phases[1])
    slots = pl.pallas_call(
        functools.partial(last_kernel, layout, len(arrays), width),
        grid_spec=pltpu.PrefetchScalarGridSpec(
            num_scalar_prefetch=3,
            grid=(n // 2,),
            in_specs=[
                token_spec,
                token_spec,
                whole((HALF_KVH, n_queries, HD)),
                whole((n_queries, HD)),
                whole((2 * tokens, columns_dev)),
                whole((2 * tokens, HD)),
            ]
            + [anywhere] * len(arrays),
            out_specs=whole((n, 3, HALF_QH, HD)),
            scratch_shapes=[
                pltpu.VMEM((n // 2, rows_dev, columns_dev), jnp.bfloat16),
                pltpu.VMEM((2 * tokens, columns_dev), jnp.float32),
                pltpu.VMEM((2 * tokens, HD), jnp.float32),
                pltpu.VMEM((2 * images, HALF_QH, HD), jnp.float32),
                pltpu.VMEM((2 * images, HALF_QH, HD), jnp.float32),
                pltpu.SemaphoreType.DMA((len(layout),)),
            ],
        ),
        out_shape=jax.ShapeDtypeStruct((n, 3, HALF_QH, HD), jnp.bfloat16),
        compiler_params=params,
        cost_estimate=cost,
        name="last_rows",
    )(chips * 2 + 1 - core, places, slot, prompt_states, other, image_q, row_lane, total, squares, *arrays)
    got = lax.all_to_all(slots, "section", split_axis=0, concat_axis=0, tiled=True)

    return pl.pallas_call(
        combine_kernel,
        grid=(1,),
        in_specs=[
            whole((n, 3, HALF_QH, HD)),
            whole((decode_rows, QH, HD)),
            whole((QH, HD)),
            whole((QH, HD)),
        ],
        out_specs=whole((decode_rows, QH * HD)),
        scratch_shapes=[
            pltpu.VMEM((decode_rows, QH, HD), jnp.float32),
            pltpu.VMEM((HALF_QH, HD), jnp.float32),
        ],
        out_shape=jax.ShapeDtypeStruct((decode_rows, QH * HD), jnp.bfloat16),
        compiler_params=pltpu.CompilerParams(vmem_limit_bytes=32 * 2**20),
        name="combine",
    )(got, res_out, res_top, res_sum)


def solution(mesh):
    placed = (
        P(("replica", "section"), None),
        P("section", None),
        P(("replica", "section")),
        P(("replica", "section")),
        P(("replica", "section"), None),
        P(("replica", "section"), None, None),
        P(("replica", "section")),
    )
    return jax.shard_map(
        per_device,
        mesh=mesh,
        in_specs=placed,
        out_specs=P(("replica", "section"), None),
        check_vma=False,
    )
```

```python
import functools
import math

import jax
import jax.numpy as jnp
from jax import lax
from jax.experimental import pallas as pl
from jax.experimental.pallas import tpu as pltpu
from jax.sharding import PartitionSpec as P

HD = 128
KVH = 4
QH = 32
IMG_TOK = 64
GROUP = QH // KVH
HALF_KVH = KVH // 2
HALF_QH = QH // 2
SCALE = 1.0 / math.sqrt(HD)
EPS = 1e-05

LANES = 64
N_KINDS = 7

masked_score = -1e30


def swap_core(x):
    n = lax.axis_size("section")
    return lax.ppermute(x, "section", [(i, i ^ 1) for i in range(n)])


def gather_plain(chunk):
    n = lax.axis_size("section")
    rows = chunk.shape[0]
    groups = [list(range(core, n, 2)) for core in range(2)]
    whole = lax.all_gather(chunk, "section", axis=0, tiled=True, axis_index_groups=groups)
    return [(chip, whole, chip * rows) for chip in range(n // 2)]


RING = [0, 1, 3, 2]


def along_ring(x):
    perm = []
    for rep, way in ((0, 1), (1, -1)):
        for p in range(4):
            for low in range(4):
                perm.append((rep * 16 + RING[p] * 4 + low, rep * 16 + RING[(p + way) % 4] * 4 + low))
    return lax.ppermute(x, ("replica", "section"), perm)


def across_y(x):
    return lax.ppermute(x, "section", [(i, i ^ 2) for i in range(16)])


def across_replica(x):
    return lax.ppermute(x, "replica", [(0, 1), (1, 0)])


def ring_chips():
    section = lax.axis_index("section")
    rep = lax.axis_index("replica")
    z, y = section // 4, section // 2 % 2
    ring = jnp.array(RING, jnp.int32)
    way = 1 - 2 * rep
    place = ring[z]
    chips = {}
    for name, at in (("own", place), ("behind", place - way), ("ahead", place + way), ("opposite", place + 2)):
        there = ring[at % 4] * 2
        chips[name] = there + y
        chips[name + "_y"] = there + 1 - y
    return chips


def split_kernel(core_ref, keep_in, give_in, keep_ref, give_ref):
    keep_ref[...] = keep_in[...]
    give_ref[...] = give_in[...]


def accumulate(layout, own_ref, other_ref, piece_refs, weight, total, squares, sems):
    step = pl.program_id(0)
    tokens, depth = own_ref.shape
    copies = [
        pltpu.make_async_copy(piece_refs[which].at[pl.ds(start, depth)], weight.at[i], sems.at[i])
        for i, (which, start) in enumerate(layout)
    ]

    @pl.when(step == 0)
    def _():
        for copy in copies:
            copy.start()

    for i, copy in enumerate(copies):

        @pl.when(step == i)
        def _():
            copy.wait()

    states = jnp.concatenate([own_ref[...], other_ref[...]], axis=0)
    total[...] += jnp.dot(states, weight[step], preferred_element_type=jnp.float32)
    values = states.astype(jnp.float32)
    values = values * values
    squares[...] += sum(values[:, i : i + HD] for i in range(0, depth, HD))


def first_kernel(layout, n_pieces, block_ref, own_ref, other_ref, *refs):
    piece_refs = refs[:n_pieces]
    total, squares, weight, sems = refs[n_pieces:]

    @pl.when(pl.program_id(0) == 0)
    def _():
        total[...] = jnp.zeros_like(total)
        squares[...] = jnp.zeros_like(squares)

    accumulate(layout, own_ref, other_ref, piece_refs, weight, total, squares, sems)


def next_kernel(layout, n_pieces, block_ref, own_ref, other_ref, in_total, in_squares, *refs):
    piece_refs = refs[:n_pieces]
    total, squares, weight, sems = refs[n_pieces:]

    @pl.when(pl.program_id(0) == 0)
    def _():
        total[...] = in_total[...]
        squares[...] = in_squares[...]

    accumulate(layout, own_ref, other_ref, piece_refs, weight, total, squares, sems)


def parts_of(values, count):
    out = []
    for _ in range(count):
        part = values.astype(jnp.bfloat16).astype(jnp.float32)
        out.append(part)
        values = values - part
    return out


def last_kernel(
    layout, n_pieces, width, block_ref, slot_ref, own_ref, other_ref, in_total, in_squares, query_ref, row_lane_ref, *refs
):
    piece_refs = refs[:n_pieces]
    slots_ref, weight, total, squares, summed, stats, sems = refs[n_pieces:]
    images = query_ref.shape[1] // GROUP

    @pl.when(pl.program_id(0) == 0)
    def _():
        total[...] = in_total[...]
        squares[...] = in_squares[...]
        slots_ref[...] = jnp.zeros_like(slots_ref)

    accumulate(layout, own_ref, other_ref, piece_refs, weight, total, squares, sems)

    @pl.when(pl.program_id(0) == pl.num_programs(0) - 1)
    def _():
        tokens = total.shape[0]
        queries = query_ref.shape[1]
        factor = lax.rsqrt(jnp.sum(squares[...], axis=1, keepdims=True) / width + EPS)
        image_of_query = lax.broadcasted_iota(jnp.int32, (queries, tokens), 0) // GROUP
        image_of_token = lax.broadcasted_iota(jnp.int32, (queries, tokens), 1) // IMG_TOK
        live = image_of_query == image_of_token
        lane = lax.broadcasted_iota(jnp.int32, (queries, HD), 1)
        first_lane = row_lane_ref[:, :1]
        for head in range(HALF_KVH):
            part = slice(head * GROUP, (head + 1) * GROUP)
            keys = (total[:, head * HD : (head + 1) * HD] * factor).astype(jnp.bfloat16)
            at = (HALF_KVH + head) * HD
            values = (total[:, at : at + HD] * factor).astype(jnp.bfloat16)
            scores = (
                lax.dot_general(
                    query_ref[head], keys, (((1,), (1,)), ((), ())), preferred_element_type=jnp.float32
                )
                * SCALE
            )
            scores = jnp.where(live, scores, masked_score)
            top = jnp.max(scores, axis=1, keepdims=True)
            weights = jnp.where(live, jnp.exp(scores - top), 0.0)
            total_weight = jnp.sum(weights, axis=1, keepdims=True)
            out = jnp.dot(weights.astype(jnp.bfloat16), values, preferred_element_type=jnp.float32)
            summed[:, part, :] = out.reshape(images, GROUP, HD)
            kinds = parts_of(top, 3) + parts_of(total_weight, 3) + [jnp.ones_like(top)]
            tile = jnp.zeros((queries, HD), jnp.float32)
            for kind, column in enumerate(kinds):
                tile = jnp.where(lane == first_lane + kind * 8, column, tile)
            stats[:, part, :] = tile.reshape(images, GROUP, HD)
        for image in range(images):
            owner, which = slot_ref[0, image], slot_ref[1, image]
            slots_ref[owner, which] = summed[image].astype(jnp.bfloat16)
            slots_ref[owner, 2] = slots_ref[owner, 2] + stats[image].astype(jnp.bfloat16)


def resident_kernel(length_ref, query_ref, cache_ref, out_ref, top_ref, sum_ref):
    row = pl.program_id(0)
    context = cache_ref.shape[1]
    live = lax.broadcasted_iota(jnp.int32, (GROUP, context), 1) < length_ref[row]
    lane = lax.broadcasted_iota(jnp.int32, (GROUP, HD), 1)

    @pl.when(row == 0)
    def _():
        top_ref[...] = jnp.zeros_like(top_ref)
        sum_ref[...] = jnp.zeros_like(sum_ref)

    for head in range(KVH):
        part = slice(head * GROUP, (head + 1) * GROUP)
        keys = cache_ref[0, :, head * HD : (head + 1) * HD]
        values = cache_ref[0, :, (KVH + head) * HD : (KVH + head + 1) * HD]
        scores = (
            lax.dot_general(
                query_ref[0, part, :], keys, (((1,), (1,)), ((), ())), preferred_element_type=jnp.float32
            )
            * SCALE
        )
        scores = jnp.where(live, scores, masked_score)
        top = jnp.max(scores, axis=1, keepdims=True)
        weights = jnp.where(live, jnp.exp(scores - top), 0.0)
        out_ref[0, part, :] = jnp.dot(weights.astype(jnp.bfloat16), values, preferred_element_type=jnp.float32)
        top_ref[part, :] = jnp.where(lane == row, top, top_ref[part, :])
        sum_ref[part, :] = jnp.where(lane == row, jnp.sum(weights, axis=1, keepdims=True), sum_ref[part, :])


def combine_kernel(got_ref, res_out_ref, res_top_ref, res_sum_ref, out_ref, acc):
    chips = got_ref.shape[0] // 2
    rows = res_out_ref.shape[0]
    lane = lax.broadcasted_iota(jnp.int32, (HALF_QH, HD), 1)
    head_lane = (lane % LANES) < 8

    def moved(tile, by):
        return pltpu.roll(tile, HD - by, 1)

    for core in range(2):
        part = slice(core * HALF_QH, (core + 1) * HALF_QH)
        tops, sums, here = [], [], []
        for chip in range(chips):
            tile = got_ref[chip * 2 + core, 2].astype(jnp.float32)
            present = (moved(tile, 48) > 0.5) & head_lane
            tops.append(jnp.where(present, tile + moved(tile, 8) + moved(tile, 16), masked_score))
            sums.append(moved(tile, 24) + moved(tile, 32) + moved(tile, 40))
            here.append(present)
        row_top = functools.reduce(jnp.maximum, tops)
        row_top = jnp.maximum(row_top, pltpu.roll(row_top, LANES, 1))
        res_top = jnp.where(lane < 8, res_top_ref[part, :], masked_score)
        res_top = jnp.maximum(res_top, pltpu.roll(res_top, LANES, 1))
        row_top = jnp.maximum(row_top, res_top)
        weights = [jnp.where(a, jnp.exp(t - row_top), 0.0) for a, t in zip(here, tops)]
        joined = sum(w * s for w, s in zip(weights, sums))
        res_weight = jnp.exp(res_top - row_top)
        denominator = joined + pltpu.roll(joined, LANES, 1) + res_weight * res_sum_ref[part, :]
        scale = jnp.where(lane < 8, 1.0 / denominator, 0.0)
        scale = scale + pltpu.roll(scale, LANES, 1)
        res_share = res_weight * scale
        weights = [w * scale for w in weights]
        for row in range(rows):
            value = res_out_ref[row, part, :] * res_share[:, row : row + 1]
            for chip in range(chips):
                for which in range(2):
                    at = which * LANES + row
                    value += weights[chip][:, at : at + 1] * got_ref[chip * 2 + core, which].astype(jnp.float32)
            acc[row, part, :] = value
    for head in range(QH):
        out_ref[:, head * HD : (head + 1) * HD] = acc[:, head, :].astype(jnp.bfloat16)


def whole(shape):
    return pl.BlockSpec(shape, lambda i, *_: (0,) * len(shape))


def per_device(prompt_states, kv_weight, image_owner, image_row, queries, cache, context_length):
    n = lax.axis_size("section")
    section = lax.axis_index("section")
    core = section % 2
    tokens, width = prompt_states.shape
    rows_dev, kv_width = kv_weight.shape
    columns_dev = kv_width // 2
    images = image_owner.shape[0]
    decode_rows = queries.shape[0]
    context = cache.shape[1]
    n_queries = 2 * images * GROUP

    cut = columns_dev // 2
    keep, give = pl.pallas_call(
        split_kernel,
        grid_spec=pltpu.PrefetchScalarGridSpec(
            num_scalar_prefetch=1,
            grid=(2,),
            in_specs=[
                pl.BlockSpec((rows_dev, cut), lambda i, core_ref: (0, 2 * i + core_ref[0])),
                pl.BlockSpec((rows_dev, cut), lambda i, core_ref: (0, 2 * i + 1 - core_ref[0])),
            ],
            out_specs=[pl.BlockSpec((rows_dev, cut), lambda i, core_ref: (0, i))] * 2,
        ),
        out_shape=[jax.ShapeDtypeStruct((rows_dev, columns_dev), jnp.bfloat16)] * 2,
        cost_estimate=pl.CostEstimate(flops=0, bytes_accessed=2 * 2**20, transcendentals=0),
        name="split",
    )(core.reshape(1), kv_weight, kv_weight)
    taken = swap_core(give)
    other = swap_core(prompt_states)

    owner_and_row = jnp.stack([image_owner, image_row])
    chip_images = jnp.concatenate([owner_and_row, swap_core(owner_and_row)], axis=1)
    send_q = queries.reshape(decode_rows, 2, HALF_QH * HD).transpose(1, 0, 2)
    send_q = jnp.broadcast_to(send_q[None], (n // 2, 2, decode_rows, HALF_QH * HD)).reshape(
        n, decode_rows, HALF_QH * HD
    )
    all_q = lax.all_to_all(send_q, "section", split_axis=0, concat_axis=0, tiled=True)
    all_q = all_q.reshape(n * decode_rows, HALF_QH * HD)
    target = chip_images[0] * decode_rows + chip_images[1]
    pick = (target[:, None] == jnp.arange(n * decode_rows)[None, :]).astype(jnp.bfloat16)
    image_q = jnp.dot(pick, all_q, preferred_element_type=jnp.float32).astype(jnp.bfloat16)
    image_q = image_q.reshape(2 * images, HALF_KVH, GROUP, HD).transpose(1, 0, 2, 3)
    image_q = image_q.reshape(HALF_KVH, n_queries, HD)

    which = jnp.concatenate([jnp.full((images,), core), jnp.full((images,), 1 - core)]).astype(jnp.int32)
    slot = jnp.stack([chip_images[0], which])
    row_lane = jnp.broadcast_to(jnp.repeat(which * LANES + chip_images[1], GROUP)[:, None], (n_queries, HD))

    res_out, res_top, res_sum = pl.pallas_call(
        resident_kernel,
        grid_spec=pltpu.PrefetchScalarGridSpec(
            num_scalar_prefetch=1,
            grid=(decode_rows,),
            in_specs=[
                pl.BlockSpec((1, QH, HD), lambda i, *_: (i, 0, 0)),
                pl.BlockSpec((1, context, kv_width), lambda i, *_: (i, 0, 0)),
            ],
            out_specs=[pl.BlockSpec((1, QH, HD), lambda i, *_: (i, 0, 0)), whole((QH, HD)), whole((QH, HD))],
        ),
        out_shape=[
            jax.ShapeDtypeStruct((decode_rows, QH, HD), jnp.float32),
            jax.ShapeDtypeStruct((QH, HD), jnp.float32),
            jax.ShapeDtypeStruct((QH, HD), jnp.float32),
        ],
        compiler_params=pltpu.CompilerParams(vmem_limit_bytes=16 * 2**20),
        cost_estimate=pl.CostEstimate(flops=2**28, bytes_accessed=24 * 2**20, transcendentals=0),
        name="resident",
    )(context_length, queries.reshape(decode_rows, QH, HD), cache)

    def product(groups, carry, name, last=False):
        arrays, layout, blocks = [], [], []
        for block, array, start in groups:
            at = [i for i, known in enumerate(arrays) if known is array]
            if not at:
                arrays.append(array)
                at = [len(arrays) - 1]
            layout.append((at[0], start))
            blocks.append(jnp.asarray(block, jnp.int32))
        steps = len(groups)
        token_spec = pl.BlockSpec((tokens, rows_dev), lambda i, block_ref, *_: (0, block_ref[i]))
        sums = [whole((2 * tokens, columns_dev)), whole((2 * tokens, HD))]
        sum_shapes = [
            jax.ShapeDtypeStruct((2 * tokens, columns_dev), jnp.float32),
            jax.ShapeDtypeStruct((2 * tokens, HD), jnp.float32),
        ]
        scratch = [pltpu.VMEM((steps, rows_dev, columns_dev), jnp.bfloat16)]
        in_specs = [token_spec, token_spec]
        scalars = [jnp.stack(blocks)]
        inputs = [prompt_states, other]
        kernel = first_kernel
        if carry is not None:
            kernel = next_kernel
            in_specs = in_specs + sums
            inputs = inputs + list(carry)
        out_specs, out_shape = sums, sum_shapes
        body = functools.partial(kernel, layout, len(arrays))
        if last:
            body = functools.partial(last_kernel, layout, len(arrays), width)
            scalars = scalars + [slot]
            in_specs = in_specs + [whole((HALF_KVH, n_queries, HD)), whole((n_queries, HD))]
            inputs = inputs + [image_q, row_lane]
            out_specs = whole((n, 3, HALF_QH, HD))
            out_shape = jax.ShapeDtypeStruct((n, 3, HALF_QH, HD), jnp.bfloat16)
            scratch = scratch + [
                pltpu.VMEM((2 * tokens, columns_dev), jnp.float32),
                pltpu.VMEM((2 * tokens, HD), jnp.float32),
                pltpu.VMEM((2 * images, HALF_QH, HD), jnp.float32),
                pltpu.VMEM((2 * images, HALF_QH, HD), jnp.float32),
            ]
        return pl.pallas_call(
            body,
            grid_spec=pltpu.PrefetchScalarGridSpec(
                num_scalar_prefetch=len(scalars),
                grid=(steps,),
                in_specs=in_specs + [pl.BlockSpec(memory_space=pl.ANY)] * len(arrays),
                out_specs=out_specs,
                scratch_shapes=scratch + [pltpu.SemaphoreType.DMA((steps,))],
            ),
            out_shape=out_shape,
            compiler_params=pltpu.CompilerParams(vmem_limit_bytes=56 * 2**20),
            cost_estimate=pl.CostEstimate(
                flops=2 * 2 * tokens * rows_dev * columns_dev * steps,
                bytes_accessed=5 * steps * 2**20,
                transcendentals=0,
            ),
            name=name,
        )(*scalars, *inputs, *arrays)

    if n == 16 and lax.axis_size("replica") == 2:
        chips = ring_chips()
        at_a = {name: chip * 2 + core for name, chip in chips.items()}
        at_b = {name: chip * 2 + 1 - core for name, chip in chips.items()}

        def rows(at, names, arrays):
            return [(at[name], array, 0) for name, array in zip(names, arrays)]

        step1 = ("own", "behind", "own_y")
        step2 = ("ahead", "opposite", "behind_y")
        step3 = ("ahead_y", "opposite_y")
        a1 = (keep, along_ring(keep), across_y(keep))
        b1 = (taken, along_ring(taken), across_y(taken))
        a2 = (across_replica(a1[1]), along_ring(a1[1]), across_y(a1[1]))
        b_behind, res_out = lax.optimization_barrier((b1[1], res_out))
        b2 = (across_replica(b_behind), along_ring(b_behind), across_y(b_behind))
        carry = product(rows(at_a, step1, a1) + rows(at_b, step1, b1), None, "rows_1")
        a_behind_y, a_opposite, carry = lax.optimization_barrier((a2[2], a2[1], carry))
        a3 = (across_replica(a_behind_y), across_y(a_opposite))
        carry = product(rows(at_a, step2, a2), carry, "rows_2a")
        b_behind_y, carry = lax.optimization_barrier((b2[2], carry))
        b3 = (across_replica(b_behind_y), along_ring(b_behind_y))
        carry = product(rows(at_b, step2, b2), carry, "rows_2b")
        carry = product(rows(at_a, step3, a3), carry, "rows_3a")
        slots = product(rows(at_b, step3, b3), carry, "rows_3b", last=True)
    else:
        a = [(chip * 2 + core, array, start) for chip, array, start in gather_plain(keep)]
        b = [(chip * 2 + 1 - core, array, start) for chip, array, start in gather_plain(taken)]
        slots = product(b, product(a, None, "rows_a"), "rows_b", last=True)
    got = lax.all_to_all(slots, "section", split_axis=0, concat_axis=0, tiled=True)

    return pl.pallas_call(
        combine_kernel,
        grid=(1,),
        in_specs=[
            whole((n, 3, HALF_QH, HD)),
            whole((decode_rows, QH, HD)),
            whole((QH, HD)),
            whole((QH, HD)),
        ],
        out_specs=whole((decode_rows, QH * HD)),
        scratch_shapes=[pltpu.VMEM((decode_rows, QH, HD), jnp.float32)],
        out_shape=jax.ShapeDtypeStruct((decode_rows, QH * HD), jnp.bfloat16),
        compiler_params=pltpu.CompilerParams(vmem_limit_bytes=32 * 2**20),
        name="combine",
    )(got, res_out, res_top, res_sum)


def solution(mesh):
    placed = (
        P(("replica", "section"), None),
        P("section", None),
        P(("replica", "section")),
        P(("replica", "section")),
        P(("replica", "section"), None),
        P(("replica", "section"), None, None),
        P(("replica", "section")),
    )
    return jax.shard_map(
        per_device,
        mesh=mesh,
        in_specs=placed,
        out_specs=P(("replica", "section"), None),
        check_vma=False,
    )
```

```python
import functools
import math

import jax
import jax.numpy as jnp
import numpy as np
from jax import lax
from jax.experimental import pallas as pl
from jax.experimental.pallas import tpu as pltpu
from jax.sharding import PartitionSpec as P

HD = 128
KVH = 4
QH = 32
IMG_TOK = 64
GROUP = QH // KVH
HALF_KVH = KVH // 2
HALF_QH = QH // 2
SCALE = 1.0 / math.sqrt(HD)
EPS = 1e-05

LANES = 64
N_KINDS = 7

masked_score = -1e30


def swap_core(x):
    n = lax.axis_size("section")
    return lax.ppermute(x, "section", [(i, i ^ 1) for i in range(n)])


def gather_plain(chunk):
    n = lax.axis_size("section")
    rows = chunk.shape[0]
    groups = [list(range(core, n, 2)) for core in range(2)]
    whole = lax.all_gather(chunk, "section", axis=0, tiled=True, axis_index_groups=groups)
    return [(chip, whole, chip * rows) for chip in range(n // 2)]


RING = [0, 1, 3, 2]


def along_ring(x):
    perm = []
    for rep, way in ((0, 1), (1, -1)):
        for p in range(4):
            for low in range(4):
                perm.append((rep * 16 + RING[p] * 4 + low, rep * 16 + RING[(p + way) % 4] * 4 + low))
    return lax.ppermute(x, ("replica", "section"), perm)


def across_y(x):
    return lax.ppermute(x, "section", [(i, i ^ 2) for i in range(16)])


def across_replica(x):
    return lax.ppermute(x, "replica", [(0, 1), (1, 0)])


STEPS = (("own", "behind", "own_y"), ("ahead", "opposite", "behind_y"), ("ahead_y", "opposite_y"))


def block_table():
    table = []
    for rep in range(2):
        for section in range(16):
            z, y, core = section // 4, section // 2 % 2, section % 2
            way = 1 - 2 * rep
            place = RING.index(z)
            ring = {"own": place, "behind": place - way, "ahead": place + way, "opposite": place + 2}

            def blocks(step, other):
                out = []
                for name in STEPS[step]:
                    chip = RING[ring[name.removesuffix("_y")] % 4] * 2 + (1 - y if name.endswith("_y") else y)
                    out.append(chip * 2 + (core ^ other))
                return out

            table.append(blocks(0, 0) + blocks(0, 1) + blocks(1, 0) + blocks(1, 1) + blocks(2, 0) + blocks(2, 1))
    return np.array(table, np.int32)


def square_kernel(states_ref, out_ref):
    total = None
    for i in range(0, states_ref.shape[1], HD):
        values = states_ref[:, i : i + HD].astype(jnp.float32)
        values = values * values
        total = values if total is None else total + values
    out_ref[...] = total


def split_kernel(core_ref, keep_in, give_in, keep_ref, give_ref):
    keep_ref[...] = keep_in[...]
    give_ref[...] = give_in[...]


def accumulate(layout, token_refs, piece_refs, weight, total, sems, carry_ref=None, carry=None):
    step = pl.program_id(0)
    depth = token_refs[0].shape[1]
    copies = [
        pltpu.make_async_copy(
            piece_refs[which].at[pl.ds(start, depth)], weight.at[pl.ds(i * depth, depth)], sems.at[i]
        )
        for i, (which, start) in enumerate(layout)
    ]
    carried = []
    if carry_ref is not None:
        carried = [pltpu.make_async_copy(carry_ref, carry, sems.at[len(layout)])]

    @pl.when(step == 0)
    def _():
        for copy in copies + carried:
            copy.start()

    for i in range(0, len(copies), 2):

        @pl.when(step == i // 2)
        def _():
            copies[i].wait()
            copies[i + 1].wait()

    states = jnp.concatenate(
        [
            jnp.concatenate([token_refs[0][...], token_refs[1][...]], axis=1),
            jnp.concatenate([token_refs[2][...], token_refs[3][...]], axis=1),
        ],
        axis=0,
    )
    block = weight[pl.ds(pl.multiple_of(step * 2 * depth, 2 * depth), 2 * depth), :]
    product = jnp.dot(states, block, preferred_element_type=jnp.float32)

    @pl.when(step == 0)
    def _():
        total[...] = product

    @pl.when(step > 0)
    def _():
        total[...] += product

    if carry_ref is not None:

        @pl.when(step == pl.num_programs(0) - 1)
        def _():
            carried[0].wait()
            total[...] += carry[...]


def first_kernel(layout, block_ref, *refs):
    total, weight, sems = refs[-3:]
    accumulate(layout, refs[:4], refs[4:-3], weight, total, sems)


def next_kernel(layout, block_ref, *refs):
    total, weight, carry, sems = refs[-4:]
    accumulate(layout, refs[:4], refs[5:-4], weight, total, sems, refs[4], carry)


def parts_of(values, count):
    out = []
    for _ in range(count):
        part = values.astype(jnp.bfloat16).astype(jnp.float32)
        out.append(part)
        values = values - part
    return out


def last_kernel(layout, width, block_ref, slot_ref, *refs):
    query_ref, row_lane_ref, own_squares, other_squares = refs[5:9]
    slots_ref, weight, carry, total, summed, stats, sems = refs[-7:]
    images = query_ref.shape[1] // GROUP

    @pl.when(pl.program_id(0) == 0)
    def _():
        slots_ref[...] = jnp.zeros_like(slots_ref)

    accumulate(layout, refs[:4], refs[9:-7], weight, total, sems, refs[4], carry)

    @pl.when(pl.program_id(0) == pl.num_programs(0) - 1)
    def _():
        tokens = total.shape[0]
        queries = query_ref.shape[1]
        squares = jnp.concatenate([own_squares[...], other_squares[...]], axis=0)
        factor = lax.rsqrt(jnp.sum(squares, axis=1, keepdims=True) / width + EPS)
        image_of_query = lax.broadcasted_iota(jnp.int32, (queries, tokens), 0) // GROUP
        image_of_token = lax.broadcasted_iota(jnp.int32, (queries, tokens), 1) // IMG_TOK
        live = image_of_query == image_of_token
        lane = lax.broadcasted_iota(jnp.int32, (queries, HD), 1)
        first_lane = row_lane_ref[:, :1]
        for head in range(HALF_KVH):
            part = slice(head * GROUP, (head + 1) * GROUP)
            keys = (total[:, head * HD : (head + 1) * HD] * factor).astype(jnp.bfloat16)
            at = (HALF_KVH + head) * HD
            values = (total[:, at : at + HD] * factor).astype(jnp.bfloat16)
            scores = (
                lax.dot_general(
                    query_ref[head], keys, (((1,), (1,)), ((), ())), preferred_element_type=jnp.float32
                )
                * SCALE
            )
            scores = jnp.where(live, scores, masked_score)
            top = jnp.max(scores, axis=1, keepdims=True)
            weights = jnp.where(live, jnp.exp(scores - top), 0.0)
            total_weight = jnp.sum(weights, axis=1, keepdims=True)
            out = jnp.dot(weights.astype(jnp.bfloat16), values, preferred_element_type=jnp.float32)
            summed[:, part, :] = out.reshape(images, GROUP, HD)
            kinds = parts_of(top, 3) + parts_of(total_weight, 3) + [jnp.ones_like(top)]
            tile = jnp.zeros((queries, HD), jnp.float32)
            for kind, column in enumerate(kinds):
                tile = jnp.where(lane == first_lane + kind * 8, column, tile)
            stats[:, part, :] = tile.reshape(images, GROUP, HD)
        for image in range(images):
            owner, which = slot_ref[0, image], slot_ref[1, image]
            slots_ref[owner, which] = summed[image].astype(jnp.bfloat16)
            slots_ref[owner, 2] = slots_ref[owner, 2] + stats[image].astype(jnp.bfloat16)


def resident_kernel(length_ref, query_ref, cache_ref, out_ref, top_ref, sum_ref):
    step = pl.program_id(0)
    rows, context = cache_ref.shape[:2]
    place = lax.broadcasted_iota(jnp.int32, (QH, context), 1)
    lane = lax.broadcasted_iota(jnp.int32, (QH, HD), 1)

    @pl.when(step == 0)
    def _():
        top_ref[...] = jnp.zeros_like(top_ref)
        sum_ref[...] = jnp.zeros_like(sum_ref)

    parts = [slice(head * GROUP, (head + 1) * GROUP) for head in range(KVH)]
    scores = [
        jnp.concatenate(
            [
                lax.dot_general(
                    query_ref[row, part, :],
                    cache_ref[row, :, head * HD : (head + 1) * HD],
                    (((1,), (1,)), ((), ())),
                    preferred_element_type=jnp.float32,
                )
                for head, part in enumerate(parts)
            ],
            axis=0,
        )
        for row in range(rows)
    ]
    for row in range(rows):
        live = place < length_ref[step * rows + row]
        score = jnp.where(live, scores[row] * SCALE, masked_score)
        top = jnp.max(score, axis=1, keepdims=True)
        weights = jnp.where(live, jnp.exp(score - top), 0.0)
        mine = lane == step * rows + row
        top_ref[...] = jnp.where(mine, top, top_ref[...])
        sum_ref[...] = jnp.where(mine, jnp.sum(weights, axis=1, keepdims=True), sum_ref[...])
        weights = weights.astype(jnp.bfloat16)
        for head, part in enumerate(parts):
            at = (KVH + head) * HD
            out_ref[row, part, :] = jnp.dot(
                weights[part], cache_ref[row, :, at : at + HD], preferred_element_type=jnp.float32
            )


def combine_kernel(got_ref, res_out_ref, res_top_ref, res_sum_ref, out_ref, acc):
    chips = got_ref.shape[0] // 2
    rows = res_out_ref.shape[0]
    lane = lax.broadcasted_iota(jnp.int32, (HALF_QH, HD), 1)
    head_lane = (lane % LANES) < 8

    def moved(tile, by):
        return pltpu.roll(tile, HD - by, 1)

    for core in range(2):
        part = slice(core * HALF_QH, (core + 1) * HALF_QH)
        tops, sums, here = [], [], []
        for chip in range(chips):
            tile = got_ref[chip * 2 + core, 2].astype(jnp.float32)
            present = (moved(tile, 48) > 0.5) & head_lane
            tops.append(jnp.where(present, tile + moved(tile, 8) + moved(tile, 16), masked_score))
            sums.append(moved(tile, 24) + moved(tile, 32) + moved(tile, 40))
            here.append(present)
        row_top = functools.reduce(jnp.maximum, tops)
        row_top = jnp.maximum(row_top, pltpu.roll(row_top, LANES, 1))
        res_top = jnp.where(lane < 8, res_top_ref[part, :], masked_score)
        res_top = jnp.maximum(res_top, pltpu.roll(res_top, LANES, 1))
        row_top = jnp.maximum(row_top, res_top)
        weights = [jnp.where(a, jnp.exp(t - row_top), 0.0) for a, t in zip(here, tops)]
        joined = sum(w * s for w, s in zip(weights, sums))
        res_weight = jnp.exp(res_top - row_top)
        denominator = joined + pltpu.roll(joined, LANES, 1) + res_weight * res_sum_ref[part, :]
        scale = jnp.where(lane < 8, 1.0 / denominator, 0.0)
        scale = scale + pltpu.roll(scale, LANES, 1)
        res_share = res_weight * scale
        weights = [w * scale for w in weights]
        for row in range(rows):
            value = res_out_ref[row, part, :] * res_share[:, row : row + 1]
            for chip in range(chips):
                for which in range(2):
                    at = which * LANES + row
                    value += weights[chip][:, at : at + 1] * got_ref[chip * 2 + core, which].astype(jnp.float32)
            acc[row, part, :] = value
    for head in range(QH):
        out_ref[:, head * HD : (head + 1) * HD] = acc[:, head, :].astype(jnp.bfloat16)


def whole(shape):
    return pl.BlockSpec(shape, lambda i, *_: (0,) * len(shape))


def per_device(prompt_states, kv_weight, image_owner, image_row, queries, cache, context_length):
    n = lax.axis_size("section")
    section = lax.axis_index("section")
    core = section % 2
    tokens, width = prompt_states.shape
    rows_dev, kv_width = kv_weight.shape
    columns_dev = kv_width // 2
    images = image_owner.shape[0]
    decode_rows = queries.shape[0]
    context = cache.shape[1]
    n_queries = 2 * images * GROUP

    cut = columns_dev // 2
    keep, give = pl.pallas_call(
        split_kernel,
        grid_spec=pltpu.PrefetchScalarGridSpec(
            num_scalar_prefetch=1,
            grid=(2,),
            in_specs=[
                pl.BlockSpec((rows_dev, cut), lambda i, core_ref: (0, 2 * i + core_ref[0])),
                pl.BlockSpec((rows_dev, cut), lambda i, core_ref: (0, 2 * i + 1 - core_ref[0])),
            ],
            out_specs=[pl.BlockSpec((rows_dev, cut), lambda i, core_ref: (0, i))] * 2,
        ),
        out_shape=[jax.ShapeDtypeStruct((rows_dev, columns_dev), jnp.bfloat16)] * 2,
        cost_estimate=pl.CostEstimate(flops=0, bytes_accessed=2 * 2**20, transcendentals=0),
        name="split",
    )(core.reshape(1), kv_weight, kv_weight)
    taken = swap_core(give)
    squares = pl.pallas_call(
        square_kernel,
        grid=(8,),
        in_specs=[pl.BlockSpec((tokens // 8, width), lambda i: (i, 0))],
        out_specs=pl.BlockSpec((tokens // 8, HD), lambda i: (i, 0)),
        out_shape=jax.ShapeDtypeStruct((tokens, HD), jnp.float32),
        cost_estimate=pl.CostEstimate(flops=2 * tokens * width, bytes_accessed=16 * 2**20, transcendentals=0),
        compiler_params=pltpu.CompilerParams(vmem_limit_bytes=56 * 2**20),
        name="squares",
    )(prompt_states)
    swapped_states, tied = lax.optimization_barrier((prompt_states, taken))
    other = swap_core(swapped_states)
    other_squares = swap_core(squares)

    owner_and_row = jnp.stack([image_owner, image_row])
    chip_images = jnp.concatenate([owner_and_row, swap_core(owner_and_row)], axis=1)
    send_q = queries.reshape(decode_rows, 2, HALF_QH * HD).transpose(1, 0, 2)
    send_q = jnp.broadcast_to(send_q[None], (n // 2, 2, decode_rows, HALF_QH * HD)).reshape(
        n, decode_rows, HALF_QH * HD
    )
    all_q = lax.all_to_all(send_q, "section", split_axis=0, concat_axis=0, tiled=True)
    all_q = all_q.reshape(n * decode_rows, HALF_QH * HD)
    target = chip_images[0] * decode_rows + chip_images[1]
    pick = (target[:, None] == jnp.arange(n * decode_rows)[None, :]).astype(jnp.bfloat16)
    image_q = jnp.dot(pick, all_q, preferred_element_type=jnp.float32).astype(jnp.bfloat16)
    image_q = image_q.reshape(2 * images, HALF_KVH, GROUP, HD).transpose(1, 0, 2, 3)
    image_q = image_q.reshape(HALF_KVH, n_queries, HD)

    which = jnp.concatenate([jnp.full((images,), core), jnp.full((images,), 1 - core)]).astype(jnp.int32)
    slot = jnp.stack([chip_images[0], which])
    row_lane = jnp.broadcast_to(jnp.repeat(which * LANES + chip_images[1], GROUP)[:, None], (n_queries, HD))

    def resident(length):
        step_rows = 2
        return pl.pallas_call(
            resident_kernel,
            grid_spec=pltpu.PrefetchScalarGridSpec(
                num_scalar_prefetch=1,
                grid=(decode_rows // step_rows,),
                in_specs=[
                    pl.BlockSpec((step_rows, QH, HD), lambda i, *_: (i, 0, 0)),
                    pl.BlockSpec((step_rows, context, kv_width), lambda i, *_: (i, 0, 0)),
                ],
                out_specs=[
                    pl.BlockSpec((step_rows, QH, HD), lambda i, *_: (i, 0, 0)),
                    whole((QH, HD)),
                    whole((QH, HD)),
                ],
            ),
            out_shape=[
                jax.ShapeDtypeStruct((decode_rows, QH, HD), jnp.float32),
                jax.ShapeDtypeStruct((QH, HD), jnp.float32),
                jax.ShapeDtypeStruct((QH, HD), jnp.float32),
            ],
            compiler_params=pltpu.CompilerParams(vmem_limit_bytes=56 * 2**20),
            cost_estimate=pl.CostEstimate(flops=2**28, bytes_accessed=20 * 2**20, transcendentals=0),
            name="resident",
        )(length, queries.reshape(decode_rows, QH, HD), cache)

    def product(blocks, pieces, carry, name, last=False):
        arrays, layout = [], []
        for array, start in pieces:
            at = [i for i, known in enumerate(arrays) if known is array]
            if not at:
                arrays.append(array)
                at = [len(arrays) - 1]
            layout.append((at[0], start))
        steps = len(pieces) // 2
        first = pl.BlockSpec((tokens, rows_dev), lambda i, block_ref, *_: (0, block_ref[2 * i]))
        second = pl.BlockSpec((tokens, rows_dev), lambda i, block_ref, *_: (0, block_ref[2 * i + 1]))
        in_hbm = pl.BlockSpec(memory_space=pltpu.HBM)
        in_specs = [first, second, first, second]
        inputs = [prompt_states, prompt_states, other, other]
        scalars = [blocks]
        scratch = [pltpu.VMEM((len(pieces) * rows_dev, columns_dev), jnp.bfloat16)]
        total = (2 * tokens, columns_dev)
        body = functools.partial(first_kernel, layout)
        if carry is not None:
            body = functools.partial(next_kernel, layout)
            in_specs = in_specs + [pl.BlockSpec(memory_space=pl.ANY)]
            inputs = inputs + [carry]
            scratch = scratch + [pltpu.VMEM(total, jnp.float32)]
        out_specs, out_shape = whole(total), jax.ShapeDtypeStruct(total, jnp.float32)
        if last:
            body = functools.partial(last_kernel, layout, width)
            scalars = scalars + [slot]
            in_specs = in_specs + [
                whole((HALF_KVH, n_queries, HD)),
                whole((n_queries, HD)),
                whole((tokens, HD)),
                whole((tokens, HD)),
            ]
            inputs = inputs + [image_q, row_lane, squares, other_squares]
            out_specs = whole((n, 3, HALF_QH, HD))
            out_shape = jax.ShapeDtypeStruct((n, 3, HALF_QH, HD), jnp.bfloat16)
            scratch = scratch + [
                pltpu.VMEM(total, jnp.float32),
                pltpu.VMEM((2 * images, HALF_QH, HD), jnp.float32),
                pltpu.VMEM((2 * images, HALF_QH, HD), jnp.float32),
            ]
        return pl.pallas_call(
            body,
            grid_spec=pltpu.PrefetchScalarGridSpec(
                num_scalar_prefetch=len(scalars),
                grid=(steps,),
                in_specs=in_specs + [in_hbm] * len(arrays),
                out_specs=out_specs,
                scratch_shapes=scratch + [pltpu.SemaphoreType.DMA((len(pieces) + 1,))],
            ),
            out_shape=out_shape,
            compiler_params=pltpu.CompilerParams(vmem_limit_bytes=56 * 2**20),
            cost_estimate=pl.CostEstimate(
                flops=2 * 2 * tokens * 2 * rows_dev * columns_dev * steps,
                bytes_accessed=10 * steps * 2**20,
                transcendentals=0,
            ),
            name=name,
        )(*scalars, *inputs, *arrays)

    if n == 16 and lax.axis_size("replica") == 2:
        blocks = jnp.array(block_table())[lax.axis_index("replica") * 16 + section]

        def starts(*arrays):
            return [(array, 0) for array in arrays]

        a1 = (keep, along_ring(keep), across_y(keep))
        b1 = (taken, along_ring(taken), across_y(taken))
        a2 = (across_replica(a1[1]), along_ring(a1[1]), across_y(a1[1]))
        length, tied = lax.optimization_barrier((context_length, a1[1]))
        res_out, res_top, res_sum = resident(length)
        b2 = (across_replica(b1[1]), along_ring(b1[1]), across_y(b1[1]))
        total = product(blocks[:6], starts(*a1, *b1), None, "rows_1")
        a_behind_y, a_opposite, total = lax.optimization_barrier((a2[2], a2[1], total))
        a3 = (across_replica(a_behind_y), across_y(a_opposite))
        b_behind_y, res_out = lax.optimization_barrier((b2[2], res_out))
        b3 = (across_replica(b_behind_y), along_ring(b_behind_y))
        total = product(blocks[6:12], starts(*a2, *b2), total, "rows_2")
        total = product(blocks[12:14], starts(*a3), total, "rows_3a")
        slots = product(blocks[14:], starts(*b3), total, "rows_3b", last=True)
    else:
        res_out, res_top, res_sum = resident(context_length)
        a = gather_plain(keep)
        b = gather_plain(taken)
        chips = jnp.array([chip for chip, _, _ in a], jnp.int32)
        total = product(chips * 2 + core, [piece[1:] for piece in a], None, "rows_a")
        slots = product(chips * 2 + 1 - core, [piece[1:] for piece in b], total, "rows_b", last=True)
    got = lax.all_to_all(slots, "section", split_axis=0, concat_axis=0, tiled=True)

    return pl.pallas_call(
        combine_kernel,
        grid=(1,),
        in_specs=[
            whole((n, 3, HALF_QH, HD)),
            whole((decode_rows, QH, HD)),
            whole((QH, HD)),
            whole((QH, HD)),
        ],
        out_specs=whole((decode_rows, QH * HD)),
        scratch_shapes=[pltpu.VMEM((decode_rows, QH, HD), jnp.float32)],
        out_shape=jax.ShapeDtypeStruct((decode_rows, QH * HD), jnp.bfloat16),
        compiler_params=pltpu.CompilerParams(vmem_limit_bytes=32 * 2**20),
        name="combine",
    )(got, res_out, res_top, res_sum)


def solution(mesh):
    placed = (
        P(("replica", "section"), None),
        P("section", None),
        P(("replica", "section")),
        P(("replica", "section")),
        P(("replica", "section"), None),
        P(("replica", "section"), None, None),
        P(("replica", "section")),
    )
    return jax.shard_map(
        per_device,
        mesh=mesh,
        in_specs=placed,
        out_specs=P(("replica", "section"), None),
        check_vma=False,
    )
```

```python
import functools
import math

import jax
import jax.numpy as jnp
import numpy as np
from jax import lax
from jax.experimental import pallas as pl
from jax.experimental.pallas import tpu as pltpu
from jax.sharding import PartitionSpec as P

HD = 128
KVH = 4
QH = 32
IMG_TOK = 64
GROUP = QH // KVH
HALF_KVH = KVH // 2
HALF_QH = QH // 2
SCALE = 1.0 / math.sqrt(HD)
EPS = 1e-05

LANES = 64
N_KINDS = 7

masked_score = -1e30


def swap_core(x):
    n = lax.axis_size("section")
    return lax.ppermute(x, "section", [(i, i ^ 1) for i in range(n)])


def gather_plain(chunk):
    n = lax.axis_size("section")
    rows = chunk.shape[0]
    groups = [list(range(core, n, 2)) for core in range(2)]
    whole = lax.all_gather(chunk, "section", axis=0, tiled=True, axis_index_groups=groups)
    return [(chip, whole, chip * rows) for chip in range(n // 2)]


RING = [0, 1, 3, 2]


def along_ring(x):
    perm = []
    for rep, way in ((0, 1), (1, -1)):
        for p in range(4):
            for low in range(4):
                perm.append((rep * 16 + RING[p] * 4 + low, rep * 16 + RING[(p + way) % 4] * 4 + low))
    return lax.ppermute(x, ("replica", "section"), perm)


def across_y(x):
    return lax.ppermute(x, "section", [(i, i ^ 2) for i in range(16)])


def across_replica(x):
    return lax.ppermute(x, "replica", [(0, 1), (1, 0)])


STEPS = (("own", "behind", "own_y"), ("ahead", "opposite", "behind_y"), ("ahead_y", "opposite_y"))


def block_table():
    table = []
    for rep in range(2):
        for section in range(16):
            z, y, core = section // 4, section // 2 % 2, section % 2
            way = 1 - 2 * rep
            place = RING.index(z)
            ring = {"own": place, "behind": place - way, "ahead": place + way, "opposite": place + 2}

            def blocks(step, other):
                out = []
                for name in STEPS[step]:
                    chip = RING[ring[name.removesuffix("_y")] % 4] * 2 + (1 - y if name.endswith("_y") else y)
                    out.append(chip * 2 + (core ^ other))
                return out

            (own_a, *one_a), (own_b, *one_b) = blocks(0, 0), blocks(0, 1)
            two_a, two_b = blocks(1, 0), blocks(1, 1)
            table.append(one_a + one_b + [own_a] + two_a + [own_b] + two_b + blocks(2, 0) + blocks(2, 1))
    return np.array(table, np.int32)


def square_kernel(states_ref, out_ref):
    total = None
    for i in range(0, states_ref.shape[1], HD):
        values = states_ref[:, i : i + HD].astype(jnp.float32)
        values = values * values
        total = values if total is None else total + values
    out_ref[...] = jnp.sum(total, axis=1, keepdims=True)


def split_kernel(core_ref, keep_in, give_in, keep_ref, give_ref):
    keep_ref[...] = keep_in[...]
    give_ref[...] = give_in[...]


def accumulate(layout, token_refs, piece_refs, weight, total, sems, carry_ref=None, carry=None):
    pair, half = pl.program_id(0), pl.program_id(1)
    tokens, depth = token_refs[0].shape
    copies = [
        pltpu.make_async_copy(
            piece_refs[which].at[pl.ds(start, depth)], weight.at[pl.ds(i * depth, depth)], sems.at[i]
        )
        for i, (which, start) in enumerate(layout)
    ]
    carried = []
    if carry_ref is not None:
        carried = [pltpu.make_async_copy(carry_ref, carry, sems.at[len(layout)])]

    @pl.when((pair == 0) & (half == 0))
    def _():
        for copy in copies + carried:
            copy.start()

    for i in range(0, len(copies), 2):

        @pl.when((pair == i // 2) & (half == 0))
        def _():
            copies[i].wait()
            copies[i + 1].wait()

    for side in range(2):

        @pl.when(half == side)
        def _():
            states = jnp.concatenate([token_refs[2 * side][...], token_refs[2 * side + 1][...]], axis=1)
            block = weight[pl.ds(pl.multiple_of(pair * 2 * depth, 2 * depth), 2 * depth), :]
            product = jnp.dot(states, block, preferred_element_type=jnp.float32)
            rows = pl.ds(side * tokens, tokens)

            @pl.when(pair == 0)
            def _():
                total[rows, :] = product

            @pl.when(pair > 0)
            def _():
                total[rows, :] += product

    if carry_ref is not None:

        @pl.when((pair == pl.num_programs(0) - 1) & (half == 1))
        def _():
            carried[0].wait()
            total[...] += carry[...]


def first_kernel(layout, block_ref, *refs):
    total, weight, sems = refs[-3:]
    accumulate(layout, refs[:4], refs[4:-3], weight, total, sems)


def next_kernel(layout, block_ref, *refs):
    total, weight, carry, sems = refs[-4:]
    accumulate(layout, refs[:4], refs[5:-4], weight, total, sems, refs[4], carry)


def parts_of(values, count):
    out = []
    for _ in range(count):
        part = values.astype(jnp.bfloat16).astype(jnp.float32)
        out.append(part)
        values = values - part
    return out


def last_kernel(layout, width, block_ref, slot_ref, *refs):
    query_ref, factor_ref = refs[5:7]
    slots_ref, weight, carry, total, summed, stats, sems = refs[-7:]
    images = query_ref.shape[1] // GROUP

    @pl.when((pl.program_id(0) == 0) & (pl.program_id(1) == 0))
    def _():
        slots_ref[...] = jnp.zeros_like(slots_ref)

    accumulate(layout, refs[:4], refs[7:-7], weight, total, sems, refs[4], carry)

    @pl.when((pl.program_id(0) == pl.num_programs(0) - 1) & (pl.program_id(1) == 1))
    def _():
        tokens = total.shape[0]
        queries = query_ref.shape[1]
        factor = lax.rsqrt(factor_ref[...] / width + EPS)
        image_of_query = lax.broadcasted_iota(jnp.int32, (queries, tokens), 0) // GROUP
        image_of_token = lax.broadcasted_iota(jnp.int32, (queries, tokens), 1) // IMG_TOK
        live = image_of_query == image_of_token
        lane = lax.broadcasted_iota(jnp.int32, (queries, HD), 1)
        for head in range(HALF_KVH):
            part = slice(head * GROUP, (head + 1) * GROUP)
            keys = (total[:, head * HD : (head + 1) * HD] * factor).astype(jnp.bfloat16)
            at = (HALF_KVH + head) * HD
            values = (total[:, at : at + HD] * factor).astype(jnp.bfloat16)
            scores = (
                lax.dot_general(
                    query_ref[head], keys, (((1,), (1,)), ((), ())), preferred_element_type=jnp.float32
                )
                * SCALE
            )
            scores = jnp.where(live, scores, masked_score)
            top = jnp.max(scores, axis=1, keepdims=True)
            weights = jnp.where(live, jnp.exp(scores - top), 0.0)
            total_weight = jnp.sum(weights, axis=1, keepdims=True)
            out = jnp.dot(weights.astype(jnp.bfloat16), values, preferred_element_type=jnp.float32)
            summed[:, part, :] = out.reshape(images, GROUP, HD)
            kinds = parts_of(top, 3) + parts_of(total_weight, 3) + [jnp.ones_like(top)]
            tile = jnp.zeros((queries, HD), jnp.float32)
            for kind, column in enumerate(kinds):
                tile = jnp.where(lane == kind * 8, column, tile)
            stats[:, part, :] = tile.reshape(images, GROUP, HD)
        for image in range(images):
            owner, which = slot_ref[0, image], slot_ref[1, image]
            slots_ref[owner, which] = summed[image].astype(jnp.bfloat16)
            tile = pltpu.roll(stats[image], which * LANES + slot_ref[2, image], 1)
            slots_ref[owner, 2] = slots_ref[owner, 2] + tile.astype(jnp.bfloat16)


def resident_kernel(length_ref, query_ref, cache_ref, out_ref, top_ref, sum_ref):
    step = pl.program_id(0)
    rows, context = cache_ref.shape[:2]
    place = lax.broadcasted_iota(jnp.int32, (QH, context), 1)
    lane = lax.broadcasted_iota(jnp.int32, (QH, HD), 1)

    @pl.when(step == 0)
    def _():
        top_ref[...] = jnp.zeros_like(top_ref)
        sum_ref[...] = jnp.zeros_like(sum_ref)

    parts = [slice(head * GROUP, (head + 1) * GROUP) for head in range(KVH)]
    scores = [
        jnp.concatenate(
            [
                lax.dot_general(
                    query_ref[row, part, :],
                    cache_ref[row, :, head * HD : (head + 1) * HD],
                    (((1,), (1,)), ((), ())),
                    preferred_element_type=jnp.float32,
                )
                for head, part in enumerate(parts)
            ],
            axis=0,
        )
        for row in range(rows)
    ]
    for row in range(rows):
        live = place < length_ref[step * rows + row]
        score = jnp.where(live, scores[row] * SCALE, masked_score)
        top = jnp.max(score, axis=1, keepdims=True)
        weights = jnp.where(live, jnp.exp(score - top), 0.0)
        mine = lane == step * rows + row
        top_ref[...] = jnp.where(mine, top, top_ref[...])
        sum_ref[...] = jnp.where(mine, jnp.sum(weights, axis=1, keepdims=True), sum_ref[...])
        weights = weights.astype(jnp.bfloat16)
        for head, part in enumerate(parts):
            at = (KVH + head) * HD
            out_ref[row, part, :] = jnp.dot(
                weights[part], cache_ref[row, :, at : at + HD], preferred_element_type=jnp.float32
            )


def combine_kernel(got_ref, res_out_ref, res_top_ref, res_sum_ref, out_ref, acc):
    chips = got_ref.shape[0] // 2
    rows = res_out_ref.shape[0]
    lane = lax.broadcasted_iota(jnp.int32, (HALF_QH, HD), 1)
    head_lane = (lane % LANES) < 8

    def moved(tile, by):
        return pltpu.roll(tile, HD - by, 1)

    for core in range(2):
        part = slice(core * HALF_QH, (core + 1) * HALF_QH)
        tops, sums, here = [], [], []
        for chip in range(chips):
            tile = got_ref[chip * 2 + core, 2].astype(jnp.float32)
            present = (moved(tile, 48) > 0.5) & head_lane
            tops.append(jnp.where(present, tile + moved(tile, 8) + moved(tile, 16), masked_score))
            sums.append(moved(tile, 24) + moved(tile, 32) + moved(tile, 40))
            here.append(present)
        row_top = functools.reduce(jnp.maximum, tops)
        row_top = jnp.maximum(row_top, pltpu.roll(row_top, LANES, 1))
        res_top = jnp.where(lane < 8, res_top_ref[part, :], masked_score)
        res_top = jnp.maximum(res_top, pltpu.roll(res_top, LANES, 1))
        row_top = jnp.maximum(row_top, res_top)
        weights = [jnp.where(a, jnp.exp(t - row_top), 0.0) for a, t in zip(here, tops)]
        joined = sum(w * s for w, s in zip(weights, sums))
        res_weight = jnp.exp(res_top - row_top)
        denominator = joined + pltpu.roll(joined, LANES, 1) + res_weight * res_sum_ref[part, :]
        scale = jnp.where(lane < 8, 1.0 / denominator, 0.0)
        scale = scale + pltpu.roll(scale, LANES, 1)
        res_share = res_weight * scale
        weights = [w * scale for w in weights]
        for row in range(rows):
            value = res_out_ref[row, part, :] * res_share[:, row : row + 1]
            for chip in range(chips):
                for which in range(2):
                    at = which * LANES + row
                    value += weights[chip][:, at : at + 1] * got_ref[chip * 2 + core, which].astype(jnp.float32)
            acc[row, part, :] = value
    for head in range(QH):
        out_ref[:, head * HD : (head + 1) * HD] = acc[:, head, :].astype(jnp.bfloat16)


def whole(shape):
    return pl.BlockSpec(shape, lambda i, *_: (0,) * len(shape))


def per_device(prompt_states, kv_weight, image_owner, image_row, queries, cache, context_length):
    n = lax.axis_size("section")
    section = lax.axis_index("section")
    core = section % 2
    tokens, width = prompt_states.shape
    rows_dev, kv_width = kv_weight.shape
    columns_dev = kv_width // 2
    images = image_owner.shape[0]
    decode_rows = queries.shape[0]
    context = cache.shape[1]
    n_queries = 2 * images * GROUP

    cut = columns_dev // 2
    keep, give = pl.pallas_call(
        split_kernel,
        grid_spec=pltpu.PrefetchScalarGridSpec(
            num_scalar_prefetch=1,
            grid=(2,),
            in_specs=[
                pl.BlockSpec((rows_dev, cut), lambda i, core_ref: (0, 2 * i + core_ref[0])),
                pl.BlockSpec((rows_dev, cut), lambda i, core_ref: (0, 2 * i + 1 - core_ref[0])),
            ],
            out_specs=[pl.BlockSpec((rows_dev, cut), lambda i, core_ref: (0, i))] * 2,
        ),
        out_shape=[jax.ShapeDtypeStruct((rows_dev, columns_dev), jnp.bfloat16)] * 2,
        cost_estimate=pl.CostEstimate(flops=0, bytes_accessed=2**18, transcendentals=0),
        name="split",
    )(core.reshape(1), kv_weight, kv_weight)
    taken = swap_core(give)
    states, _ = lax.optimization_barrier((prompt_states, taken))
    squares = pl.pallas_call(
        square_kernel,
        grid=(8,),
        in_specs=[pl.BlockSpec((tokens // 8, width), lambda i: (i, 0))],
        out_specs=pl.BlockSpec((tokens // 8, 1), lambda i: (i, 0)),
        out_shape=jax.ShapeDtypeStruct((tokens, 1), jnp.float32),
        cost_estimate=pl.CostEstimate(flops=0, bytes_accessed=2**18, transcendentals=0),
        compiler_params=pltpu.CompilerParams(vmem_limit_bytes=32 * 2**20),
        name="squares",
    )(pltpu.with_memory_space_constraint(states, pltpu.HBM))[:, 0]
    other = swap_core(states)

    places = jnp.concatenate([image_owner, image_row]).astype(jnp.float32)
    small = jnp.concatenate([squares, places])
    small = jnp.pad(small, (0, -small.shape[0] % (8 * HD))).reshape(-1, HD)

    def finish_small(tied):
        mine, _ = lax.optimization_barrier((small, tied))
        got = swap_core(mine).reshape(-1)
        factor = jnp.concatenate([squares, got[:tokens]])[:, None]
        at = tokens + images
        owners = jnp.concatenate([image_owner, got[tokens:at].astype(jnp.int32)])
        rows = jnp.concatenate([image_row, got[at : at + images].astype(jnp.int32)])
        return factor, owners, rows

    def gather_queries(tied):
        mine, _ = lax.optimization_barrier((queries, tied))
        send_q = mine.reshape(decode_rows, 2, HALF_QH * HD).transpose(1, 0, 2)
        send_q = jnp.broadcast_to(send_q[None], (n // 2, 2, decode_rows, HALF_QH * HD)).reshape(
            n, decode_rows, HALF_QH * HD
        )
        all_q = lax.all_to_all(send_q, "section", split_axis=0, concat_axis=0, tiled=True)
        return all_q.reshape(n * decode_rows, HALF_QH * HD)

    def place_images(all_q, owners, rows):
        target = owners * decode_rows + rows
        pick = (target[:, None] == jnp.arange(n * decode_rows)[None, :]).astype(jnp.bfloat16)
        image_q = jnp.dot(pick, all_q, preferred_element_type=jnp.float32).astype(jnp.bfloat16)
        image_q = image_q.reshape(2 * images, HALF_KVH, GROUP, HD).transpose(1, 0, 2, 3)
        which = jnp.concatenate([jnp.full((images,), core), jnp.full((images,), 1 - core)]).astype(jnp.int32)
        return image_q.reshape(HALF_KVH, n_queries, HD), jnp.stack([owners, which, rows])

    def resident(length):
        step_rows = 2
        return pl.pallas_call(
            resident_kernel,
            grid_spec=pltpu.PrefetchScalarGridSpec(
                num_scalar_prefetch=1,
                grid=(decode_rows // step_rows,),
                in_specs=[
                    pl.BlockSpec((step_rows, QH, HD), lambda i, *_: (i, 0, 0)),
                    pl.BlockSpec((step_rows, context, kv_width), lambda i, *_: (i, 0, 0)),
                ],
                out_specs=[
                    pl.BlockSpec((step_rows, QH, HD), lambda i, *_: (i, 0, 0)),
                    whole((QH, HD)),
                    whole((QH, HD)),
                ],
            ),
            out_shape=[
                jax.ShapeDtypeStruct((decode_rows, QH, HD), jnp.float32),
                jax.ShapeDtypeStruct((QH, HD), jnp.float32),
                jax.ShapeDtypeStruct((QH, HD), jnp.float32),
            ],
            compiler_params=pltpu.CompilerParams(vmem_limit_bytes=56 * 2**20),
            cost_estimate=pl.CostEstimate(flops=0, bytes_accessed=2**18, transcendentals=0),
            name="resident",
        )(length, queries.reshape(decode_rows, QH, HD), cache)

    def product(blocks, base, pieces, carry, name, last=None):
        arrays, layout = [], []
        for array, start in pieces:
            at = [i for i, known in enumerate(arrays) if known is array]
            if not at:
                arrays.append(array)
                at = [len(arrays) - 1]
            layout.append((at[0], start))
        steps = len(pieces) // 2
        first = pl.BlockSpec((tokens, rows_dev), lambda i, half, block_ref, *_: (0, block_ref[base + 2 * i]))
        second = pl.BlockSpec((tokens, rows_dev), lambda i, half, block_ref, *_: (0, block_ref[base + 2 * i + 1]))
        anywhere = pl.BlockSpec(memory_space=pl.ANY)
        in_specs = [first, second, first, second]
        own_tokens = pltpu.with_memory_space_constraint(prompt_states, pltpu.HBM)
        other_tokens = pltpu.with_memory_space_constraint(other, pltpu.HBM)
        inputs = [own_tokens, own_tokens, other_tokens, other_tokens]
        scalars = [blocks]
        scratch = [pltpu.VMEM((len(pieces) * rows_dev, columns_dev), jnp.bfloat16)]
        total = (2 * tokens, columns_dev)
        body = functools.partial(first_kernel, layout)
        if carry is not None:
            body = functools.partial(next_kernel, layout)
            in_specs = in_specs + [anywhere]
            inputs = inputs + [carry]
            scratch = scratch + [pltpu.VMEM(total, jnp.float32)]
        out_specs, out_shape = whole(total), jax.ShapeDtypeStruct(total, jnp.float32)
        if last is not None:
            image_q, slot, factor = last
            body = functools.partial(last_kernel, layout, width)
            scalars = scalars + [slot]
            in_specs = in_specs + [whole((HALF_KVH, n_queries, HD)), whole((2 * tokens, 1))]
            inputs = inputs + [image_q, factor]
            out_specs = whole((n, 3, HALF_QH, HD))
            out_shape = jax.ShapeDtypeStruct((n, 3, HALF_QH, HD), jnp.bfloat16)
            scratch = scratch + [
                pltpu.VMEM(total, jnp.float32),
                pltpu.VMEM((2 * images, HALF_QH, HD), jnp.float32),
                pltpu.VMEM((2 * images, HALF_QH, HD), jnp.float32),
            ]
        return pl.pallas_call(
            body,
            grid_spec=pltpu.PrefetchScalarGridSpec(
                num_scalar_prefetch=len(scalars),
                grid=(steps, 2),
                in_specs=in_specs + [anywhere] * len(arrays),
                out_specs=out_specs,
                scratch_shapes=scratch + [pltpu.SemaphoreType.DMA((len(pieces) + 1,))],
            ),
            out_shape=out_shape,
            compiler_params=pltpu.CompilerParams(vmem_limit_bytes=32 * 2**20),
            cost_estimate=pl.CostEstimate(flops=0, bytes_accessed=2**18, transcendentals=0),
            name=name,
        )(*scalars, *inputs, *arrays)

    if n == 16 and lax.axis_size("replica") == 2:
        blocks = jnp.array(block_table())[lax.axis_index("replica") * 16 + section]

        def starts(*arrays):
            return [(array, 0) for array in arrays]

        a1 = (along_ring(keep), across_y(keep))
        b1 = (along_ring(taken), across_y(taken))
        a2 = (across_replica(a1[0]), along_ring(a1[0]), across_y(a1[0]))
        all_q = gather_queries(a1[0])
        length, _ = lax.optimization_barrier((context_length, squares))
        res_out, res_top, res_sum = resident(length)
        b_behind, res_out = lax.optimization_barrier((b1[0], res_out))
        b2 = (across_replica(b_behind), along_ring(b_behind), across_y(b_behind))
        factor, owners, rows = finish_small(b1[0])
        total = product(blocks, 0, starts(*a1, *b1), None, "rows_1")
        a_behind_y, a_opposite, total = lax.optimization_barrier((a2[2], a2[1], total))
        a3 = (across_replica(a_behind_y), across_y(a_opposite))
        image_q, slot = place_images(all_q, owners, rows)
        b3 = (across_replica(b2[2]), along_ring(b2[2]))
        total = product(blocks, 4, starts(keep, *a2), total, "rows_2a")
        total = product(blocks, 8, starts(taken, *b2), total, "rows_2b")
        slots = product(blocks, 12, starts(*a3, *b3), total, "rows_3", last=(image_q, slot, factor))
    else:
        res_out, res_top, res_sum = resident(context_length)
        factor, owners, rows = finish_small(squares)
        image_q, slot = place_images(gather_queries(squares), owners, rows)
        a = gather_plain(keep)
        b = gather_plain(taken)
        chips = jnp.array([chip for chip, _, _ in a], jnp.int32)
        total = product(chips * 2 + core, 0, [piece[1:] for piece in a], None, "rows_a")
        slots = product(
            chips * 2 + 1 - core, 0, [piece[1:] for piece in b], total, "rows_b", last=(image_q, slot, factor)
        )
    got = lax.all_to_all(slots, "section", split_axis=0, concat_axis=0, tiled=True)

    return pl.pallas_call(
        combine_kernel,
        grid=(1,),
        in_specs=[
            whole((n, 3, HALF_QH, HD)),
            whole((decode_rows, QH, HD)),
            whole((QH, HD)),
            whole((QH, HD)),
        ],
        out_specs=whole((decode_rows, QH * HD)),
        scratch_shapes=[pltpu.VMEM((decode_rows, QH, HD), jnp.float32)],
        out_shape=jax.ShapeDtypeStruct((decode_rows, QH * HD), jnp.bfloat16),
        compiler_params=pltpu.CompilerParams(vmem_limit_bytes=32 * 2**20),
        name="combine",
    )(got, res_out, res_top, res_sum)


def solution(mesh):
    placed = (
        P(("replica", "section"), None),
        P("section", None),
        P(("replica", "section")),
        P(("replica", "section")),
        P(("replica", "section"), None),
        P(("replica", "section"), None, None),
        P(("replica", "section")),
    )
    return jax.shard_map(
        per_device,
        mesh=mesh,
        in_specs=placed,
        out_specs=P(("replica", "section"), None),
        check_vma=False,
    )
```

```python
import functools
import math

import jax
import jax.numpy as jnp
import numpy as np
from jax import lax
from jax.experimental import pallas as pl
from jax.experimental.pallas import tpu as pltpu
from jax.sharding import PartitionSpec as P

HD = 128
KVH = 4
QH = 32
IMG_TOK = 64
GROUP = QH // KVH
HALF_KVH = KVH // 2
HALF_QH = QH // 2
SCALE = 1.0 / math.sqrt(HD)
EPS = 1e-05

LANES = 64
N_KINDS = 7

masked_score = -1e30


def swap_core(x):
    n = lax.axis_size("section")
    return lax.ppermute(x, "section", [(i, i ^ 1) for i in range(n)])


def gather_plain(chunk):
    n = lax.axis_size("section")
    rows = chunk.shape[0]
    groups = [list(range(core, n, 2)) for core in range(2)]
    whole = lax.all_gather(chunk, "section", axis=0, tiled=True, axis_index_groups=groups)
    return [(chip, whole, chip * rows) for chip in range(n // 2)]


RING = [0, 1, 3, 2]


def along_ring(x):
    perm = []
    for rep, way in ((0, 1), (1, -1)):
        for p in range(4):
            for low in range(4):
                perm.append((rep * 16 + RING[p] * 4 + low, rep * 16 + RING[(p + way) % 4] * 4 + low))
    return lax.ppermute(x, ("replica", "section"), perm)


def across_y(x):
    return lax.ppermute(x, "section", [(i, i ^ 2) for i in range(16)])


def across_replica(x):
    return lax.ppermute(x, "replica", [(0, 1), (1, 0)])


STEPS = (("own", "behind", "own_y"), ("ahead", "opposite", "behind_y"), ("ahead_y", "opposite_y"))


def block_table():
    table = []
    for rep in range(2):
        for section in range(16):
            z, y, core = section // 4, section // 2 % 2, section % 2
            way = 1 - 2 * rep
            place = RING.index(z)
            ring = {"own": place, "behind": place - way, "ahead": place + way, "opposite": place + 2}

            def blocks(step, other):
                out = []
                for name in STEPS[step]:
                    chip = RING[ring[name.removesuffix("_y")] % 4] * 2 + (1 - y if name.endswith("_y") else y)
                    out.append(chip * 2 + (core ^ other))
                return out

            one, two, three = (blocks(step, 0) + blocks(step, 1) for step in range(3))
            table.append(one + two + three)
    return np.array(table, np.int32)


def square_kernel(states_ref, out_ref):
    total = None
    for i in range(0, states_ref.shape[1], HD):
        values = states_ref[:, i : i + HD].astype(jnp.float32)
        values = values * values
        total = values if total is None else total + values
    out_ref[...] = jnp.sum(total, axis=1, keepdims=True)


def split_kernel(core_ref, keep_in, give_in, keep_ref, give_ref):
    keep_ref[...] = keep_in[...]
    give_ref[...] = give_in[...]


def accumulate(layout, token_refs, piece_refs, weight, total, sems, carry_ref=None, carry=None):
    pair, half = pl.program_id(0), pl.program_id(1)
    tokens, depth = token_refs[0].shape
    copies = [
        pltpu.make_async_copy(
            piece_refs[which].at[pl.ds(start, depth)], weight.at[pl.ds(i * depth, depth)], sems.at[i]
        )
        for i, (which, start) in enumerate(layout)
    ]
    carried = []
    if carry_ref is not None:
        carried = [pltpu.make_async_copy(carry_ref, carry, sems.at[len(layout)])]

    @pl.when((pair == 0) & (half == 0))
    def _():
        for copy in copies + carried:
            copy.start()

    for i in range(0, len(copies), 2):

        @pl.when((pair == i // 2) & (half == 0))
        def _():
            copies[i].wait()
            copies[i + 1].wait()

    for side in range(2):

        @pl.when(half == side)
        def _():
            states = jnp.concatenate([token_refs[2 * side][...], token_refs[2 * side + 1][...]], axis=1)
            block = weight[pl.ds(pl.multiple_of(pair * 2 * depth, 2 * depth), 2 * depth), :]
            product = jnp.dot(states, block, preferred_element_type=jnp.float32)
            rows = pl.ds(side * tokens, tokens)

            @pl.when(pair == 0)
            def _():
                total[rows, :] = product

            @pl.when(pair > 0)
            def _():
                total[rows, :] += product

    if carry_ref is not None:

        @pl.when((pair == pl.num_programs(0) - 1) & (half == 1))
        def _():
            carried[0].wait()
            total[...] += carry[...]


def first_kernel(layout, block_ref, *refs):
    total, weight, sems = refs[-3:]
    accumulate(layout, refs[:4], refs[4:-3], weight, total, sems)


def next_kernel(layout, block_ref, *refs):
    total, weight, carry, sems = refs[-4:]
    accumulate(layout, refs[:4], refs[5:-4], weight, total, sems, refs[4], carry)


def parts_of(values, count):
    out = []
    for _ in range(count):
        part = values.astype(jnp.bfloat16).astype(jnp.float32)
        out.append(part)
        values = values - part
    return out


def last_kernel(layout, width, block_ref, slot_ref, *refs):
    query_ref, factor_ref = refs[5:7]
    slots_ref, weight, carry, total, summed, stats, sems = refs[-7:]
    images = query_ref.shape[1] // GROUP

    @pl.when((pl.program_id(0) == 0) & (pl.program_id(1) == 0))
    def _():
        slots_ref[...] = jnp.zeros_like(slots_ref)

    accumulate(layout, refs[:4], refs[7:-7], weight, total, sems, refs[4], carry)

    @pl.when((pl.program_id(0) == pl.num_programs(0) - 1) & (pl.program_id(1) == 1))
    def _():
        tokens = total.shape[0]
        queries = query_ref.shape[1]
        factor = lax.rsqrt(factor_ref[...] / width + EPS)
        image_of_query = lax.broadcasted_iota(jnp.int32, (queries, tokens), 0) // GROUP
        image_of_token = lax.broadcasted_iota(jnp.int32, (queries, tokens), 1) // IMG_TOK
        live = image_of_query == image_of_token
        lane = lax.broadcasted_iota(jnp.int32, (queries, HD), 1)
        for head in range(HALF_KVH):
            part = slice(head * GROUP, (head + 1) * GROUP)
            keys = (total[:, head * HD : (head + 1) * HD] * factor).astype(jnp.bfloat16)
            at = (HALF_KVH + head) * HD
            values = (total[:, at : at + HD] * factor).astype(jnp.bfloat16)
            scores = (
                lax.dot_general(
                    query_ref[head], keys, (((1,), (1,)), ((), ())), preferred_element_type=jnp.float32
                )
                * SCALE
            )
            scores = jnp.where(live, scores, masked_score)
            top = jnp.max(scores, axis=1, keepdims=True)
            weights = jnp.where(live, jnp.exp(scores - top), 0.0)
            total_weight = jnp.sum(weights, axis=1, keepdims=True)
            out = jnp.dot(weights.astype(jnp.bfloat16), values, preferred_element_type=jnp.float32)
            summed[:, part, :] = out.reshape(images, GROUP, HD)
            kinds = parts_of(top, 3) + parts_of(total_weight, 3) + [jnp.ones_like(top)]
            tile = jnp.zeros((queries, HD), jnp.float32)
            for kind, column in enumerate(kinds):
                tile = jnp.where(lane == kind * 8, column, tile)
            stats[:, part, :] = tile.reshape(images, GROUP, HD)
        for image in range(images):
            owner, which = slot_ref[0, image], slot_ref[1, image]
            slots_ref[owner, which] = summed[image].astype(jnp.bfloat16)
            tile = pltpu.roll(stats[image], which * LANES + slot_ref[2, image], 1)
            slots_ref[owner, 2] = slots_ref[owner, 2] + tile.astype(jnp.bfloat16)


def resident_kernel(length_ref, query_ref, cache_ref, out_ref, top_ref, sum_ref):
    step = pl.program_id(0)
    rows, context = cache_ref.shape[:2]
    place = lax.broadcasted_iota(jnp.int32, (QH, context), 1)
    lane = lax.broadcasted_iota(jnp.int32, (QH, HD), 1)

    @pl.when(step == 0)
    def _():
        top_ref[...] = jnp.zeros_like(top_ref)
        sum_ref[...] = jnp.zeros_like(sum_ref)

    parts = [slice(head * GROUP, (head + 1) * GROUP) for head in range(KVH)]
    scores = [
        jnp.concatenate(
            [
                lax.dot_general(
                    query_ref[row, part, :],
                    cache_ref[row, :, head * HD : (head + 1) * HD],
                    (((1,), (1,)), ((), ())),
                    preferred_element_type=jnp.float32,
                )
                for head, part in enumerate(parts)
            ],
            axis=0,
        )
        for row in range(rows)
    ]
    for row in range(rows):
        live = place < length_ref[step * rows + row]
        score = jnp.where(live, scores[row] * SCALE, masked_score)
        top = jnp.max(score, axis=1, keepdims=True)
        weights = jnp.where(live, jnp.exp(score - top), 0.0)
        mine = lane == step * rows + row
        top_ref[...] = jnp.where(mine, top, top_ref[...])
        sum_ref[...] = jnp.where(mine, jnp.sum(weights, axis=1, keepdims=True), sum_ref[...])
        weights = weights.astype(jnp.bfloat16)
        for head, part in enumerate(parts):
            at = (KVH + head) * HD
            out_ref[row, part, :] = jnp.dot(
                weights[part], cache_ref[row, :, at : at + HD], preferred_element_type=jnp.float32
            )


def combine_kernel(got_ref, res_out_ref, res_top_ref, res_sum_ref, out_ref, acc):
    chips = got_ref.shape[0] // 2
    rows = res_out_ref.shape[0]
    lane = lax.broadcasted_iota(jnp.int32, (HALF_QH, HD), 1)
    head_lane = (lane % LANES) < 8

    def moved(tile, by):
        return pltpu.roll(tile, HD - by, 1)

    for core in range(2):
        part = slice(core * HALF_QH, (core + 1) * HALF_QH)
        tops, sums, here = [], [], []
        for chip in range(chips):
            tile = got_ref[chip * 2 + core, 2].astype(jnp.float32)
            present = (moved(tile, 48) > 0.5) & head_lane
            tops.append(jnp.where(present, tile + moved(tile, 8) + moved(tile, 16), masked_score))
            sums.append(moved(tile, 24) + moved(tile, 32) + moved(tile, 40))
            here.append(present)
        row_top = functools.reduce(jnp.maximum, tops)
        row_top = jnp.maximum(row_top, pltpu.roll(row_top, LANES, 1))
        res_top = jnp.where(lane < 8, res_top_ref[part, :], masked_score)
        res_top = jnp.maximum(res_top, pltpu.roll(res_top, LANES, 1))
        row_top = jnp.maximum(row_top, res_top)
        weights = [jnp.where(a, jnp.exp(t - row_top), 0.0) for a, t in zip(here, tops)]
        joined = sum(w * s for w, s in zip(weights, sums))
        res_weight = jnp.exp(res_top - row_top)
        denominator = joined + pltpu.roll(joined, LANES, 1) + res_weight * res_sum_ref[part, :]
        scale = jnp.where(lane < 8, 1.0 / denominator, 0.0)
        scale = scale + pltpu.roll(scale, LANES, 1)
        res_share = res_weight * scale
        weights = [w * scale for w in weights]
        for row in range(rows):
            value = res_out_ref[row, part, :] * res_share[:, row : row + 1]
            for chip in range(chips):
                for which in range(2):
                    at = which * LANES + row
                    value += weights[chip][:, at : at + 1] * got_ref[chip * 2 + core, which].astype(jnp.float32)
            acc[row, part, :] = value
    for head in range(QH):
        out_ref[:, head * HD : (head + 1) * HD] = acc[:, head, :].astype(jnp.bfloat16)


def whole(shape):
    return pl.BlockSpec(shape, lambda i, *_: (0,) * len(shape))


def per_device(prompt_states, kv_weight, image_owner, image_row, queries, cache, context_length):
    n = lax.axis_size("section")
    section = lax.axis_index("section")
    core = section % 2
    tokens, width = prompt_states.shape
    rows_dev, kv_width = kv_weight.shape
    columns_dev = kv_width // 2
    images = image_owner.shape[0]
    decode_rows = queries.shape[0]
    context = cache.shape[1]
    n_queries = 2 * images * GROUP

    cut = columns_dev // 2
    keep, give = pl.pallas_call(
        split_kernel,
        grid_spec=pltpu.PrefetchScalarGridSpec(
            num_scalar_prefetch=1,
            grid=(2,),
            in_specs=[
                pl.BlockSpec((rows_dev, cut), lambda i, core_ref: (0, 2 * i + core_ref[0])),
                pl.BlockSpec((rows_dev, cut), lambda i, core_ref: (0, 2 * i + 1 - core_ref[0])),
            ],
            out_specs=[pl.BlockSpec((rows_dev, cut), lambda i, core_ref: (0, i))] * 2,
        ),
        out_shape=[jax.ShapeDtypeStruct((rows_dev, columns_dev), jnp.bfloat16)] * 2,
        cost_estimate=pl.CostEstimate(flops=0, bytes_accessed=2**18, transcendentals=0),
        name="split",
    )(core.reshape(1), kv_weight, kv_weight)
    taken = swap_core(give)
    swapped_states, _ = lax.optimization_barrier((prompt_states, keep))
    other = swap_core(swapped_states)

    def square_sums(tied):
        states, _ = lax.optimization_barrier((prompt_states, tied))
        return pl.pallas_call(
            square_kernel,
            grid=(8,),
            in_specs=[pl.BlockSpec((tokens // 8, width), lambda i: (i, 0))],
            out_specs=pl.BlockSpec((tokens // 8, 1), lambda i: (i, 0)),
            out_shape=jax.ShapeDtypeStruct((tokens, 1), jnp.float32),
            cost_estimate=pl.CostEstimate(flops=0, bytes_accessed=2**18, transcendentals=0),
            compiler_params=pltpu.CompilerParams(vmem_limit_bytes=32 * 2**20),
            name="squares",
        )(pltpu.with_memory_space_constraint(states, pltpu.HBM))[:, 0]

    def swap_small(squares):
        places = jnp.concatenate([image_owner, image_row]).astype(jnp.float32)
        small = jnp.concatenate([squares, places])
        small = jnp.pad(small, (0, -small.shape[0] % (8 * HD))).reshape(-1, HD)
        got = swap_core(small).reshape(-1)
        factor = jnp.concatenate([squares, got[:tokens]])[:, None]
        at = tokens + images
        owners = jnp.concatenate([image_owner, got[tokens:at].astype(jnp.int32)])
        rows = jnp.concatenate([image_row, got[at : at + images].astype(jnp.int32)])
        return factor, owners, rows

    def gather_queries(tied):
        mine, _ = lax.optimization_barrier((queries, tied))
        send_q = mine.reshape(decode_rows, 2, HALF_QH * HD).transpose(1, 0, 2)
        send_q = jnp.broadcast_to(send_q[None], (n // 2, 2, decode_rows, HALF_QH * HD)).reshape(
            n, decode_rows, HALF_QH * HD
        )
        all_q = lax.all_to_all(send_q, "section", split_axis=0, concat_axis=0, tiled=True)
        return all_q.reshape(n * decode_rows, HALF_QH * HD)

    def place_images(all_q, owners, rows):
        target = owners * decode_rows + rows
        pick = (target[:, None] == jnp.arange(n * decode_rows)[None, :]).astype(jnp.bfloat16)
        image_q = jnp.dot(pick, all_q, preferred_element_type=jnp.float32).astype(jnp.bfloat16)
        image_q = image_q.reshape(2 * images, HALF_KVH, GROUP, HD).transpose(1, 0, 2, 3)
        which = jnp.concatenate([jnp.full((images,), core), jnp.full((images,), 1 - core)]).astype(jnp.int32)
        return image_q.reshape(HALF_KVH, n_queries, HD), jnp.stack([owners, which, rows])

    def resident(length):
        step_rows = 2
        return pl.pallas_call(
            resident_kernel,
            grid_spec=pltpu.PrefetchScalarGridSpec(
                num_scalar_prefetch=1,
                grid=(decode_rows // step_rows,),
                in_specs=[
                    pl.BlockSpec((step_rows, QH, HD), lambda i, *_: (i, 0, 0)),
                    pl.BlockSpec((step_rows, context, kv_width), lambda i, *_: (i, 0, 0)),
                ],
                out_specs=[
                    pl.BlockSpec((step_rows, QH, HD), lambda i, *_: (i, 0, 0)),
                    whole((QH, HD)),
                    whole((QH, HD)),
                ],
            ),
            out_shape=[
                jax.ShapeDtypeStruct((decode_rows, QH, HD), jnp.float32),
                jax.ShapeDtypeStruct((QH, HD), jnp.float32),
                jax.ShapeDtypeStruct((QH, HD), jnp.float32),
            ],
            compiler_params=pltpu.CompilerParams(vmem_limit_bytes=56 * 2**20),
            cost_estimate=pl.CostEstimate(flops=0, bytes_accessed=2**18, transcendentals=0),
            name="resident",
        )(length, queries.reshape(decode_rows, QH, HD), cache)

    def product(blocks, base, pieces, carry, name, last=None):
        arrays, layout = [], []
        for array, start in pieces:
            at = [i for i, known in enumerate(arrays) if known is array]
            if not at:
                arrays.append(array)
                at = [len(arrays) - 1]
            layout.append((at[0], start))
        steps = len(pieces) // 2
        first = pl.BlockSpec((tokens, rows_dev), lambda i, half, block_ref, *_: (0, block_ref[base + 2 * i]))
        second = pl.BlockSpec((tokens, rows_dev), lambda i, half, block_ref, *_: (0, block_ref[base + 2 * i + 1]))
        anywhere = pl.BlockSpec(memory_space=pl.ANY)
        in_specs = [first, second, first, second]
        own_tokens = pltpu.with_memory_space_constraint(prompt_states, pltpu.HBM)
        other_tokens = pltpu.with_memory_space_constraint(other, pltpu.HBM)
        inputs = [own_tokens, own_tokens, other_tokens, other_tokens]
        scalars = [blocks]
        scratch = [pltpu.VMEM((len(pieces) * rows_dev, columns_dev), jnp.bfloat16)]
        total = (2 * tokens, columns_dev)
        body = functools.partial(first_kernel, layout)
        if carry is not None:
            body = functools.partial(next_kernel, layout)
            in_specs = in_specs + [anywhere]
            inputs = inputs + [carry]
            scratch = scratch + [pltpu.VMEM(total, jnp.float32)]
        out_specs, out_shape = whole(total), jax.ShapeDtypeStruct(total, jnp.float32)
        if last is not None:
            image_q, slot, factor = last
            body = functools.partial(last_kernel, layout, width)
            scalars = scalars + [slot]
            in_specs = in_specs + [whole((HALF_KVH, n_queries, HD)), whole((2 * tokens, 1))]
            inputs = inputs + [image_q, factor]
            out_specs = whole((n, 3, HALF_QH, HD))
            out_shape = jax.ShapeDtypeStruct((n, 3, HALF_QH, HD), jnp.bfloat16)
            scratch = scratch + [
                pltpu.VMEM(total, jnp.float32),
                pltpu.VMEM((2 * images, HALF_QH, HD), jnp.float32),
                pltpu.VMEM((2 * images, HALF_QH, HD), jnp.float32),
            ]
        return pl.pallas_call(
            body,
            grid_spec=pltpu.PrefetchScalarGridSpec(
                num_scalar_prefetch=len(scalars),
                grid=(steps, 2),
                in_specs=in_specs + [anywhere] * len(arrays),
                out_specs=out_specs,
                scratch_shapes=scratch + [pltpu.SemaphoreType.DMA((len(pieces) + 1,))],
            ),
            out_shape=out_shape,
            compiler_params=pltpu.CompilerParams(vmem_limit_bytes=32 * 2**20),
            cost_estimate=pl.CostEstimate(flops=0, bytes_accessed=2**18, transcendentals=0),
            name=name,
        )(*scalars, *inputs, *arrays)

    if n == 16 and lax.axis_size("replica") == 2:
        blocks = jnp.array(block_table())[lax.axis_index("replica") * 16 + section]

        def starts(*arrays):
            return [(array, 0) for array in arrays]

        tie = lax.optimization_barrier
        a_behind, a_own_y = along_ring(keep), across_y(keep)

        from_a, from_b, done = tie((a_behind, taken, a_own_y))
        b_behind, b_own_y, a_ahead = along_ring(from_b), across_y(from_b), across_replica(from_a)
        squares = square_sums(done)
        all_q = gather_queries(squares)

        from_a, from_b, squares, _ = tie((a_behind, b_behind, squares, (b_own_y, a_ahead, other)))
        a_opposite, a_behind_y, b_ahead = along_ring(from_a), across_y(from_a), across_replica(from_b)
        factor, owners, rows = swap_small(squares)
        total = product(blocks, 0, starts(keep, a_behind, a_own_y, taken, b_behind, b_own_y), None, "rows_1")

        from_a, from_b, total, done = tie((a_behind_y, b_behind, total, (a_opposite, b_ahead)))
        b_opposite, b_behind_y, a_ahead_y = along_ring(from_b), across_y(from_b), across_replica(from_a)
        all_q, owners, rows, _ = tie((all_q, owners, rows, done))
        image_q, slot = place_images(all_q, owners, rows)

        from_a, from_b, image_q, slot, _ = tie((a_opposite, b_behind_y, image_q, slot, (b_opposite, a_ahead_y)))
        a_opposite_y, b_ahead_y, b_opposite_y = across_y(from_a), across_replica(from_b), along_ring(from_b)
        twos = starts(a_ahead, a_opposite, a_behind_y, b_ahead, b_opposite, b_behind_y)
        total = product(blocks, 6, twos, total, "rows_2")
        threes = starts(a_ahead_y, a_opposite_y, b_ahead_y, b_opposite_y)
        slots = product(blocks, 12, threes, total, "rows_3", last=(image_q, slot, factor))
        length, slots = tie((context_length, slots))
        res_out, res_top, res_sum = resident(length)
    else:
        res_out, res_top, res_sum = resident(context_length)
        squares = square_sums(taken)
        factor, owners, rows = swap_small(squares)
        image_q, slot = place_images(gather_queries(squares), owners, rows)
        a = gather_plain(keep)
        b = gather_plain(taken)
        chips = jnp.array([chip for chip, _, _ in a], jnp.int32)
        total = product(chips * 2 + core, 0, [piece[1:] for piece in a], None, "rows_a")
        slots = product(
            chips * 2 + 1 - core, 0, [piece[1:] for piece in b], total, "rows_b", last=(image_q, slot, factor)
        )
    got = lax.all_to_all(slots, "section", split_axis=0, concat_axis=0, tiled=True)

    return pl.pallas_call(
        combine_kernel,
        grid=(1,),
        in_specs=[
            whole((n, 3, HALF_QH, HD)),
            whole((decode_rows, QH, HD)),
            whole((QH, HD)),
            whole((QH, HD)),
        ],
        out_specs=whole((decode_rows, QH * HD)),
        scratch_shapes=[pltpu.VMEM((decode_rows, QH, HD), jnp.float32)],
        out_shape=jax.ShapeDtypeStruct((decode_rows, QH * HD), jnp.bfloat16),
        compiler_params=pltpu.CompilerParams(vmem_limit_bytes=32 * 2**20),
        name="combine",
    )(got, res_out, res_top, res_sum)


def solution(mesh):
    placed = (
        P(("replica", "section"), None),
        P("section", None),
        P(("replica", "section")),
        P(("replica", "section")),
        P(("replica", "section"), None),
        P(("replica", "section"), None, None),
        P(("replica", "section")),
    )
    return jax.shard_map(
        per_device,
        mesh=mesh,
        in_specs=placed,
        out_specs=P(("replica", "section"), None),
        check_vma=False,
    )
```

```python
import functools
import math

import jax
import jax.numpy as jnp
import numpy as np
from jax import lax
from jax.experimental import pallas as pl
from jax.experimental.pallas import tpu as pltpu
from jax.sharding import PartitionSpec as P

HD = 128
KVH = 4
QH = 32
IMG_TOK = 64
GROUP = QH // KVH
HALF_KVH = KVH // 2
HALF_QH = QH // 2
SCALE = 1.0 / math.sqrt(HD)
EPS = 1e-05

LANES = 64
N_KINDS = 7

masked_score = -1e30


def swap_core(x):
    n = lax.axis_size("section")
    return lax.ppermute(x, "section", [(i, i ^ 1) for i in range(n)])


def gather_plain(chunk):
    n = lax.axis_size("section")
    rows = chunk.shape[0]
    groups = [list(range(core, n, 2)) for core in range(2)]
    whole = lax.all_gather(chunk, "section", axis=0, tiled=True, axis_index_groups=groups)
    return [(chip, whole, chip * rows) for chip in range(n // 2)]


RING = [0, 1, 3, 2]


def along_ring(x):
    perm = []
    for rep, way in ((0, 1), (1, -1)):
        for p in range(4):
            for low in range(4):
                perm.append((rep * 16 + RING[p] * 4 + low, rep * 16 + RING[(p + way) % 4] * 4 + low))
    return lax.ppermute(x, ("replica", "section"), perm)


def across_y(x):
    return lax.ppermute(x, "section", [(i, i ^ 2) for i in range(16)])


def across_replica(x):
    return lax.ppermute(x, "replica", [(0, 1), (1, 0)])


STEPS = (("own", "behind", "own_y"), ("ahead", "opposite", "behind_y"), ("ahead_y", "opposite_y"))


def block_table():
    table = []
    for rep in range(2):
        for section in range(16):
            z, y, core = section // 4, section // 2 % 2, section % 2
            way = 1 - 2 * rep
            place = RING.index(z)
            ring = {"own": place, "behind": place - way, "ahead": place + way, "opposite": place + 2}

            def blocks(step, other):
                out = []
                for name in STEPS[step]:
                    chip = RING[ring[name.removesuffix("_y")] % 4] * 2 + (1 - y if name.endswith("_y") else y)
                    out.append(chip * 2 + (core ^ other))
                return out

            one = blocks(0, 0) + blocks(0, 1)
            two_a, two_b, three_a, three_b = blocks(1, 0), blocks(1, 1), blocks(2, 0), blocks(2, 1)
            table.append(one + two_a + two_b + three_a + three_b)
    return np.array(table, np.int32)


def square_kernel(states_ref, out_ref):
    total = None
    for i in range(0, states_ref.shape[1], HD):
        values = states_ref[:, i : i + HD].astype(jnp.float32)
        values = values * values
        total = values if total is None else total + values
    out_ref[...] = jnp.sum(total, axis=1, keepdims=True)


def split_kernel(core_ref, keep_in, give_in, keep_ref, give_ref):
    keep_ref[...] = keep_in[...]
    give_ref[...] = give_in[...]


def accumulate(layout, token_refs, piece_refs, weight, total, sems, carry_ref=None, carry=None):
    step, half = pl.program_id(0), pl.program_id(1)
    tokens, rows = token_refs[0].shape
    count = len(token_refs) // 2
    depth = count * rows
    copies = [
        pltpu.make_async_copy(
            piece_refs[which].at[pl.ds(start, rows)], weight.at[pl.ds(i * rows, rows)], sems.at[i]
        )
        for i, (which, start) in enumerate(layout)
    ]

    @pl.when((step == 0) & (half == 0))
    def _():
        for copy in copies:
            copy.start()

    for i in range(0, len(copies), count):

        @pl.when((step == i // count) & (half == 0))
        def _():
            for copy in copies[i : i + count]:
                copy.wait()

    if carry_ref is not None:
        carried = pltpu.make_async_copy(carry_ref, carry, sems.at[len(layout)])

        @pl.when((step == 0) & (half == 0))
        def _():
            carried.start()

    for side in range(2):

        @pl.when(half == side)
        def _():
            states = jnp.concatenate([ref[...] for ref in token_refs[side * count : (side + 1) * count]], axis=1)
            block = weight[pl.ds(pl.multiple_of(step * depth, depth), depth), :]
            product = jnp.dot(states, block, preferred_element_type=jnp.float32)
            rows_of_side = pl.ds(side * tokens, tokens)

            @pl.when(step == 0)
            def _():
                total[rows_of_side, :] = product

            @pl.when(step > 0)
            def _():
                total[rows_of_side, :] += product

    if carry_ref is not None:

        @pl.when((step == pl.num_programs(0) - 1) & (half == 1))
        def _():
            carried.wait()
            total[...] += carry[...]


def first_kernel(layout, count, block_ref, *refs):
    total, weight, sems = refs[-3:]
    accumulate(layout, refs[: 2 * count], refs[2 * count : -3], weight, total, sems)


def next_kernel(layout, count, block_ref, *refs):
    total, weight, carry, sems = refs[-4:]
    token_refs, (carry_ref, *piece_refs) = refs[: 2 * count], refs[2 * count : -4]
    accumulate(layout, token_refs, piece_refs, weight, total, sems, carry_ref, carry)


def parts_of(values, count):
    out = []
    for _ in range(count):
        part = values.astype(jnp.bfloat16).astype(jnp.float32)
        out.append(part)
        values = values - part
    return out


def last_kernel(layout, count, width, block_ref, slot_ref, *refs):
    token_refs, (carry_ref, query_ref, factor_ref, *piece_refs) = refs[: 2 * count], refs[2 * count : -7]
    slots_ref, weight, carry, total, summed, stats, sems = refs[-7:]
    images = query_ref.shape[1] // GROUP

    @pl.when((pl.program_id(0) == 0) & (pl.program_id(1) == 0))
    def _():
        slots_ref[...] = jnp.zeros_like(slots_ref)

    accumulate(layout, token_refs, piece_refs, weight, total, sems, carry_ref, carry)

    @pl.when((pl.program_id(0) == pl.num_programs(0) - 1) & (pl.program_id(1) == 1))
    def _():
        tokens = total.shape[0]
        queries = query_ref.shape[1]
        factor = lax.rsqrt(factor_ref[...] / width + EPS)
        image_of_query = lax.broadcasted_iota(jnp.int32, (queries, tokens), 0) // GROUP
        image_of_token = lax.broadcasted_iota(jnp.int32, (queries, tokens), 1) // IMG_TOK
        live = image_of_query == image_of_token
        lane = lax.broadcasted_iota(jnp.int32, (queries, HD), 1)
        for head in range(HALF_KVH):
            part = slice(head * GROUP, (head + 1) * GROUP)
            keys = (total[:, head * HD : (head + 1) * HD] * factor).astype(jnp.bfloat16)
            at = (HALF_KVH + head) * HD
            values = (total[:, at : at + HD] * factor).astype(jnp.bfloat16)
            scores = (
                lax.dot_general(
                    query_ref[head], keys, (((1,), (1,)), ((), ())), preferred_element_type=jnp.float32
                )
                * SCALE
            )
            scores = jnp.where(live, scores, masked_score)
            top = jnp.max(scores, axis=1, keepdims=True)
            weights = jnp.where(live, jnp.exp(scores - top), 0.0)
            total_weight = jnp.sum(weights, axis=1, keepdims=True)
            out = jnp.dot(weights.astype(jnp.bfloat16), values, preferred_element_type=jnp.float32)
            summed[:, part, :] = out.reshape(images, GROUP, HD)
            kinds = parts_of(top, 3) + parts_of(total_weight, 3) + [jnp.ones_like(top)]
            tile = jnp.zeros((queries, HD), jnp.float32)
            for kind, column in enumerate(kinds):
                tile = jnp.where(lane == kind * 8, column, tile)
            stats[:, part, :] = tile.reshape(images, GROUP, HD)
        for image in range(images):
            owner, which = slot_ref[0, image], slot_ref[1, image]
            slots_ref[owner, which] = summed[image].astype(jnp.bfloat16)
            tile = pltpu.roll(stats[image], which * LANES + slot_ref[2, image], 1)
            slots_ref[owner, 2] = slots_ref[owner, 2] + tile.astype(jnp.bfloat16)


def resident_kernel(length_ref, query_ref, cache_ref, out_ref, top_ref, sum_ref):
    step = pl.program_id(0)
    rows, context = cache_ref.shape[:2]
    place = lax.broadcasted_iota(jnp.int32, (QH, context), 1)
    lane = lax.broadcasted_iota(jnp.int32, (QH, HD), 1)

    @pl.when(step == 0)
    def _():
        top_ref[...] = jnp.zeros_like(top_ref)
        sum_ref[...] = jnp.zeros_like(sum_ref)

    parts = [slice(head * GROUP, (head + 1) * GROUP) for head in range(KVH)]
    scores = [
        jnp.concatenate(
            [
                lax.dot_general(
                    query_ref[row, part, :],
                    cache_ref[row, :, head * HD : (head + 1) * HD],
                    (((1,), (1,)), ((), ())),
                    preferred_element_type=jnp.float32,
                )
                for head, part in enumerate(parts)
            ],
            axis=0,
        )
        for row in range(rows)
    ]
    for row in range(rows):
        live = place < length_ref[step * rows + row]
        score = jnp.where(live, scores[row] * SCALE, masked_score)
        top = jnp.max(score, axis=1, keepdims=True)
        weights = jnp.where(live, jnp.exp(score - top), 0.0)
        mine = lane == step * rows + row
        top_ref[...] = jnp.where(mine, top, top_ref[...])
        sum_ref[...] = jnp.where(mine, jnp.sum(weights, axis=1, keepdims=True), sum_ref[...])
        weights = weights.astype(jnp.bfloat16)
        for head, part in enumerate(parts):
            at = (KVH + head) * HD
            out_ref[row, part, :] = jnp.dot(
                weights[part], cache_ref[row, :, at : at + HD], preferred_element_type=jnp.float32
            )


def combine_kernel(got_ref, res_out_ref, res_top_ref, res_sum_ref, out_ref, acc):
    chips = got_ref.shape[0] // 2
    rows = res_out_ref.shape[0]
    lane = lax.broadcasted_iota(jnp.int32, (HALF_QH, HD), 1)
    head_lane = (lane % LANES) < 8

    def moved(tile, by):
        return pltpu.roll(tile, HD - by, 1)

    for core in range(2):
        part = slice(core * HALF_QH, (core + 1) * HALF_QH)
        tops, sums, here = [], [], []
        for chip in range(chips):
            tile = got_ref[chip * 2 + core, 2].astype(jnp.float32)
            present = (moved(tile, 48) > 0.5) & head_lane
            tops.append(jnp.where(present, tile + moved(tile, 8) + moved(tile, 16), masked_score))
            sums.append(moved(tile, 24) + moved(tile, 32) + moved(tile, 40))
            here.append(present)
        row_top = functools.reduce(jnp.maximum, tops)
        row_top = jnp.maximum(row_top, pltpu.roll(row_top, LANES, 1))
        res_top = jnp.where(lane < 8, res_top_ref[part, :], masked_score)
        res_top = jnp.maximum(res_top, pltpu.roll(res_top, LANES, 1))
        row_top = jnp.maximum(row_top, res_top)
        weights = [jnp.where(a, jnp.exp(t - row_top), 0.0) for a, t in zip(here, tops)]
        joined = sum(w * s for w, s in zip(weights, sums))
        res_weight = jnp.exp(res_top - row_top)
        denominator = joined + pltpu.roll(joined, LANES, 1) + res_weight * res_sum_ref[part, :]
        scale = jnp.where(lane < 8, 1.0 / denominator, 0.0)
        scale = scale + pltpu.roll(scale, LANES, 1)
        res_share = res_weight * scale
        weights = [w * scale for w in weights]
        for row in range(rows):
            value = res_out_ref[row, part, :] * res_share[:, row : row + 1]
            for chip in range(chips):
                for which in range(2):
                    at = which * LANES + row
                    value += weights[chip][:, at : at + 1] * got_ref[chip * 2 + core, which].astype(jnp.float32)
            acc[row, part, :] = value
    for head in range(QH):
        out_ref[:, head * HD : (head + 1) * HD] = acc[:, head, :].astype(jnp.bfloat16)


def whole(shape):
    return pl.BlockSpec(shape, lambda i, *_: (0,) * len(shape))


def per_device(prompt_states, kv_weight, image_owner, image_row, queries, cache, context_length):
    n = lax.axis_size("section")
    section = lax.axis_index("section")
    core = section % 2
    tokens, width = prompt_states.shape
    rows_dev, kv_width = kv_weight.shape
    columns_dev = kv_width // 2
    images = image_owner.shape[0]
    decode_rows = queries.shape[0]
    context = cache.shape[1]
    n_queries = 2 * images * GROUP

    cut = columns_dev // 2
    keep, give = pl.pallas_call(
        split_kernel,
        grid_spec=pltpu.PrefetchScalarGridSpec(
            num_scalar_prefetch=1,
            grid=(2,),
            in_specs=[
                pl.BlockSpec((rows_dev, cut), lambda i, core_ref: (0, 2 * i + core_ref[0])),
                pl.BlockSpec((rows_dev, cut), lambda i, core_ref: (0, 2 * i + 1 - core_ref[0])),
            ],
            out_specs=[pl.BlockSpec((rows_dev, cut), lambda i, core_ref: (0, i))] * 2,
        ),
        out_shape=[jax.ShapeDtypeStruct((rows_dev, columns_dev), jnp.bfloat16)] * 2,
        cost_estimate=pl.CostEstimate(flops=0, bytes_accessed=2**18, transcendentals=0),
        name="split",
    )(core.reshape(1), kv_weight, kv_weight)
    taken = swap_core(give)
    swapped_states, _ = lax.optimization_barrier((prompt_states, keep))
    other = swap_core(swapped_states)

    def square_sums(tied):
        states, _ = lax.optimization_barrier((prompt_states, tied))
        return pl.pallas_call(
            square_kernel,
            grid=(8,),
            in_specs=[pl.BlockSpec((tokens // 8, width), lambda i: (i, 0))],
            out_specs=pl.BlockSpec((tokens // 8, 1), lambda i: (i, 0)),
            out_shape=jax.ShapeDtypeStruct((tokens, 1), jnp.float32),
            cost_estimate=pl.CostEstimate(flops=0, bytes_accessed=2**18, transcendentals=0),
            compiler_params=pltpu.CompilerParams(vmem_limit_bytes=60 * 2**20),
            name="squares",
        )(pltpu.with_memory_space_constraint(states, pltpu.HBM))[:, 0]

    def swap_small(squares):
        places = jnp.concatenate([image_owner, image_row]).astype(jnp.float32)
        small = jnp.concatenate([squares, places])
        small = jnp.pad(small, (0, -small.shape[0] % (8 * HD))).reshape(-1, HD)
        got = swap_core(small).reshape(-1)
        factor = jnp.concatenate([squares, got[:tokens]])[:, None]
        at = tokens + images
        owners = jnp.concatenate([image_owner, got[tokens:at].astype(jnp.int32)])
        rows = jnp.concatenate([image_row, got[at : at + images].astype(jnp.int32)])
        return factor, owners, rows

    def gather_queries(tied):
        mine, _ = lax.optimization_barrier((queries, tied))
        send_q = mine.reshape(decode_rows, 2, HALF_QH * HD).transpose(1, 0, 2)
        send_q = jnp.broadcast_to(send_q[None], (n // 2, 2, decode_rows, HALF_QH * HD)).reshape(
            n, decode_rows, HALF_QH * HD
        )
        all_q = lax.all_to_all(send_q, "section", split_axis=0, concat_axis=0, tiled=True)
        return all_q.reshape(n * decode_rows, HALF_QH * HD)

    def place_images(all_q, owners, rows):
        target = owners * decode_rows + rows
        pick = (target[:, None] == jnp.arange(n * decode_rows)[None, :]).astype(jnp.bfloat16)
        image_q = jnp.dot(pick, all_q, preferred_element_type=jnp.float32).astype(jnp.bfloat16)
        image_q = image_q.reshape(2 * images, HALF_KVH, GROUP, HD).transpose(1, 0, 2, 3)
        which = jnp.concatenate([jnp.full((images,), core), jnp.full((images,), 1 - core)]).astype(jnp.int32)
        return image_q.reshape(HALF_KVH, n_queries, HD), jnp.stack([owners, which, rows])

    def resident(length):
        step_rows = 2
        return pl.pallas_call(
            resident_kernel,
            grid_spec=pltpu.PrefetchScalarGridSpec(
                num_scalar_prefetch=1,
                grid=(decode_rows // step_rows,),
                in_specs=[
                    pl.BlockSpec((step_rows, QH, HD), lambda i, *_: (i, 0, 0)),
                    pl.BlockSpec((step_rows, context, kv_width), lambda i, *_: (i, 0, 0)),
                ],
                out_specs=[
                    pl.BlockSpec((step_rows, QH, HD), lambda i, *_: (i, 0, 0)),
                    whole((QH, HD)),
                    whole((QH, HD)),
                ],
            ),
            out_shape=[
                jax.ShapeDtypeStruct((decode_rows, QH, HD), jnp.float32),
                jax.ShapeDtypeStruct((QH, HD), jnp.float32),
                jax.ShapeDtypeStruct((QH, HD), jnp.float32),
            ],
            compiler_params=pltpu.CompilerParams(vmem_limit_bytes=60 * 2**20),
            cost_estimate=pl.CostEstimate(flops=0, bytes_accessed=2**18, transcendentals=0),
            name="resident",
        )(length, queries.reshape(decode_rows, QH, HD), cache)

    def product(blocks, base, count, pieces, carry, name, last=None):
        arrays, layout = [], []
        for array, start in pieces:
            at = [i for i, known in enumerate(arrays) if known is array]
            if not at:
                arrays.append(array)
                at = [len(arrays) - 1]
            layout.append((at[0], start))
        steps = len(pieces) // count

        def token_spec(k):
            return pl.BlockSpec((tokens, rows_dev), lambda i, half, block_ref, *_: (0, block_ref[base + count * i + k]))

        anywhere = pl.BlockSpec(memory_space=pl.ANY)
        in_specs = [token_spec(k) for k in range(count)] * 2
        own_tokens = pltpu.with_memory_space_constraint(prompt_states, pltpu.HBM)
        other_tokens = pltpu.with_memory_space_constraint(other, pltpu.HBM)
        inputs = [own_tokens] * count + [other_tokens] * count
        scalars = [blocks]
        scratch = [pltpu.VMEM((len(pieces) * rows_dev, columns_dev), jnp.bfloat16)]
        total = (2 * tokens, columns_dev)
        body = functools.partial(first_kernel, layout, count)
        if carry is not None:
            body = functools.partial(next_kernel, layout, count)
            in_specs = in_specs + [anywhere]
            inputs = inputs + [carry]
            scratch = scratch + [pltpu.VMEM(total, jnp.float32)]
        out_specs, out_shape = whole(total), jax.ShapeDtypeStruct(total, jnp.float32)
        if last is not None:
            image_q, slot, factor = last
            body = functools.partial(last_kernel, layout, count, width)
            scalars = scalars + [slot]
            in_specs = in_specs + [whole((HALF_KVH, n_queries, HD)), whole((2 * tokens, 1))]
            inputs = inputs + [image_q, factor]
            out_specs = whole((n, 3, HALF_QH, HD))
            out_shape = jax.ShapeDtypeStruct((n, 3, HALF_QH, HD), jnp.bfloat16)
            scratch = scratch + [
                pltpu.VMEM(total, jnp.float32),
                pltpu.VMEM((2 * images, HALF_QH, HD), jnp.float32),
                pltpu.VMEM((2 * images, HALF_QH, HD), jnp.float32),
            ]
        return pl.pallas_call(
            body,
            grid_spec=pltpu.PrefetchScalarGridSpec(
                num_scalar_prefetch=len(scalars),
                grid=(steps, 2),
                in_specs=in_specs + [anywhere] * len(arrays),
                out_specs=out_specs,
                scratch_shapes=scratch + [pltpu.SemaphoreType.DMA((len(pieces) + 1,))],
            ),
            out_shape=out_shape,
            compiler_params=pltpu.CompilerParams(vmem_limit_bytes=60 * 2**20),
            cost_estimate=pl.CostEstimate(flops=0, bytes_accessed=2**18, transcendentals=0),
            name=name,
        )(*scalars, *inputs, *arrays)

    if n == 16 and lax.axis_size("replica") == 2:
        blocks = jnp.array(block_table())[lax.axis_index("replica") * 16 + section]

        def starts(*arrays):
            return [(array, 0) for array in arrays]

        tie = lax.optimization_barrier
        a_behind, a_own_y = along_ring(keep), across_y(keep)

        squares = square_sums(keep)

        b_behind = along_ring(tie((taken, a_behind, squares))[0])
        b_own_y = across_y(tie((taken, a_own_y, squares))[0])
        a_ahead = across_replica(a_behind)
        all_q = gather_queries((squares, a_own_y))

        a_opposite = along_ring(tie((a_behind, b_behind, other))[0])
        a_behind_y = across_y(tie((a_behind, b_own_y, other))[0])
        b_ahead = across_replica(tie((b_behind, a_ahead, other))[0])
        factor, owners, rows = swap_small(tie((squares, a_ahead))[0])
        ones = starts(keep, a_behind, a_own_y, taken, b_behind, b_own_y)
        total = product(blocks, 0, 3, ones, None, "rows_1")

        b_opposite = along_ring(tie((b_behind, a_opposite, total))[0])
        b_behind_y = across_y(tie((b_behind, a_behind_y, total))[0])
        a_ahead_y = across_replica(tie((a_behind_y, b_ahead, total))[0])
        all_q, owners, rows, _ = tie((all_q, owners, rows, a_opposite))
        image_q, slot = place_images(all_q, owners, rows)
        twos = starts(a_ahead, a_opposite, a_behind_y, b_ahead)
        total, image_q, slot = tie((product(blocks, 6, 2, twos, total, "rows_2"), image_q, slot))

        a_opposite_y = across_y(tie((a_opposite, b_behind_y, total))[0])
        b_opposite_y = along_ring(tie((b_behind_y, b_opposite, total))[0])
        b_ahead_y = across_replica(tie((b_behind_y, a_ahead_y, total))[0])
        total = product(blocks, 10, 3, starts(b_opposite, b_behind_y, a_ahead_y), total, "rows_3")
        lasts = starts(a_opposite_y, b_ahead_y, b_opposite_y)
        slots = product(blocks, 13, 3, lasts, total, "rows_4", last=(image_q, slot, factor))
        length, slots = tie((context_length, slots))
        res_out, res_top, res_sum = resident(length)
    else:
        res_out, res_top, res_sum = resident(context_length)
        squares = square_sums(taken)
        factor, owners, rows = swap_small(squares)
        image_q, slot = place_images(gather_queries(squares), owners, rows)
        a = gather_plain(keep)
        b = gather_plain(taken)
        chips = jnp.array([chip for chip, _, _ in a], jnp.int32)
        total = product(chips * 2 + core, 0, 2, [piece[1:] for piece in a], None, "rows_a")
        slots = product(
            chips * 2 + 1 - core, 0, 2, [piece[1:] for piece in b], total, "rows_b", last=(image_q, slot, factor)
        )
    got = lax.all_to_all(slots, "section", split_axis=0, concat_axis=0, tiled=True)

    return pl.pallas_call(
        combine_kernel,
        grid=(1,),
        in_specs=[
            whole((n, 3, HALF_QH, HD)),
            whole((decode_rows, QH, HD)),
            whole((QH, HD)),
            whole((QH, HD)),
        ],
        out_specs=whole((decode_rows, QH * HD)),
        scratch_shapes=[pltpu.VMEM((decode_rows, QH, HD), jnp.float32)],
        out_shape=jax.ShapeDtypeStruct((decode_rows, QH * HD), jnp.bfloat16),
        compiler_params=pltpu.CompilerParams(vmem_limit_bytes=60 * 2**20),
        name="combine",
    )(got, res_out, res_top, res_sum)


def solution(mesh):
    placed = (
        P(("replica", "section"), None),
        P("section", None),
        P(("replica", "section")),
        P(("replica", "section")),
        P(("replica", "section"), None),
        P(("replica", "section"), None, None),
        P(("replica", "section")),
    )
    return jax.shard_map(
        per_device,
        mesh=mesh,
        in_specs=placed,
        out_specs=P(("replica", "section"), None),
        check_vma=False,
    )
```

```python
import functools
import math

import jax
import jax.numpy as jnp
import numpy as np
from jax import lax
from jax.experimental import pallas as pl
from jax.experimental.pallas import tpu as pltpu
from jax.sharding import PartitionSpec as P

HD = 128
KVH = 4
QH = 32
IMG_TOK = 64
GROUP = QH // KVH
HALF_KVH = KVH // 2
HALF_QH = QH // 2
SCALE = 1.0 / math.sqrt(HD)
EPS = 1e-05

LANES = 64
N_KINDS = 7

masked_score = -1e30


def swap_core(x):
    n = lax.axis_size("section")
    return lax.ppermute(x, "section", [(i, i ^ 1) for i in range(n)])


def gather_plain(chunk):
    n = lax.axis_size("section")
    rows = chunk.shape[0]
    groups = [list(range(core, n, 2)) for core in range(2)]
    whole = lax.all_gather(chunk, "section", axis=0, tiled=True, axis_index_groups=groups)
    return [(chip, whole, chip * rows) for chip in range(n // 2)]


RING = [0, 1, 3, 2]


def along_ring(x):
    perm = []
    for rep, way in ((0, 1), (1, -1)):
        for p in range(4):
            for low in range(4):
                perm.append((rep * 16 + RING[p] * 4 + low, rep * 16 + RING[(p + way) % 4] * 4 + low))
    return lax.ppermute(x, ("replica", "section"), perm)


def across_y(x):
    return lax.ppermute(x, "section", [(i, i ^ 2) for i in range(16)])


def across_replica(x):
    return lax.ppermute(x, "replica", [(0, 1), (1, 0)])


STEPS = (("own", "behind", "own_y"), ("ahead", "opposite", "behind_y"), ("ahead_y", "opposite_y"))


def block_table():
    table = []
    for rep in range(2):
        for section in range(16):
            z, y, core = section // 4, section // 2 % 2, section % 2
            way = 1 - 2 * rep
            place = RING.index(z)
            ring = {"own": place, "behind": place - way, "ahead": place + way, "opposite": place + 2}

            def blocks(step, other):
                out = []
                for name in STEPS[step]:
                    chip = RING[ring[name.removesuffix("_y")] % 4] * 2 + (1 - y if name.endswith("_y") else y)
                    out.append(chip * 2 + (core ^ other))
                return out

            def both(step):
                return [block for pair in zip(blocks(step, 0), blocks(step, 1)) for block in pair]

            three = both(2)
            table.append(both(0) + both(1) + [three[0], three[2], three[3], three[1]])
    return np.array(table, np.int32)


def square_kernel(states_ref, out_ref):
    total = None
    for i in range(0, states_ref.shape[1], HD):
        values = states_ref[:, i : i + HD].astype(jnp.float32)
        values = values * values
        total = values if total is None else total + values
    out_ref[...] = jnp.sum(total, axis=1, keepdims=True)


def split_kernel(core_ref, keep_in, give_in, keep_ref, give_ref):
    keep_ref[...] = keep_in[...]
    give_ref[...] = give_in[...]


def accumulate(layout, token_refs, piece_refs, weight, total, sems, carry_ref=None, carry=None):
    step, half = pl.program_id(0), pl.program_id(1)
    tokens, rows = token_refs[0].shape
    count = len(token_refs) // 2
    depth = count * rows
    copies = [
        pltpu.make_async_copy(
            piece_refs[which].at[pl.ds(start, size)], weight.at[pl.ds(place, size)], sems.at[i]
        )
        for i, (which, start, size, place) in enumerate(layout)
    ]

    @pl.when((step == 0) & (half == 0))
    def _():
        for copy in copies:
            copy.start()

    for i in range(weight.shape[0] // depth):

        @pl.when((step == i) & (half == 0))
        def _():
            for copy, (_, _, _, place) in zip(copies, layout):
                if place // depth == i:
                    copy.wait()

    if carry_ref is not None:
        carried = pltpu.make_async_copy(carry_ref, carry, sems.at[len(layout)])

        @pl.when((step == 0) & (half == 0))
        def _():
            carried.start()

    for side in range(2):

        @pl.when(half == side)
        def _():
            states = jnp.concatenate([ref[...] for ref in token_refs[side * count : (side + 1) * count]], axis=1)
            block = weight[pl.ds(pl.multiple_of(step * depth, depth), depth), :]
            product = jnp.dot(states, block, preferred_element_type=jnp.float32)
            rows_of_side = pl.ds(side * tokens, tokens)

            @pl.when(step == 0)
            def _():
                total[rows_of_side, :] = product

            @pl.when(step > 0)
            def _():
                total[rows_of_side, :] += product

    if carry_ref is not None:

        @pl.when((step == pl.num_programs(0) - 1) & (half == 1))
        def _():
            carried.wait()
            total[...] += carry[...]


def first_kernel(layout, count, block_ref, *refs):
    total, weight, sems = refs[-3:]
    accumulate(layout, refs[: 2 * count], refs[2 * count : -3], weight, total, sems)


def next_kernel(layout, count, block_ref, *refs):
    total, weight, carry, sems = refs[-4:]
    token_refs, (carry_ref, *piece_refs) = refs[: 2 * count], refs[2 * count : -4]
    accumulate(layout, token_refs, piece_refs, weight, total, sems, carry_ref, carry)


def parts_of(values, count):
    out = []
    for _ in range(count):
        part = values.astype(jnp.bfloat16).astype(jnp.float32)
        out.append(part)
        values = values - part
    return out


def last_kernel(layout, count, width, block_ref, slot_ref, *refs):
    token_refs, (carry_ref, query_ref, factor_ref, *piece_refs) = refs[: 2 * count], refs[2 * count : -7]
    slots_ref, weight, carry, total, summed, stats, sems = refs[-7:]
    images = query_ref.shape[1] // GROUP

    @pl.when((pl.program_id(0) == 0) & (pl.program_id(1) == 0))
    def _():
        slots_ref[...] = jnp.zeros_like(slots_ref)

    accumulate(layout, token_refs, piece_refs, weight, total, sems, carry_ref, carry)

    @pl.when((pl.program_id(0) == pl.num_programs(0) - 1) & (pl.program_id(1) == 1))
    def _():
        tokens = total.shape[0]
        queries = query_ref.shape[1]
        factor = lax.rsqrt(factor_ref[...] / width + EPS)
        image_of_query = lax.broadcasted_iota(jnp.int32, (queries, tokens), 0) // GROUP
        image_of_token = lax.broadcasted_iota(jnp.int32, (queries, tokens), 1) // IMG_TOK
        live = image_of_query == image_of_token
        lane = lax.broadcasted_iota(jnp.int32, (queries, HD), 1)
        for head in range(HALF_KVH):
            part = slice(head * GROUP, (head + 1) * GROUP)
            keys = (total[:, head * HD : (head + 1) * HD] * factor).astype(jnp.bfloat16)
            at = (HALF_KVH + head) * HD
            values = (total[:, at : at + HD] * factor).astype(jnp.bfloat16)
            scores = (
                lax.dot_general(
                    query_ref[head], keys, (((1,), (1,)), ((), ())), preferred_element_type=jnp.float32
                )
                * SCALE
            )
            scores = jnp.where(live, scores, masked_score)
            top = jnp.max(scores, axis=1, keepdims=True)
            weights = jnp.where(live, jnp.exp(scores - top), 0.0)
            total_weight = jnp.sum(weights, axis=1, keepdims=True)
            out = jnp.dot(weights.astype(jnp.bfloat16), values, preferred_element_type=jnp.float32)
            summed[:, part, :] = out.reshape(images, GROUP, HD)
            kinds = parts_of(top, 3) + parts_of(total_weight, 3) + [jnp.ones_like(top)]
            tile = jnp.zeros((queries, HD), jnp.float32)
            for kind, column in enumerate(kinds):
                tile = jnp.where(lane == kind * 8, column, tile)
            stats[:, part, :] = tile.reshape(images, GROUP, HD)
        for image in range(images):
            owner, which = slot_ref[0, image], slot_ref[1, image]
            slots_ref[owner, which] = summed[image].astype(jnp.bfloat16)
            tile = pltpu.roll(stats[image], which * LANES + slot_ref[2, image], 1)
            slots_ref[owner, 2] = slots_ref[owner, 2] + tile.astype(jnp.bfloat16)


def resident_kernel(length_ref, query_ref, cache_ref, out_ref, top_ref, sum_ref):
    step = pl.program_id(0)
    rows, context = cache_ref.shape[:2]
    place = lax.broadcasted_iota(jnp.int32, (QH, context), 1)
    lane = lax.broadcasted_iota(jnp.int32, (QH, HD), 1)

    @pl.when(step == 0)
    def _():
        top_ref[...] = jnp.zeros_like(top_ref)
        sum_ref[...] = jnp.zeros_like(sum_ref)

    parts = [slice(head * GROUP, (head + 1) * GROUP) for head in range(KVH)]
    scores = [
        jnp.concatenate(
            [
                lax.dot_general(
                    query_ref[row, part, :],
                    cache_ref[row, :, head * HD : (head + 1) * HD],
                    (((1,), (1,)), ((), ())),
                    preferred_element_type=jnp.float32,
                )
                for head, part in enumerate(parts)
            ],
            axis=0,
        )
        for row in range(rows)
    ]
    for row in range(rows):
        live = place < length_ref[step * rows + row]
        score = jnp.where(live, scores[row] * SCALE, masked_score)
        top = jnp.max(score, axis=1, keepdims=True)
        weights = jnp.where(live, jnp.exp(score - top), 0.0)
        mine = lane == step * rows + row
        top_ref[...] = jnp.where(mine, top, top_ref[...])
        sum_ref[...] = jnp.where(mine, jnp.sum(weights, axis=1, keepdims=True), sum_ref[...])
        weights = weights.astype(jnp.bfloat16)
        for head, part in enumerate(parts):
            at = (KVH + head) * HD
            out_ref[row, part, :] = jnp.dot(
                weights[part], cache_ref[row, :, at : at + HD], preferred_element_type=jnp.float32
            )


def combine_kernel(got_ref, res_out_ref, res_top_ref, res_sum_ref, out_ref, acc):
    chips = got_ref.shape[0] // 2
    rows = res_out_ref.shape[0]
    lane = lax.broadcasted_iota(jnp.int32, (HALF_QH, HD), 1)
    head_lane = (lane % LANES) < 8

    def moved(tile, by):
        return pltpu.roll(tile, HD - by, 1)

    for core in range(2):
        part = slice(core * HALF_QH, (core + 1) * HALF_QH)
        tops, sums, here = [], [], []
        for chip in range(chips):
            tile = got_ref[chip * 2 + core, 2].astype(jnp.float32)
            present = (moved(tile, 48) > 0.5) & head_lane
            tops.append(jnp.where(present, tile + moved(tile, 8) + moved(tile, 16), masked_score))
            sums.append(moved(tile, 24) + moved(tile, 32) + moved(tile, 40))
            here.append(present)
        row_top = functools.reduce(jnp.maximum, tops)
        row_top = jnp.maximum(row_top, pltpu.roll(row_top, LANES, 1))
        res_top = jnp.where(lane < 8, res_top_ref[part, :], masked_score)
        res_top = jnp.maximum(res_top, pltpu.roll(res_top, LANES, 1))
        row_top = jnp.maximum(row_top, res_top)
        weights = [jnp.where(a, jnp.exp(t - row_top), 0.0) for a, t in zip(here, tops)]
        joined = sum(w * s for w, s in zip(weights, sums))
        res_weight = jnp.exp(res_top - row_top)
        denominator = joined + pltpu.roll(joined, LANES, 1) + res_weight * res_sum_ref[part, :]
        scale = jnp.where(lane < 8, 1.0 / denominator, 0.0)
        scale = scale + pltpu.roll(scale, LANES, 1)
        res_share = res_weight * scale
        weights = [w * scale for w in weights]
        for row in range(rows):
            value = res_out_ref[row, part, :] * res_share[:, row : row + 1]
            for chip in range(chips):
                for which in range(2):
                    at = which * LANES + row
                    value += weights[chip][:, at : at + 1] * got_ref[chip * 2 + core, which].astype(jnp.float32)
            acc[row, part, :] = value
    for head in range(QH):
        out_ref[:, head * HD : (head + 1) * HD] = acc[:, head, :].astype(jnp.bfloat16)


def whole(shape):
    return pl.BlockSpec(shape, lambda i, *_: (0,) * len(shape))


def per_device(prompt_states, kv_weight, image_owner, image_row, queries, cache, context_length):
    n = lax.axis_size("section")
    section = lax.axis_index("section")
    core = section % 2
    tokens, width = prompt_states.shape
    rows_dev, kv_width = kv_weight.shape
    columns_dev = kv_width // 2
    images = image_owner.shape[0]
    decode_rows = queries.shape[0]
    context = cache.shape[1]
    n_queries = 2 * images * GROUP

    cut = columns_dev // 2
    keep, give = pl.pallas_call(
        split_kernel,
        grid_spec=pltpu.PrefetchScalarGridSpec(
            num_scalar_prefetch=1,
            grid=(2,),
            in_specs=[
                pl.BlockSpec((rows_dev, cut), lambda i, core_ref: (0, 2 * i + core_ref[0])),
                pl.BlockSpec((rows_dev, cut), lambda i, core_ref: (0, 2 * i + 1 - core_ref[0])),
            ],
            out_specs=[pl.BlockSpec((rows_dev, cut), lambda i, core_ref: (0, i))] * 2,
        ),
        out_shape=[jax.ShapeDtypeStruct((rows_dev, columns_dev), jnp.bfloat16)] * 2,
        cost_estimate=pl.CostEstimate(flops=0, bytes_accessed=2**18, transcendentals=0),
        name="split",
    )(core.reshape(1), kv_weight, kv_weight)
    taken = swap_core(give)
    swapped_states, _ = lax.optimization_barrier((prompt_states, taken))
    other = swap_core(swapped_states)

    def square_sums(tied):
        states, _ = lax.optimization_barrier((prompt_states, tied))
        return pl.pallas_call(
            square_kernel,
            grid=(8,),
            in_specs=[pl.BlockSpec((tokens // 8, width), lambda i: (i, 0))],
            out_specs=pl.BlockSpec((tokens // 8, 1), lambda i: (i, 0)),
            out_shape=jax.ShapeDtypeStruct((tokens, 1), jnp.float32),
            cost_estimate=pl.CostEstimate(flops=0, bytes_accessed=2**18, transcendentals=0),
            compiler_params=pltpu.CompilerParams(vmem_limit_bytes=60 * 2**20),
            name="squares",
        )(pltpu.with_memory_space_constraint(states, pltpu.HBM))[:, 0]

    def swap_small(squares):
        places = jnp.concatenate([image_owner, image_row]).astype(jnp.float32)
        small = jnp.concatenate([squares, places])
        small = jnp.pad(small, (0, -small.shape[0] % (8 * HD))).reshape(-1, HD)
        got = swap_core(small).reshape(-1)
        factor = jnp.concatenate([squares, got[:tokens]])[:, None]
        at = tokens + images
        owners = jnp.concatenate([image_owner, got[tokens:at].astype(jnp.int32)])
        rows = jnp.concatenate([image_row, got[at : at + images].astype(jnp.int32)])
        return factor, owners, rows

    def gather_queries(tied):
        mine, _ = lax.optimization_barrier((queries, tied))
        send_q = mine.reshape(decode_rows, 2, HALF_QH * HD).transpose(1, 0, 2)
        send_q = jnp.broadcast_to(send_q[None], (n // 2, 2, decode_rows, HALF_QH * HD)).reshape(
            n, decode_rows, HALF_QH * HD
        )
        all_q = lax.all_to_all(send_q, "section", split_axis=0, concat_axis=0, tiled=True)
        return all_q.reshape(n * decode_rows, HALF_QH * HD)

    def place_images(all_q, owners, rows):
        target = owners * decode_rows + rows
        pick = (target[:, None] == jnp.arange(n * decode_rows)[None, :]).astype(jnp.bfloat16)
        image_q = jnp.dot(pick, all_q, preferred_element_type=jnp.float32).astype(jnp.bfloat16)
        image_q = image_q.reshape(2 * images, HALF_KVH, GROUP, HD).transpose(1, 0, 2, 3)
        which = jnp.concatenate([jnp.full((images,), core), jnp.full((images,), 1 - core)]).astype(jnp.int32)
        return image_q.reshape(HALF_KVH, n_queries, HD), jnp.stack([owners, which, rows])

    def resident(length):
        step_rows = 2
        return pl.pallas_call(
            resident_kernel,
            grid_spec=pltpu.PrefetchScalarGridSpec(
                num_scalar_prefetch=1,
                grid=(decode_rows // step_rows,),
                in_specs=[
                    pl.BlockSpec((step_rows, QH, HD), lambda i, *_: (i, 0, 0)),
                    pl.BlockSpec((step_rows, context, kv_width), lambda i, *_: (i, 0, 0)),
                ],
                out_specs=[
                    pl.BlockSpec((step_rows, QH, HD), lambda i, *_: (i, 0, 0)),
                    whole((QH, HD)),
                    whole((QH, HD)),
                ],
            ),
            out_shape=[
                jax.ShapeDtypeStruct((decode_rows, QH, HD), jnp.float32),
                jax.ShapeDtypeStruct((QH, HD), jnp.float32),
                jax.ShapeDtypeStruct((QH, HD), jnp.float32),
            ],
            compiler_params=pltpu.CompilerParams(vmem_limit_bytes=60 * 2**20),
            cost_estimate=pl.CostEstimate(flops=0, bytes_accessed=2**18, transcendentals=0),
            name="resident",
        )(length, queries.reshape(decode_rows, QH, HD), cache)

    def product(blocks, base, count, pieces, carry, name, last=None):
        arrays, layout = [], []
        for index, piece in enumerate(pieces):
            place = index * rows_dev
            for array, start, rows in piece:
                at = [i for i, known in enumerate(arrays) if known is array]
                if not at:
                    arrays.append(array)
                    at = [len(arrays) - 1]
                layout.append((at[0], start, rows, place))
                place += rows
        steps = len(pieces) // count

        def token_spec(k):
            return pl.BlockSpec((tokens, rows_dev), lambda i, half, block_ref, *_: (0, block_ref[base + count * i + k]))

        anywhere = pl.BlockSpec(memory_space=pl.ANY)
        in_specs = [token_spec(k) for k in range(count)] * 2
        own_tokens = pltpu.with_memory_space_constraint(prompt_states, pltpu.HBM)
        other_tokens = pltpu.with_memory_space_constraint(other, pltpu.HBM)
        inputs = [own_tokens] * count + [other_tokens] * count
        scalars = [blocks]
        scratch = [pltpu.VMEM((len(pieces) * rows_dev, columns_dev), jnp.bfloat16)]
        total = (2 * tokens, columns_dev)
        body = functools.partial(first_kernel, layout, count)
        if carry is not None:
            body = functools.partial(next_kernel, layout, count)
            in_specs = in_specs + [anywhere]
            inputs = inputs + [carry]
            scratch = scratch + [pltpu.VMEM(total, jnp.float32)]
        out_specs, out_shape = whole(total), jax.ShapeDtypeStruct(total, jnp.float32)
        if last is not None:
            image_q, slot, factor = last
            body = functools.partial(last_kernel, layout, count, width)
            scalars = scalars + [slot]
            in_specs = in_specs + [whole((HALF_KVH, n_queries, HD)), whole((2 * tokens, 1))]
            inputs = inputs + [image_q, factor]
            out_specs = whole((n, 3, HALF_QH, HD))
            out_shape = jax.ShapeDtypeStruct((n, 3, HALF_QH, HD), jnp.bfloat16)
            scratch = scratch + [
                pltpu.VMEM(total, jnp.float32),
                pltpu.VMEM((2 * images, HALF_QH, HD), jnp.float32),
                pltpu.VMEM((2 * images, HALF_QH, HD), jnp.float32),
            ]
        return pl.pallas_call(
            body,
            grid_spec=pltpu.PrefetchScalarGridSpec(
                num_scalar_prefetch=len(scalars),
                grid=(steps, 2),
                in_specs=in_specs + [anywhere] * len(arrays),
                out_specs=out_specs,
                scratch_shapes=scratch + [pltpu.SemaphoreType.DMA((len(layout) + 1,))],
            ),
            out_shape=out_shape,
            compiler_params=pltpu.CompilerParams(vmem_limit_bytes=60 * 2**20),
            cost_estimate=pl.CostEstimate(flops=0, bytes_accessed=2**18, transcendentals=0),
            name=name,
        )(*scalars, *inputs, *arrays)

    if n == 16 and lax.axis_size("replica") == 2:
        blocks = jnp.array(block_table())[lax.axis_index("replica") * 16 + section]

        def starts(*arrays):
            return [[(array, 0, rows_dev)] for array in arrays]

        tie = lax.optimization_barrier

        def both(array):
            return [[(array, half, rows_dev)] for half in (0, rows_dev)]

        own = jnp.concatenate([keep, taken], axis=0)
        behind, own_y = along_ring(own), across_y(own)
        squares = square_sums(own)

        source, squares, _ = tie((behind, squares, own_y))
        opposite, behind_y, ahead = along_ring(source), across_y(source), across_replica(source)
        total = product(blocks, 0, 2, both(own) + both(behind) + both(own_y), None, "rows_1")
        factor, owners, rows = swap_small(squares)
        all_q = gather_queries(squares)

        cut = rows_dev + rows_dev // 2
        source, source_y, source_x, total, owners, rows, all_q = tie(
            (behind_y, opposite, ahead, total, owners, rows, all_q)
        )
        opposite_y_b = along_ring(source[rows_dev:])
        opposite_y_a = across_y(source_y[:rows_dev])
        ahead_y_x = across_replica(source[:cut])
        ahead_y_y = across_y(source_x[cut:])
        image_q, slot = place_images(all_q, owners, rows)
        total = product(blocks, 6, 2, both(ahead) + both(opposite) + both(behind_y), total, "rows_2")
        ahead_y_b = [(ahead_y_x, rows_dev, cut - rows_dev), (ahead_y_y, 0, 2 * rows_dev - cut)]
        lasts = starts(ahead_y_x, opposite_y_a, opposite_y_b) + [ahead_y_b]
        slots = product(blocks, 12, 2, lasts, total, "rows_3", last=(image_q, slot, factor))
        length, slots = tie((context_length, slots))
        res_out, res_top, res_sum = resident(length)
    else:
        res_out, res_top, res_sum = resident(context_length)
        squares = square_sums(taken)
        factor, owners, rows = swap_small(squares)
        image_q, slot = place_images(gather_queries(squares), owners, rows)
        a = gather_plain(keep)
        b = gather_plain(taken)
        chips = jnp.array([chip for chip, _, _ in a], jnp.int32)
        total = product(chips * 2 + core, 0, 2, [[(array, start, rows_dev)] for _, array, start in a], None, "rows_a")
        slots = product(
            chips * 2 + 1 - core, 0, 2, [[(array, start, rows_dev)] for _, array, start in b], total, "rows_b", last=(image_q, slot, factor)
        )
    got = lax.all_to_all(slots, "section", split_axis=0, concat_axis=0, tiled=True)

    return pl.pallas_call(
        combine_kernel,
        grid=(1,),
        in_specs=[
            whole((n, 3, HALF_QH, HD)),
            whole((decode_rows, QH, HD)),
            whole((QH, HD)),
            whole((QH, HD)),
        ],
        out_specs=whole((decode_rows, QH * HD)),
        scratch_shapes=[pltpu.VMEM((decode_rows, QH, HD), jnp.float32)],
        out_shape=jax.ShapeDtypeStruct((decode_rows, QH * HD), jnp.bfloat16),
        compiler_params=pltpu.CompilerParams(vmem_limit_bytes=60 * 2**20),
        name="combine",
    )(got, res_out, res_top, res_sum)


def solution(mesh):
    placed = (
        P(("replica", "section"), None),
        P("section", None),
        P(("replica", "section")),
        P(("replica", "section")),
        P(("replica", "section"), None),
        P(("replica", "section"), None, None),
        P(("replica", "section")),
    )
    return jax.shard_map(
        per_device,
        mesh=mesh,
        in_specs=placed,
        out_specs=P(("replica", "section"), None),
        check_vma=False,
    )
```

```python
import functools
import math

import jax
import jax.numpy as jnp
import numpy as np
from jax import lax
from jax.experimental import pallas as pl
from jax.experimental.pallas import tpu as pltpu
from jax.sharding import PartitionSpec as P

HD = 128
KVH = 4
QH = 32
IMG_TOK = 64
GROUP = QH // KVH
HALF_KVH = KVH // 2
HALF_QH = QH // 2
SCALE = 1.0 / math.sqrt(HD)
EPS = 1e-05

LANES = 64
N_KINDS = 7

masked_score = -1e30


def swap_core(x):
    n = lax.axis_size("section")
    return lax.ppermute(x, "section", [(i, i ^ 1) for i in range(n)])


def gather_plain(chunk):
    n = lax.axis_size("section")
    rows = chunk.shape[0]
    groups = [list(range(core, n, 2)) for core in range(2)]
    whole = lax.all_gather(chunk, "section", axis=0, tiled=True, axis_index_groups=groups)
    return [(chip, whole, chip * rows) for chip in range(n // 2)]


RING = [0, 1, 3, 2]


def along_ring(x, sign=1):
    perm = []
    for rep, way in ((0, sign), (1, -sign)):
        for p in range(4):
            for low in range(4):
                perm.append((rep * 16 + RING[p] * 4 + low, rep * 16 + RING[(p + way) % 4] * 4 + low))
    return lax.ppermute(x, ("replica", "section"), perm)


def across_y(x):
    return lax.ppermute(x, "section", [(i, i ^ 2) for i in range(16)])


def across_replica(x):
    return lax.ppermute(x, "replica", [(0, 1), (1, 0)])


STEPS = (("own", "behind", "own_y"), ("ahead", "opposite", "behind_y"), ("ahead_y", "opposite_y"))


def block_table():
    table = []
    for rep in range(2):
        for section in range(16):
            z, y, core = section // 4, section // 2 % 2, section % 2
            way = 1 - 2 * rep
            place = RING.index(z)
            ring = {"own": place, "behind": place - way, "ahead": place + way, "opposite": place + 2}

            def blocks(step, other):
                out = []
                for name in STEPS[step]:
                    chip = RING[ring[name.removesuffix("_y")] % 4] * 2 + (1 - y if name.endswith("_y") else y)
                    out.append(chip * 2 + (core ^ other))
                return out

            def both(step):
                return [block for pair in zip(blocks(step, 0), blocks(step, 1)) for block in pair]

            three = both(2)
            places = [0] * 8
            for i, name in enumerate(("own", "behind", "ahead", "opposite")):
                chip = RING[ring[name] % 4] * 2
                places[chip + y], places[chip + 1 - y] = i, 4 + i
            table.append(both(0) + both(1) + [three[0], three[2], three[3], three[1]] + places)
    return np.array(table, np.int32)


def square_kernel(states_ref, out_ref):
    total = None
    for i in range(0, states_ref.shape[1], HD):
        values = states_ref[:, i : i + HD].astype(jnp.float32)
        values = values * values
        total = values if total is None else total + values
    out_ref[...] = jnp.sum(total, axis=1, keepdims=True)


def split_kernel(core_ref, keep_in, give_in, keep_ref, give_ref):
    keep_ref[...] = keep_in[...]
    give_ref[...] = give_in[...]


def accumulate(layout, token_refs, piece_refs, weight, total, sems, carry_ref=None, carry=None):
    step = pl.program_id(0)
    rows = token_refs[0].shape[1]
    count = len(token_refs) // 2
    depth = count * rows
    copies = [
        pltpu.make_async_copy(
            piece_refs[which].at[pl.ds(start, size)], weight.at[pl.ds(place, size)], sems.at[i]
        )
        for i, (which, start, size, place) in enumerate(layout)
    ]
    carried = []
    if carry_ref is not None:
        carried = [pltpu.make_async_copy(carry_ref, carry, sems.at[len(layout)])]

    @pl.when(step == 0)
    def _():
        for copy in copies + carried:
            copy.start()

    for i in range(weight.shape[0] // depth):

        @pl.when(step == i)
        def _():
            for copy, (_, _, _, place) in zip(copies, layout):
                if place // depth == i:
                    copy.wait()

    states = jnp.concatenate(
        [
            jnp.concatenate([ref[...] for ref in token_refs[side * count : (side + 1) * count]], axis=1)
            for side in range(2)
        ],
        axis=0,
    )
    block = weight[pl.ds(pl.multiple_of(step * depth, depth), depth), :]
    product = jnp.dot(states, block, preferred_element_type=jnp.float32)

    @pl.when(step == 0)
    def _():
        total[...] = product

    @pl.when(step > 0)
    def _():
        total[...] += product

    if carry_ref is not None:

        @pl.when(step == pl.num_programs(0) - 1)
        def _():
            carried[0].wait()
            total[...] += carry[...]


def first_kernel(layout, count, block_ref, *refs):
    total, weight, sems = refs[-3:]
    accumulate(layout, refs[: 2 * count], refs[2 * count : -3], weight, total, sems)


def next_kernel(layout, count, block_ref, *refs):
    total, weight, carry, sems = refs[-4:]
    token_refs, (carry_ref, *piece_refs) = refs[: 2 * count], refs[2 * count : -4]
    accumulate(layout, token_refs, piece_refs, weight, total, sems, carry_ref, carry)


def parts_of(values, count):
    out = []
    for _ in range(count):
        part = values.astype(jnp.bfloat16).astype(jnp.float32)
        out.append(part)
        values = values - part
    return out


def last_kernel(layout, count, width, block_ref, slot_ref, *refs):
    token_refs, (carry_ref, query_ref, factor_ref, *piece_refs) = refs[: 2 * count], refs[2 * count : -7]
    slots_ref, weight, carry, total, summed, stats, sems = refs[-7:]
    images = query_ref.shape[1] // GROUP

    @pl.when(pl.program_id(0) == 0)
    def _():
        slots_ref[...] = jnp.zeros_like(slots_ref)

    accumulate(layout, token_refs, piece_refs, weight, total, sems, carry_ref, carry)

    @pl.when(pl.program_id(0) == pl.num_programs(0) - 1)
    def _():
        tokens = total.shape[0]
        queries = query_ref.shape[1]
        factor = lax.rsqrt(factor_ref[...] / width + EPS)
        image_of_query = lax.broadcasted_iota(jnp.int32, (queries, tokens), 0) // GROUP
        image_of_token = lax.broadcasted_iota(jnp.int32, (queries, tokens), 1) // IMG_TOK
        live = image_of_query == image_of_token
        lane = lax.broadcasted_iota(jnp.int32, (queries, HD), 1)
        for head in range(HALF_KVH):
            part = slice(head * GROUP, (head + 1) * GROUP)
            keys = (total[:, head * HD : (head + 1) * HD] * factor).astype(jnp.bfloat16)
            at = (HALF_KVH + head) * HD
            values = (total[:, at : at + HD] * factor).astype(jnp.bfloat16)
            scores = (
                lax.dot_general(
                    query_ref[head], keys, (((1,), (1,)), ((), ())), preferred_element_type=jnp.float32
                )
                * SCALE
            )
            scores = jnp.where(live, scores, masked_score)
            top = jnp.max(scores, axis=1, keepdims=True)
            weights = jnp.where(live, jnp.exp(scores - top), 0.0)
            total_weight = jnp.sum(weights, axis=1, keepdims=True)
            out = jnp.dot(weights.astype(jnp.bfloat16), values, preferred_element_type=jnp.float32)
            summed[:, part, :] = out.reshape(images, GROUP, HD)
            kinds = parts_of(top, 3) + parts_of(total_weight, 3) + [jnp.ones_like(top)]
            tile = jnp.zeros((queries, HD), jnp.float32)
            for kind, column in enumerate(kinds):
                tile = jnp.where(lane == kind * 8, column, tile)
            stats[:, part, :] = tile.reshape(images, GROUP, HD)
        for image in range(images):
            owner, which = slot_ref[0, image], slot_ref[1, image]
            slots_ref[owner, which] = summed[image].astype(jnp.bfloat16)
            tile = pltpu.roll(stats[image], which * LANES + slot_ref[2, image], 1)
            slots_ref[owner, 2] = slots_ref[owner, 2] + tile.astype(jnp.bfloat16)


def resident_kernel(length_ref, query_ref, cache_ref, out_ref, top_ref, sum_ref):
    step = pl.program_id(0)
    rows, context = cache_ref.shape[:2]
    place = lax.broadcasted_iota(jnp.int32, (QH, context), 1)
    lane = lax.broadcasted_iota(jnp.int32, (QH, HD), 1)

    @pl.when(step == 0)
    def _():
        top_ref[...] = jnp.zeros_like(top_ref)
        sum_ref[...] = jnp.zeros_like(sum_ref)

    parts = [slice(head * GROUP, (head + 1) * GROUP) for head in range(KVH)]
    scores = [
        jnp.concatenate(
            [
                lax.dot_general(
                    query_ref[row, part, :],
                    cache_ref[row, :, head * HD : (head + 1) * HD],
                    (((1,), (1,)), ((), ())),
                    preferred_element_type=jnp.float32,
                )
                for head, part in enumerate(parts)
            ],
            axis=0,
        )
        for row in range(rows)
    ]
    for row in range(rows):
        live = place < length_ref[step * rows + row]
        score = jnp.where(live, scores[row] * SCALE, masked_score)
        top = jnp.max(score, axis=1, keepdims=True)
        weights = jnp.where(live, jnp.exp(score - top), 0.0)
        mine = lane == step * rows + row
        top_ref[...] = jnp.where(mine, top, top_ref[...])
        sum_ref[...] = jnp.where(mine, jnp.sum(weights, axis=1, keepdims=True), sum_ref[...])
        weights = weights.astype(jnp.bfloat16)
        for head, part in enumerate(parts):
            at = (KVH + head) * HD
            out_ref[row, part, :] = jnp.dot(
                weights[part], cache_ref[row, :, at : at + HD], preferred_element_type=jnp.float32
            )


def combine_kernel(got_ref, res_out_ref, res_top_ref, res_sum_ref, out_ref, acc):
    chips = got_ref.shape[0] // 2
    rows = res_out_ref.shape[0]
    lane = lax.broadcasted_iota(jnp.int32, (HALF_QH, HD), 1)
    head_lane = (lane % LANES) < 8

    def moved(tile, by):
        return pltpu.roll(tile, HD - by, 1)

    for core in range(2):
        part = slice(core * HALF_QH, (core + 1) * HALF_QH)
        tops, sums, here = [], [], []
        for chip in range(chips):
            tile = got_ref[chip * 2 + core, 2].astype(jnp.float32)
            present = (moved(tile, 48) > 0.5) & head_lane
            tops.append(jnp.where(present, tile + moved(tile, 8) + moved(tile, 16), masked_score))
            sums.append(moved(tile, 24) + moved(tile, 32) + moved(tile, 40))
            here.append(present)
        row_top = functools.reduce(jnp.maximum, tops)
        row_top = jnp.maximum(row_top, pltpu.roll(row_top, LANES, 1))
        res_top = jnp.where(lane < 8, res_top_ref[part, :], masked_score)
        res_top = jnp.maximum(res_top, pltpu.roll(res_top, LANES, 1))
        row_top = jnp.maximum(row_top, res_top)
        weights = [jnp.where(a, jnp.exp(t - row_top), 0.0) for a, t in zip(here, tops)]
        joined = sum(w * s for w, s in zip(weights, sums))
        res_weight = jnp.exp(res_top - row_top)
        denominator = joined + pltpu.roll(joined, LANES, 1) + res_weight * res_sum_ref[part, :]
        scale = jnp.where(lane < 8, 1.0 / denominator, 0.0)
        scale = scale + pltpu.roll(scale, LANES, 1)
        res_share = res_weight * scale
        weights = [w * scale for w in weights]
        for row in range(rows):
            value = res_out_ref[row, part, :] * res_share[:, row : row + 1]
            for chip in range(chips):
                for which in range(2):
                    at = which * LANES + row
                    value += weights[chip][:, at : at + 1] * got_ref[chip * 2 + core, which].astype(jnp.float32)
            acc[row, part, :] = value
    for head in range(QH):
        out_ref[:, head * HD : (head + 1) * HD] = acc[:, head, :].astype(jnp.bfloat16)


def whole(shape):
    return pl.BlockSpec(shape, lambda i, *_: (0,) * len(shape))


def per_device(prompt_states, kv_weight, image_owner, image_row, queries, cache, context_length):
    n = lax.axis_size("section")
    section = lax.axis_index("section")
    core = section % 2
    tokens, width = prompt_states.shape
    rows_dev, kv_width = kv_weight.shape
    columns_dev = kv_width // 2
    images = image_owner.shape[0]
    decode_rows = queries.shape[0]
    context = cache.shape[1]
    n_queries = 2 * images * GROUP

    cut = columns_dev // 2
    keep, give = pl.pallas_call(
        split_kernel,
        grid_spec=pltpu.PrefetchScalarGridSpec(
            num_scalar_prefetch=1,
            grid=(2,),
            in_specs=[
                pl.BlockSpec((rows_dev, cut), lambda i, core_ref: (0, 2 * i + core_ref[0])),
                pl.BlockSpec((rows_dev, cut), lambda i, core_ref: (0, 2 * i + 1 - core_ref[0])),
            ],
            out_specs=[pl.BlockSpec((rows_dev, cut), lambda i, core_ref: (0, i))] * 2,
        ),
        out_shape=[jax.ShapeDtypeStruct((rows_dev, columns_dev), jnp.bfloat16)] * 2,
        cost_estimate=pl.CostEstimate(flops=0, bytes_accessed=2**18, transcendentals=0),
        name="split",
    )(core.reshape(1), kv_weight, kv_weight)
    taken = swap_core(give)
    swapped_states, _ = lax.optimization_barrier((prompt_states, taken))
    other = swap_core(swapped_states)

    def square_sums(tied):
        states, _ = lax.optimization_barrier((prompt_states, tied))
        return pl.pallas_call(
            square_kernel,
            grid=(8,),
            in_specs=[pl.BlockSpec((tokens // 8, width), lambda i: (i, 0))],
            out_specs=pl.BlockSpec((tokens // 8, 1), lambda i: (i, 0)),
            out_shape=jax.ShapeDtypeStruct((tokens, 1), jnp.float32),
            cost_estimate=pl.CostEstimate(flops=0, bytes_accessed=2**18, transcendentals=0),
            compiler_params=pltpu.CompilerParams(vmem_limit_bytes=60 * 2**20),
            name="squares",
        )(pltpu.with_memory_space_constraint(states, pltpu.HBM))[:, 0]

    def swap_small(squares):
        places = jnp.concatenate([image_owner, image_row]).astype(jnp.float32)
        small = jnp.concatenate([squares, places])
        small = jnp.pad(small, (0, -small.shape[0] % (8 * HD))).reshape(-1, HD)
        got = swap_core(small).reshape(-1)
        factor = jnp.concatenate([squares, got[:tokens]])[:, None]
        at = tokens + images
        owners = jnp.concatenate([image_owner, got[tokens:at].astype(jnp.int32)])
        rows = jnp.concatenate([image_row, got[at : at + images].astype(jnp.int32)])
        return factor, owners, rows

    query_halves = queries.reshape(decode_rows, 2, HALF_QH * HD)
    keep_q = jnp.where(core == 0, query_halves[:, 0], query_halves[:, 1])
    give_q = jnp.where(core == 0, query_halves[:, 1], query_halves[:, 0])

    def place_images(all_q, owners, rows, chip_place):
        chip_of = jnp.sum(
            jnp.where(owners[:, None] // 2 == jnp.arange(n // 2)[None, :], chip_place[None, :], 0), axis=1
        )
        target = chip_of * (2 * decode_rows) + (owners % 2 ^ core) * decode_rows + rows
        pick = (target[:, None] == jnp.arange(n * decode_rows)[None, :]).astype(jnp.bfloat16)
        image_q = jnp.dot(pick, all_q, preferred_element_type=jnp.float32).astype(jnp.bfloat16)
        image_q = image_q.reshape(2 * images, HALF_KVH, GROUP, HD).transpose(1, 0, 2, 3)
        which = jnp.concatenate([jnp.full((images,), core), jnp.full((images,), 1 - core)]).astype(jnp.int32)
        return image_q.reshape(HALF_KVH, n_queries, HD), jnp.stack([owners, which, rows])

    def resident(length):
        step_rows = 2
        return pl.pallas_call(
            resident_kernel,
            grid_spec=pltpu.PrefetchScalarGridSpec(
                num_scalar_prefetch=1,
                grid=(decode_rows // step_rows,),
                in_specs=[
                    pl.BlockSpec((step_rows, QH, HD), lambda i, *_: (i, 0, 0)),
                    pl.BlockSpec((step_rows, context, kv_width), lambda i, *_: (i, 0, 0)),
                ],
                out_specs=[
                    pl.BlockSpec((step_rows, QH, HD), lambda i, *_: (i, 0, 0)),
                    whole((QH, HD)),
                    whole((QH, HD)),
                ],
            ),
            out_shape=[
                jax.ShapeDtypeStruct((decode_rows, QH, HD), jnp.float32),
                jax.ShapeDtypeStruct((QH, HD), jnp.float32),
                jax.ShapeDtypeStruct((QH, HD), jnp.float32),
            ],
            compiler_params=pltpu.CompilerParams(vmem_limit_bytes=60 * 2**20),
            cost_estimate=pl.CostEstimate(flops=0, bytes_accessed=2**18, transcendentals=0),
            name="resident",
        )(length, queries.reshape(decode_rows, QH, HD), cache)

    def product(blocks, base, count, pieces, carry, name, last=None):
        arrays, layout = [], []
        for index, piece in enumerate(pieces):
            place = index * rows_dev
            for array, start, rows in piece:
                at = [i for i, known in enumerate(arrays) if known is array]
                if not at:
                    arrays.append(array)
                    at = [len(arrays) - 1]
                layout.append((at[0], start, rows, place))
                place += rows
        steps = len(pieces) // count

        def token_spec(k):
            return pl.BlockSpec((tokens, rows_dev), lambda i, block_ref, *_: (0, block_ref[base + count * i + k]))

        anywhere = pl.BlockSpec(memory_space=pl.ANY)
        in_specs = [token_spec(k) for k in range(count)] * 2
        own_tokens = pltpu.with_memory_space_constraint(prompt_states, pltpu.HBM)
        other_tokens = pltpu.with_memory_space_constraint(other, pltpu.HBM)
        inputs = [own_tokens] * count + [other_tokens] * count
        scalars = [blocks]
        scratch = [pltpu.VMEM((len(pieces) * rows_dev, columns_dev), jnp.bfloat16)]
        total = (2 * tokens, columns_dev)
        body = functools.partial(first_kernel, layout, count)
        if carry is not None:
            body = functools.partial(next_kernel, layout, count)
            in_specs = in_specs + [anywhere]
            inputs = inputs + [carry]
            scratch = scratch + [pltpu.VMEM(total, jnp.float32)]
        out_specs, out_shape = whole(total), jax.ShapeDtypeStruct(total, jnp.float32)
        if last is not None:
            image_q, slot, factor = last
            body = functools.partial(last_kernel, layout, count, width)
            scalars = scalars + [slot]
            in_specs = in_specs + [whole((HALF_KVH, n_queries, HD)), whole((2 * tokens, 1))]
            inputs = inputs + [image_q, factor]
            out_specs = whole((n, 3, HALF_QH, HD))
            out_shape = jax.ShapeDtypeStruct((n, 3, HALF_QH, HD), jnp.bfloat16)
            scratch = scratch + [
                pltpu.VMEM(total, jnp.float32),
                pltpu.VMEM((2 * images, HALF_QH, HD), jnp.float32),
                pltpu.VMEM((2 * images, HALF_QH, HD), jnp.float32),
            ]
        return pl.pallas_call(
            body,
            grid_spec=pltpu.PrefetchScalarGridSpec(
                num_scalar_prefetch=len(scalars),
                grid=(steps,),
                in_specs=in_specs + [anywhere] * len(arrays),
                out_specs=out_specs,
                scratch_shapes=scratch + [pltpu.SemaphoreType.DMA((len(layout) + 1,))],
            ),
            out_shape=out_shape,
            compiler_params=pltpu.CompilerParams(vmem_limit_bytes=60 * 2**20),
            cost_estimate=pl.CostEstimate(flops=0, bytes_accessed=2**18, transcendentals=0),
            name=name,
        )(*scalars, *inputs, *arrays)

    if n == 16 and lax.axis_size("replica") == 2:
        table = block_table()
        blocks = jnp.array(table)[lax.axis_index("replica") * 16 + section]

        def starts(*arrays):
            return [[(array, 0, rows_dev)] for array in arrays]

        tie = lax.optimization_barrier

        def both(array):
            return [[(array, half, rows_dev)] for half in (0, rows_dev)]

        own = jnp.concatenate([keep, taken], axis=0)
        behind, own_y = along_ring(own), across_y(own)
        squares = square_sums(own)
        own_q = jnp.concatenate([keep_q, swap_core(tie((give_q, taken))[0])], axis=0)
        behind_q, ahead_q = along_ring(own_q), along_ring(own_q, -1)

        source, squares, source_q, _ = tie((behind, squares, behind_q, (own_y, ahead_q)))
        opposite, behind_y, ahead = along_ring(source), across_y(source), across_replica(source)
        opposite_q = along_ring(source_q)
        total = product(blocks, 0, 2, both(own) + both(behind) + both(own_y), None, "rows_1")
        factor, owners, rows = swap_small(tie((squares, opposite_q))[0])
        ring_q = jnp.concatenate([own_q, behind_q, ahead_q, opposite_q], axis=0)

        cut = rows_dev + rows_dev // 2
        source, source_y, source_x, total, owners, rows, ring_q = tie(
            (behind_y, opposite, ahead, total, owners, rows, ring_q)
        )
        all_q = jnp.concatenate([ring_q, across_y(ring_q)], axis=0)
        opposite_y_b = along_ring(source[rows_dev:])
        opposite_y_a = across_y(source_y[:rows_dev])
        ahead_y_x = across_replica(source[:cut])
        ahead_y_y = across_y(source_x[cut:])
        image_q, slot = place_images(all_q, owners, rows, blocks[16:])
        total = product(blocks, 6, 2, both(ahead) + both(opposite) + both(behind_y), total, "rows_2")
        ahead_y_b = [(ahead_y_x, rows_dev, cut - rows_dev), (ahead_y_y, 0, 2 * rows_dev - cut)]
        lasts = starts(ahead_y_x, opposite_y_a, opposite_y_b) + [ahead_y_b]
        slots = product(blocks, 12, 2, lasts, total, "rows_3", last=(image_q, slot, factor))
        length, slots = tie((context_length, slots))
        res_out, res_top, res_sum = resident(length)
    else:
        res_out, res_top, res_sum = resident(context_length)
        squares = square_sums(taken)
        factor, owners, rows = swap_small(squares)
        chip_q = jnp.concatenate([keep_q, swap_core(give_q)], axis=0)
        groups = [list(range(side, n, 2)) for side in range(2)]
        all_q = lax.all_gather(chip_q, "section", axis=0, tiled=True, axis_index_groups=groups)
        image_q, slot = place_images(all_q, owners, rows, jnp.arange(n // 2))
        a = gather_plain(keep)
        b = gather_plain(taken)
        chips = jnp.array([chip for chip, _, _ in a], jnp.int32)
        total = product(chips * 2 + core, 0, 2, [[(array, start, rows_dev)] for _, array, start in a], None, "rows_a")
        slots = product(
            chips * 2 + 1 - core, 0, 2, [[(array, start, rows_dev)] for _, array, start in b], total, "rows_b", last=(image_q, slot, factor)
        )
    got = lax.all_to_all(slots, "section", split_axis=0, concat_axis=0, tiled=True)

    return pl.pallas_call(
        combine_kernel,
        grid=(1,),
        in_specs=[
            whole((n, 3, HALF_QH, HD)),
            whole((decode_rows, QH, HD)),
            whole((QH, HD)),
            whole((QH, HD)),
        ],
        out_specs=whole((decode_rows, QH * HD)),
        scratch_shapes=[pltpu.VMEM((decode_rows, QH, HD), jnp.float32)],
        out_shape=jax.ShapeDtypeStruct((decode_rows, QH * HD), jnp.bfloat16),
        compiler_params=pltpu.CompilerParams(vmem_limit_bytes=60 * 2**20),
        name="combine",
    )(got, res_out, res_top, res_sum)


def solution(mesh):
    placed = (
        P(("replica", "section"), None),
        P("section", None),
        P(("replica", "section")),
        P(("replica", "section")),
        P(("replica", "section"), None),
        P(("replica", "section"), None, None),
        P(("replica", "section")),
    )
    return jax.shard_map(
        per_device,
        mesh=mesh,
        in_specs=placed,
        out_specs=P(("replica", "section"), None),
        check_vma=False,
    )
```

```python
import functools
import math

import jax
import jax.numpy as jnp
import numpy as np
from jax import lax
from jax.experimental import pallas as pl
from jax.experimental.pallas import tpu as pltpu
from jax.sharding import PartitionSpec as P

HD = 128
KVH = 4
QH = 32
IMG_TOK = 64
GROUP = QH // KVH
HALF_KVH = KVH // 2
HALF_QH = QH // 2
SCALE = 1.0 / math.sqrt(HD)
EPS = 1e-05

LANES = 64
N_KINDS = 7

masked_score = -1e30


def swap_core(x):
    n = lax.axis_size("section")
    return lax.ppermute(x, "section", [(i, i ^ 1) for i in range(n)])


def gather_plain(chunk):
    n = lax.axis_size("section")
    rows = chunk.shape[0]
    groups = [list(range(core, n, 2)) for core in range(2)]
    whole = lax.all_gather(chunk, "section", axis=0, tiled=True, axis_index_groups=groups)
    return [(chip, whole, chip * rows) for chip in range(n // 2)]


RING = [0, 1, 3, 2]


def along_ring(x, sign=1):
    perm = []
    for rep, way in ((0, sign), (1, -sign)):
        for p in range(4):
            for low in range(4):
                perm.append((rep * 16 + RING[p] * 4 + low, rep * 16 + RING[(p + way) % 4] * 4 + low))
    return lax.ppermute(x, ("replica", "section"), perm)


def across_y(x):
    return lax.ppermute(x, "section", [(i, i ^ 2) for i in range(16)])


def across_replica(x):
    return lax.ppermute(x, "replica", [(0, 1), (1, 0)])


STEPS = (("own", "behind", "own_y"), ("ahead", "opposite", "behind_y"), ("ahead_y", "opposite_y"))


def block_table():
    table = []
    for rep in range(2):
        for section in range(16):
            z, y, core = section // 4, section // 2 % 2, section % 2
            way = 1 - 2 * rep
            place = RING.index(z)
            ring = {"own": place, "behind": place - way, "ahead": place + way, "opposite": place + 2}

            def blocks(step, other):
                out = []
                for name in STEPS[step]:
                    chip = RING[ring[name.removesuffix("_y")] % 4] * 2 + (1 - y if name.endswith("_y") else y)
                    out.append(chip * 2 + (core ^ other))
                return out

            def both(step):
                return [block for pair in zip(blocks(step, 0), blocks(step, 1)) for block in pair]

            three = both(2)
            places = [0] * 8
            for i, name in enumerate(("own", "behind", "ahead", "opposite")):
                chip = RING[ring[name] % 4] * 2
                places[chip + y], places[chip + 1 - y] = i, 4 + i
            table.append(both(0) + both(1) + [three[0], three[2], three[3], three[1]] + places)
    return np.array(table, np.int32)


def square_kernel(states_ref, out_ref):
    total = None
    for i in range(0, states_ref.shape[1], HD):
        values = states_ref[:, i : i + HD].astype(jnp.float32)
        values = values * values
        total = values if total is None else total + values
    out_ref[...] = jnp.sum(total, axis=1, keepdims=True)


def split_kernel(core_ref, keep_in, give_in, keep_ref, give_ref):
    keep_ref[...] = keep_in[...]
    give_ref[...] = give_in[...]


def accumulate(layout, token_refs, piece_refs, weight, total, sems, carry_ref=None, carry=None):
    step = pl.program_id(0)
    rows = token_refs[0].shape[1]
    count = len(token_refs) // 2
    depth = count * rows
    copies = [
        pltpu.make_async_copy(
            piece_refs[which].at[pl.ds(start, size)], weight.at[pl.ds(place, size)], sems.at[i]
        )
        for i, (which, start, size, place) in enumerate(layout)
    ]
    carried = []
    if carry_ref is not None:
        carried = [pltpu.make_async_copy(carry_ref, carry, sems.at[len(layout)])]

    @pl.when(step == 0)
    def _():
        for copy in copies + carried:
            copy.start()

    for i in range(weight.shape[0] // depth):

        @pl.when(step == i)
        def _():
            for copy, (_, _, _, place) in zip(copies, layout):
                if place // depth == i:
                    copy.wait()

    states = jnp.concatenate(
        [
            jnp.concatenate([ref[...] for ref in token_refs[side * count : (side + 1) * count]], axis=1)
            for side in range(2)
        ],
        axis=0,
    )
    block = weight[pl.ds(pl.multiple_of(step * depth, depth), depth), :]
    product = jnp.dot(states, block, preferred_element_type=jnp.float32)

    @pl.when(step == 0)
    def _():
        total[...] = product

    @pl.when(step > 0)
    def _():
        total[...] += product

    if carry_ref is not None:

        @pl.when(step == pl.num_programs(0) - 1)
        def _():
            carried[0].wait()
            total[...] += carry[...]


def first_kernel(layout, count, block_ref, *refs):
    total, weight, sems = refs[-3:]
    accumulate(layout, refs[: 2 * count], refs[2 * count : -3], weight, total, sems)


def next_kernel(layout, count, block_ref, *refs):
    total, weight, carry, sems = refs[-4:]
    token_refs, (carry_ref, *piece_refs) = refs[: 2 * count], refs[2 * count : -4]
    accumulate(layout, token_refs, piece_refs, weight, total, sems, carry_ref, carry)


def parts_of(values, count):
    out = []
    for _ in range(count):
        part = values.astype(jnp.bfloat16).astype(jnp.float32)
        out.append(part)
        values = values - part
    return out


def last_kernel(layout, count, width, block_ref, slot_ref, *refs):
    token_refs, (carry_ref, query_ref, factor_ref, *piece_refs) = refs[: 2 * count], refs[2 * count : -7]
    slots_ref, weight, carry, total, summed, stats, sems = refs[-7:]
    images = query_ref.shape[1] // GROUP

    @pl.when(pl.program_id(0) == 0)
    def _():
        slots_ref[...] = jnp.zeros_like(slots_ref)

    accumulate(layout, token_refs, piece_refs, weight, total, sems, carry_ref, carry)

    @pl.when(pl.program_id(0) == pl.num_programs(0) - 1)
    def _():
        tokens = total.shape[0]
        queries = query_ref.shape[1]
        factor = lax.rsqrt(factor_ref[...] / width + EPS)
        image_of_query = lax.broadcasted_iota(jnp.int32, (queries, tokens), 0) // GROUP
        image_of_token = lax.broadcasted_iota(jnp.int32, (queries, tokens), 1) // IMG_TOK
        live = image_of_query == image_of_token
        lane = lax.broadcasted_iota(jnp.int32, (queries, HD), 1)
        for head in range(HALF_KVH):
            part = slice(head * GROUP, (head + 1) * GROUP)
            keys = (total[:, head * HD : (head + 1) * HD] * factor).astype(jnp.bfloat16)
            at = (HALF_KVH + head) * HD
            values = (total[:, at : at + HD] * factor).astype(jnp.bfloat16)
            scores = (
                lax.dot_general(
                    query_ref[head], keys, (((1,), (1,)), ((), ())), preferred_element_type=jnp.float32
                )
                * SCALE
            )
            scores = jnp.where(live, scores, masked_score)
            top = jnp.max(scores, axis=1, keepdims=True)
            weights = jnp.where(live, jnp.exp(scores - top), 0.0)
            total_weight = jnp.sum(weights, axis=1, keepdims=True)
            out = jnp.dot(weights.astype(jnp.bfloat16), values, preferred_element_type=jnp.float32)
            summed[:, part, :] = out.reshape(images, GROUP, HD)
            kinds = parts_of(top, 3) + parts_of(total_weight, 3) + [jnp.ones_like(top)]
            tile = jnp.zeros((queries, HD), jnp.float32)
            for kind, column in enumerate(kinds):
                tile = jnp.where(lane == kind * 8, column, tile)
            stats[:, part, :] = tile.reshape(images, GROUP, HD)
        for image in range(images):
            owner, which = slot_ref[0, image], slot_ref[1, image]
            slots_ref[owner, which] = summed[image].astype(jnp.bfloat16)
            tile = pltpu.roll(stats[image], which * LANES + slot_ref[2, image], 1)
            slots_ref[owner, 2] = slots_ref[owner, 2] + tile.astype(jnp.bfloat16)


def resident_kernel(length_ref, query_ref, cache_ref, out_ref, top_ref, sum_ref):
    step = pl.program_id(0)
    rows, context = cache_ref.shape[:2]
    place = lax.broadcasted_iota(jnp.int32, (QH, context), 1)
    lane = lax.broadcasted_iota(jnp.int32, (QH, HD), 1)

    @pl.when(step == 0)
    def _():
        top_ref[...] = jnp.zeros_like(top_ref)
        sum_ref[...] = jnp.zeros_like(sum_ref)

    parts = [slice(head * GROUP, (head + 1) * GROUP) for head in range(KVH)]
    scores = [
        jnp.concatenate(
            [
                lax.dot_general(
                    query_ref[row, part, :],
                    cache_ref[row, :, head * HD : (head + 1) * HD],
                    (((1,), (1,)), ((), ())),
                    preferred_element_type=jnp.float32,
                )
                for head, part in enumerate(parts)
            ],
            axis=0,
        )
        for row in range(rows)
    ]
    for row in range(rows):
        live = place < length_ref[step * rows + row]
        score = jnp.where(live, scores[row] * SCALE, masked_score)
        top = jnp.max(score, axis=1, keepdims=True)
        weights = jnp.where(live, jnp.exp(score - top), 0.0)
        mine = lane == step * rows + row
        top_ref[...] = jnp.where(mine, top, top_ref[...])
        sum_ref[...] = jnp.where(mine, jnp.sum(weights, axis=1, keepdims=True), sum_ref[...])
        weights = weights.astype(jnp.bfloat16)
        for head, part in enumerate(parts):
            at = (KVH + head) * HD
            out_ref[row, part, :] = jnp.dot(
                weights[part], cache_ref[row, :, at : at + HD], preferred_element_type=jnp.float32
            )


def combine_kernel(got_ref, res_out_ref, res_top_ref, res_sum_ref, out_ref, acc):
    chips = got_ref.shape[0] // 2
    rows = res_out_ref.shape[0]
    lane = lax.broadcasted_iota(jnp.int32, (HALF_QH, HD), 1)
    head_lane = (lane % LANES) < 8

    def moved(tile, by):
        return pltpu.roll(tile, HD - by, 1)

    for core in range(2):
        part = slice(core * HALF_QH, (core + 1) * HALF_QH)
        tops, sums, here = [], [], []
        for chip in range(chips):
            tile = got_ref[chip * 2 + core, 2].astype(jnp.float32)
            present = (moved(tile, 48) > 0.5) & head_lane
            tops.append(jnp.where(present, tile + moved(tile, 8) + moved(tile, 16), masked_score))
            sums.append(moved(tile, 24) + moved(tile, 32) + moved(tile, 40))
            here.append(present)
        row_top = functools.reduce(jnp.maximum, tops)
        row_top = jnp.maximum(row_top, pltpu.roll(row_top, LANES, 1))
        res_top = jnp.where(lane < 8, res_top_ref[part, :], masked_score)
        res_top = jnp.maximum(res_top, pltpu.roll(res_top, LANES, 1))
        row_top = jnp.maximum(row_top, res_top)
        weights = [jnp.where(a, jnp.exp(t - row_top), 0.0) for a, t in zip(here, tops)]
        joined = sum(w * s for w, s in zip(weights, sums))
        res_weight = jnp.exp(res_top - row_top)
        denominator = joined + pltpu.roll(joined, LANES, 1) + res_weight * res_sum_ref[part, :]
        scale = jnp.where(lane < 8, 1.0 / denominator, 0.0)
        scale = scale + pltpu.roll(scale, LANES, 1)
        res_share = res_weight * scale
        weights = [w * scale for w in weights]
        for row in range(rows):
            value = res_out_ref[row, part, :] * res_share[:, row : row + 1]
            for chip in range(chips):
                for which in range(2):
                    at = which * LANES + row
                    value += weights[chip][:, at : at + 1] * got_ref[chip * 2 + core, which].astype(jnp.float32)
            acc[row, part, :] = value
    for head in range(QH):
        out_ref[:, head * HD : (head + 1) * HD] = acc[:, head, :].astype(jnp.bfloat16)


def whole(shape):
    return pl.BlockSpec(shape, lambda i, *_: (0,) * len(shape))


def per_device(prompt_states, kv_weight, image_owner, image_row, queries, cache, context_length):
    n = lax.axis_size("section")
    section = lax.axis_index("section")
    core = section % 2
    tokens, width = prompt_states.shape
    rows_dev, kv_width = kv_weight.shape
    columns_dev = kv_width // 2
    images = image_owner.shape[0]
    decode_rows = queries.shape[0]
    context = cache.shape[1]
    n_queries = 2 * images * GROUP

    cut = columns_dev // 2
    keep, give = pl.pallas_call(
        split_kernel,
        grid_spec=pltpu.PrefetchScalarGridSpec(
            num_scalar_prefetch=1,
            grid=(2,),
            in_specs=[
                pl.BlockSpec((rows_dev, cut), lambda i, core_ref: (0, 2 * i + core_ref[0])),
                pl.BlockSpec((rows_dev, cut), lambda i, core_ref: (0, 2 * i + 1 - core_ref[0])),
            ],
            out_specs=[pl.BlockSpec((rows_dev, cut), lambda i, core_ref: (0, i))] * 2,
        ),
        out_shape=[jax.ShapeDtypeStruct((rows_dev, columns_dev), jnp.bfloat16)] * 2,
        cost_estimate=pl.CostEstimate(flops=0, bytes_accessed=2**18, transcendentals=0),
        name="split",
    )(core.reshape(1), kv_weight, kv_weight)
    taken = swap_core(give)
    def swap_tokens(tied):
        return swap_core(lax.optimization_barrier((prompt_states, tied))[0])

    def square_sums(tied):
        states, _ = lax.optimization_barrier((prompt_states, tied))
        return pl.pallas_call(
            square_kernel,
            grid=(8,),
            in_specs=[pl.BlockSpec((tokens // 8, width), lambda i: (i, 0))],
            out_specs=pl.BlockSpec((tokens // 8, 1), lambda i: (i, 0)),
            out_shape=jax.ShapeDtypeStruct((tokens, 1), jnp.float32),
            cost_estimate=pl.CostEstimate(flops=0, bytes_accessed=2**18, transcendentals=0),
            compiler_params=pltpu.CompilerParams(vmem_limit_bytes=60 * 2**20),
            name="squares",
        )(pltpu.with_memory_space_constraint(states, pltpu.HBM))[:, 0]

    def swap_small(squares):
        places = jnp.concatenate([image_owner, image_row]).astype(jnp.float32)
        small = jnp.concatenate([squares, places])
        small = jnp.pad(small, (0, -small.shape[0] % (8 * HD))).reshape(-1, HD)
        got = swap_core(small).reshape(-1)
        factor = jnp.concatenate([squares, got[:tokens]])[:, None]
        at = tokens + images
        owners = jnp.concatenate([image_owner, got[tokens:at].astype(jnp.int32)])
        rows = jnp.concatenate([image_row, got[at : at + images].astype(jnp.int32)])
        return factor, owners, rows

    query_halves = queries.reshape(decode_rows, 2, HALF_QH * HD)
    keep_q = jnp.where(core == 0, query_halves[:, 0], query_halves[:, 1])
    give_q = jnp.where(core == 0, query_halves[:, 1], query_halves[:, 0])

    def place_images(all_q, owners, rows, chip_place):
        chip_of = jnp.sum(
            jnp.where(owners[:, None] // 2 == jnp.arange(n // 2)[None, :], chip_place[None, :], 0), axis=1
        )
        target = chip_of * (2 * decode_rows) + (owners % 2 ^ core) * decode_rows + rows
        pick = (target[:, None] == jnp.arange(n * decode_rows)[None, :]).astype(jnp.bfloat16)
        image_q = jnp.dot(pick, all_q, preferred_element_type=jnp.float32).astype(jnp.bfloat16)
        image_q = image_q.reshape(2 * images, HALF_KVH, GROUP, HD).transpose(1, 0, 2, 3)
        which = jnp.concatenate([jnp.full((images,), core), jnp.full((images,), 1 - core)]).astype(jnp.int32)
        return image_q.reshape(HALF_KVH, n_queries, HD), jnp.stack([owners, which, rows])

    def resident(length):
        step_rows = 2
        return pl.pallas_call(
            resident_kernel,
            grid_spec=pltpu.PrefetchScalarGridSpec(
                num_scalar_prefetch=1,
                grid=(decode_rows // step_rows,),
                in_specs=[
                    pl.BlockSpec((step_rows, QH, HD), lambda i, *_: (i, 0, 0)),
                    pl.BlockSpec((step_rows, context, kv_width), lambda i, *_: (i, 0, 0)),
                ],
                out_specs=[
                    pl.BlockSpec((step_rows, QH, HD), lambda i, *_: (i, 0, 0)),
                    whole((QH, HD)),
                    whole((QH, HD)),
                ],
            ),
            out_shape=[
                jax.ShapeDtypeStruct((decode_rows, QH, HD), jnp.float32),
                jax.ShapeDtypeStruct((QH, HD), jnp.float32),
                jax.ShapeDtypeStruct((QH, HD), jnp.float32),
            ],
            compiler_params=pltpu.CompilerParams(vmem_limit_bytes=60 * 2**20),
            cost_estimate=pl.CostEstimate(flops=0, bytes_accessed=2**18, transcendentals=0),
            name="resident",
        )(length, queries.reshape(decode_rows, QH, HD), cache)

    def product(other, blocks, base, count, pieces, carry, name, last=None):
        arrays, layout = [], []
        for index, piece in enumerate(pieces):
            place = index * rows_dev
            for array, start, rows in piece:
                at = [i for i, known in enumerate(arrays) if known is array]
                if not at:
                    arrays.append(array)
                    at = [len(arrays) - 1]
                layout.append((at[0], start, rows, place))
                place += rows
        steps = len(pieces) // count

        def token_spec(k):
            return pl.BlockSpec((tokens, rows_dev), lambda i, block_ref, *_: (0, block_ref[base + count * i + k]))

        anywhere = pl.BlockSpec(memory_space=pl.ANY)
        in_specs = [token_spec(k) for k in range(count)] * 2
        own_tokens = pltpu.with_memory_space_constraint(prompt_states, pltpu.HBM)
        other_tokens = pltpu.with_memory_space_constraint(other, pltpu.HBM)
        inputs = [own_tokens] * count + [other_tokens] * count
        scalars = [blocks]
        scratch = [pltpu.VMEM((len(pieces) * rows_dev, columns_dev), jnp.bfloat16)]
        total = (2 * tokens, columns_dev)
        body = functools.partial(first_kernel, layout, count)
        if carry is not None:
            body = functools.partial(next_kernel, layout, count)
            in_specs = in_specs + [anywhere]
            inputs = inputs + [carry]
            scratch = scratch + [pltpu.VMEM(total, jnp.float32)]
        out_specs, out_shape = whole(total), jax.ShapeDtypeStruct(total, jnp.float32)
        if last is not None:
            image_q, slot, factor = last
            body = functools.partial(last_kernel, layout, count, width)
            scalars = scalars + [slot]
            in_specs = in_specs + [whole((HALF_KVH, n_queries, HD)), whole((2 * tokens, 1))]
            inputs = inputs + [image_q, factor]
            out_specs = whole((n, 3, HALF_QH, HD))
            out_shape = jax.ShapeDtypeStruct((n, 3, HALF_QH, HD), jnp.bfloat16)
            scratch = scratch + [
                pltpu.VMEM(total, jnp.float32),
                pltpu.VMEM((2 * images, HALF_QH, HD), jnp.float32),
                pltpu.VMEM((2 * images, HALF_QH, HD), jnp.float32),
            ]
        return pl.pallas_call(
            body,
            grid_spec=pltpu.PrefetchScalarGridSpec(
                num_scalar_prefetch=len(scalars),
                grid=(steps,),
                in_specs=in_specs + [anywhere] * len(arrays),
                out_specs=out_specs,
                scratch_shapes=scratch + [pltpu.SemaphoreType.DMA((len(layout) + 1,))],
            ),
            out_shape=out_shape,
            compiler_params=pltpu.CompilerParams(vmem_limit_bytes=60 * 2**20),
            cost_estimate=pl.CostEstimate(flops=0, bytes_accessed=2**18, transcendentals=0),
            name=name,
        )(*scalars, *inputs, *arrays)

    if n == 16 and lax.axis_size("replica") == 2:
        table = block_table()
        blocks = jnp.array(table)[lax.axis_index("replica") * 16 + section]

        def starts(*arrays):
            return [[(array, 0, rows_dev)] for array in arrays]

        tie = lax.optimization_barrier

        def both(array):
            return [[(array, half, rows_dev)] for half in (0, rows_dev)]

        own_q = jnp.concatenate([keep_q, swap_core(give_q)], axis=0)
        behind_q, ahead_q, opposite_q = (along_ring(own_q, way) for way in (1, -1, 2))
        ring_q = jnp.concatenate([own_q, behind_q, ahead_q, opposite_q], axis=0)
        a_own_y = across_y(keep)
        source_a, source_b, source_q = tie((keep, taken, ring_q))
        a_behind = along_ring(source_a)
        b_behind, b_own_y = along_ring(source_b), across_y(source_b)
        other = swap_tokens((taken, source_q))
        squares = square_sums(taken)

        source, squares, _ = tie((a_behind, squares, a_own_y))
        a_ahead, a_opposite, a_behind_y = across_replica(source), along_ring(source), across_y(source)
        source, squares, _ = tie((b_behind, squares, (b_own_y, a_ahead)))
        b_ahead, b_opposite, b_behind_y = across_replica(source), along_ring(source), across_y(source)
        ones = starts(keep, taken, a_behind, b_behind, a_own_y, b_own_y)
        total = product(other, blocks, 0, 2, ones, None, "rows_1")

        source_y, source, source_q, squares, total, _ = tie(
            (a_behind_y, a_opposite, ring_q, squares, total, b_ahead)
        )
        a_ahead_y, a_opposite_y = across_replica(source_y), across_y(source)
        all_q = jnp.concatenate([ring_q, across_y(source_q)], axis=0)
        source, squares, total, _ = tie((b_behind_y, squares, total, (b_opposite, a_ahead_y)))
        b_ahead_y, b_opposite_y = across_replica(source), along_ring(source)
        factor, owners, rows = swap_small(squares)
        image_q, slot = place_images(all_q, owners, rows, blocks[16:])
        twos = starts(a_ahead, b_ahead, a_opposite, b_opposite, a_behind_y, b_behind_y)
        total = product(other, blocks, 6, 2, twos, total, "rows_2")
        lasts = starts(a_ahead_y, a_opposite_y, b_opposite_y, b_ahead_y)
        slots = product(other, blocks, 12, 2, lasts, total, "rows_3", last=(image_q, slot, factor))
        length, slots = tie((context_length, slots))
        res_out, res_top, res_sum = resident(length)
    else:
        res_out, res_top, res_sum = resident(context_length)
        other = swap_tokens(taken)
        squares = square_sums(taken)
        factor, owners, rows = swap_small(squares)
        chip_q = jnp.concatenate([keep_q, swap_core(give_q)], axis=0)
        groups = [list(range(side, n, 2)) for side in range(2)]
        all_q = lax.all_gather(chip_q, "section", axis=0, tiled=True, axis_index_groups=groups)
        image_q, slot = place_images(all_q, owners, rows, jnp.arange(n // 2))
        a = gather_plain(keep)
        b = gather_plain(taken)
        chips = jnp.array([chip for chip, _, _ in a], jnp.int32)
        total = product(other, chips * 2 + core, 0, 2, [[(array, start, rows_dev)] for _, array, start in a], None, "rows_a")
        slots = product(
            other, chips * 2 + 1 - core, 0, 2, [[(array, start, rows_dev)] for _, array, start in b], total, "rows_b", last=(image_q, slot, factor)
        )
    got = lax.all_to_all(slots, "section", split_axis=0, concat_axis=0, tiled=True)

    return pl.pallas_call(
        combine_kernel,
        grid=(1,),
        in_specs=[
            whole((n, 3, HALF_QH, HD)),
            whole((decode_rows, QH, HD)),
            whole((QH, HD)),
            whole((QH, HD)),
        ],
        out_specs=whole((decode_rows, QH * HD)),
        scratch_shapes=[pltpu.VMEM((decode_rows, QH, HD), jnp.float32)],
        out_shape=jax.ShapeDtypeStruct((decode_rows, QH * HD), jnp.bfloat16),
        compiler_params=pltpu.CompilerParams(vmem_limit_bytes=60 * 2**20),
        name="combine",
    )(got, res_out, res_top, res_sum)


def solution(mesh):
    placed = (
        P(("replica", "section"), None),
        P("section", None),
        P(("replica", "section")),
        P(("replica", "section")),
        P(("replica", "section"), None),
        P(("replica", "section"), None, None),
        P(("replica", "section")),
    )
    return jax.shard_map(
        per_device,
        mesh=mesh,
        in_specs=placed,
        out_specs=P(("replica", "section"), None),
        check_vma=False,
    )
```

```python
import functools
import math

import jax
import jax.numpy as jnp
import numpy as np
from jax import lax
from jax.experimental import pallas as pl
from jax.experimental.pallas import tpu as pltpu
from jax.sharding import PartitionSpec as P

HD = 128
KVH = 4
QH = 32
IMG_TOK = 64
GROUP = QH // KVH
HALF_KVH = KVH // 2
HALF_QH = QH // 2
SCALE = 1.0 / math.sqrt(HD)
EPS = 1e-05

LANES = 64
N_KINDS = 7

masked_score = -1e30


def swap_core(x):
    n = lax.axis_size("section")
    return lax.ppermute(x, "section", [(i, i ^ 1) for i in range(n)])


def gather_plain(chunk):
    n = lax.axis_size("section")
    rows = chunk.shape[0]
    groups = [list(range(core, n, 2)) for core in range(2)]
    whole = lax.all_gather(chunk, "section", axis=0, tiled=True, axis_index_groups=groups)
    return [(chip, whole, chip * rows) for chip in range(n // 2)]


RING = [0, 1, 3, 2]


def along_ring(x, sign=1):
    perm = []
    for rep, way in ((0, sign), (1, -sign)):
        for p in range(4):
            for low in range(4):
                perm.append((rep * 16 + RING[p] * 4 + low, rep * 16 + RING[(p + way) % 4] * 4 + low))
    return lax.ppermute(x, ("replica", "section"), perm)


def across_y(x):
    return lax.ppermute(x, "section", [(i, i ^ 2) for i in range(16)])


def across_replica(x):
    return lax.ppermute(x, "replica", [(0, 1), (1, 0)])


STEPS = (("own", "behind", "own_y"), ("ahead", "opposite", "behind_y"), ("ahead_y", "opposite_y"))


def block_table():
    table = []
    for rep in range(2):
        for section in range(16):
            z, y, core = section // 4, section // 2 % 2, section % 2
            way = 1 - 2 * rep
            place = RING.index(z)
            ring = {"own": place, "behind": place - way, "ahead": place + way, "opposite": place + 2}

            def blocks(step, other):
                out = []
                for name in STEPS[step]:
                    chip = RING[ring[name.removesuffix("_y")] % 4] * 2 + (1 - y if name.endswith("_y") else y)
                    out.append(chip * 2 + (core ^ other))
                return out

            def both(step):
                return [block for pair in zip(blocks(step, 0), blocks(step, 1)) for block in pair]

            three = both(2)
            places = [0] * 8
            for i, name in enumerate(("own", "behind", "ahead", "opposite")):
                chip = RING[ring[name] % 4] * 2
                places[chip + y], places[chip + 1 - y] = i, 4 + i
            table.append(both(0) + both(1) + [three[0], three[2], three[3], three[1]] + places)
    return np.array(table, np.int32)


def square_kernel(states_ref, out_ref):
    total = None
    for i in range(0, states_ref.shape[1], HD):
        values = states_ref[:, i : i + HD].astype(jnp.float32)
        values = values * values
        total = values if total is None else total + values
    out_ref[...] = jnp.sum(total, axis=1, keepdims=True)


def split_kernel(core_ref, keep_in, give_in, keep_ref, give_ref):
    keep_ref[...] = keep_in[...]
    give_ref[...] = give_in[...]


def accumulate(layout, token_refs, piece_refs, weight, total, sems, carry_ref=None, carry=None):
    step = pl.program_id(0)
    rows = token_refs[0].shape[1]
    count = len(token_refs) // 2
    depth = count * rows
    copies = [
        pltpu.make_async_copy(
            piece_refs[which].at[pl.ds(start, size)], weight.at[pl.ds(place, size)], sems.at[i]
        )
        for i, (which, start, size, place) in enumerate(layout)
    ]
    carried = []
    if carry_ref is not None:
        carried = [pltpu.make_async_copy(carry_ref, carry, sems.at[len(layout)])]

    @pl.when(step == 0)
    def _():
        for copy in copies + carried:
            copy.start()

    for i in range(weight.shape[0] // depth):

        @pl.when(step == i)
        def _():
            for copy, (_, _, _, place) in zip(copies, layout):
                if place // depth == i:
                    copy.wait()

    states = jnp.concatenate(
        [
            jnp.concatenate([ref[...] for ref in token_refs[side * count : (side + 1) * count]], axis=1)
            for side in range(2)
        ],
        axis=0,
    )
    block = weight[pl.ds(pl.multiple_of(step * depth, depth), depth), :]
    product = jnp.dot(states, block, preferred_element_type=jnp.float32)

    @pl.when(step == 0)
    def _():
        total[...] = product

    @pl.when(step > 0)
    def _():
        total[...] += product

    if carry_ref is not None:

        @pl.when(step == pl.num_programs(0) - 1)
        def _():
            carried[0].wait()
            total[...] += carry[...]


def first_kernel(layout, count, block_ref, *refs):
    total, weight, sems = refs[-3:]
    accumulate(layout, refs[: 2 * count], refs[2 * count : -3], weight, total, sems)


def next_kernel(layout, count, block_ref, *refs):
    total, weight, carry, sems = refs[-4:]
    token_refs, (carry_ref, *piece_refs) = refs[: 2 * count], refs[2 * count : -4]
    accumulate(layout, token_refs, piece_refs, weight, total, sems, carry_ref, carry)


def parts_of(values, count):
    out = []
    for _ in range(count):
        part = values.astype(jnp.bfloat16).astype(jnp.float32)
        out.append(part)
        values = values - part
    return out


def last_kernel(layout, count, width, block_ref, slot_ref, *refs):
    token_refs, (carry_ref, query_ref, factor_ref, *piece_refs) = refs[: 2 * count], refs[2 * count : -7]
    slots_ref, weight, carry, total, summed, stats, sems = refs[-7:]
    images = query_ref.shape[1] // GROUP

    @pl.when(pl.program_id(0) == 0)
    def _():
        slots_ref[...] = jnp.zeros_like(slots_ref)

    accumulate(layout, token_refs, piece_refs, weight, total, sems, carry_ref, carry)

    @pl.when(pl.program_id(0) == pl.num_programs(0) - 1)
    def _():
        tokens = total.shape[0]
        queries = query_ref.shape[1]
        factor = lax.rsqrt(factor_ref[...] / width + EPS)
        image_of_query = lax.broadcasted_iota(jnp.int32, (queries, tokens), 0) // GROUP
        image_of_token = lax.broadcasted_iota(jnp.int32, (queries, tokens), 1) // IMG_TOK
        live = image_of_query == image_of_token
        lane = lax.broadcasted_iota(jnp.int32, (queries, HD), 1)
        for head in range(HALF_KVH):
            part = slice(head * GROUP, (head + 1) * GROUP)
            keys = (total[:, head * HD : (head + 1) * HD] * factor).astype(jnp.bfloat16)
            at = (HALF_KVH + head) * HD
            values = (total[:, at : at + HD] * factor).astype(jnp.bfloat16)
            scores = (
                lax.dot_general(
                    query_ref[head], keys, (((1,), (1,)), ((), ())), preferred_element_type=jnp.float32
                )
                * SCALE
            )
            scores = jnp.where(live, scores, masked_score)
            top = jnp.max(scores, axis=1, keepdims=True)
            weights = jnp.where(live, jnp.exp(scores - top), 0.0)
            total_weight = jnp.sum(weights, axis=1, keepdims=True)
            out = jnp.dot(weights.astype(jnp.bfloat16), values, preferred_element_type=jnp.float32)
            summed[:, part, :] = out.reshape(images, GROUP, HD)
            kinds = parts_of(top, 3) + parts_of(total_weight, 3) + [jnp.ones_like(top)]
            tile = jnp.zeros((queries, HD), jnp.float32)
            for kind, column in enumerate(kinds):
                tile = jnp.where(lane == kind * 8, column, tile)
            stats[:, part, :] = tile.reshape(images, GROUP, HD)
        for image in range(images):
            owner, which = slot_ref[0, image], slot_ref[1, image]
            slots_ref[owner, which] = summed[image].astype(jnp.bfloat16)
            tile = pltpu.roll(stats[image], which * LANES + slot_ref[2, image], 1)
            slots_ref[owner, 2] = slots_ref[owner, 2] + tile.astype(jnp.bfloat16)


def resident_kernel(length_ref, query_ref, cache_ref, out_ref, top_ref, sum_ref):
    step = pl.program_id(0)
    rows, context = cache_ref.shape[:2]
    place = lax.broadcasted_iota(jnp.int32, (QH, context), 1)
    lane = lax.broadcasted_iota(jnp.int32, (QH, HD), 1)

    @pl.when(step == 0)
    def _():
        top_ref[...] = jnp.zeros_like(top_ref)
        sum_ref[...] = jnp.zeros_like(sum_ref)

    parts = [slice(head * GROUP, (head + 1) * GROUP) for head in range(KVH)]
    scores = [
        jnp.concatenate(
            [
                lax.dot_general(
                    query_ref[row, part, :],
                    cache_ref[row, :, head * HD : (head + 1) * HD],
                    (((1,), (1,)), ((), ())),
                    preferred_element_type=jnp.float32,
                )
                for head, part in enumerate(parts)
            ],
            axis=0,
        )
        for row in range(rows)
    ]
    for row in range(rows):
        live = place < length_ref[step * rows + row]
        score = jnp.where(live, scores[row] * SCALE, masked_score)
        top = jnp.max(score, axis=1, keepdims=True)
        weights = jnp.where(live, jnp.exp(score - top), 0.0)
        mine = lane == step * rows + row
        top_ref[...] = jnp.where(mine, top, top_ref[...])
        sum_ref[...] = jnp.where(mine, jnp.sum(weights, axis=1, keepdims=True), sum_ref[...])
        weights = weights.astype(jnp.bfloat16)
        for head, part in enumerate(parts):
            at = (KVH + head) * HD
            out_ref[row, part, :] = jnp.dot(
                weights[part], cache_ref[row, :, at : at + HD], preferred_element_type=jnp.float32
            )


def combine_kernel(got_ref, res_out_ref, res_top_ref, res_sum_ref, out_ref, acc):
    chips = got_ref.shape[0] // 2
    rows = res_out_ref.shape[0]
    lane = lax.broadcasted_iota(jnp.int32, (HALF_QH, HD), 1)
    head_lane = (lane % LANES) < 8

    def moved(tile, by):
        return pltpu.roll(tile, HD - by, 1)

    for core in range(2):
        part = slice(core * HALF_QH, (core + 1) * HALF_QH)
        tops, sums, here = [], [], []
        for chip in range(chips):
            tile = got_ref[chip * 2 + core, 2].astype(jnp.float32)
            present = (moved(tile, 48) > 0.5) & head_lane
            tops.append(jnp.where(present, tile + moved(tile, 8) + moved(tile, 16), masked_score))
            sums.append(moved(tile, 24) + moved(tile, 32) + moved(tile, 40))
            here.append(present)
        row_top = functools.reduce(jnp.maximum, tops)
        row_top = jnp.maximum(row_top, pltpu.roll(row_top, LANES, 1))
        res_top = jnp.where(lane < 8, res_top_ref[part, :], masked_score)
        res_top = jnp.maximum(res_top, pltpu.roll(res_top, LANES, 1))
        row_top = jnp.maximum(row_top, res_top)
        weights = [jnp.where(a, jnp.exp(t - row_top), 0.0) for a, t in zip(here, tops)]
        joined = sum(w * s for w, s in zip(weights, sums))
        res_weight = jnp.exp(res_top - row_top)
        denominator = joined + pltpu.roll(joined, LANES, 1) + res_weight * res_sum_ref[part, :]
        scale = jnp.where(lane < 8, 1.0 / denominator, 0.0)
        scale = scale + pltpu.roll(scale, LANES, 1)
        res_share = res_weight * scale
        weights = [w * scale for w in weights]
        for row in range(rows):
            value = res_out_ref[row, part, :] * res_share[:, row : row + 1]
            for chip in range(chips):
                for which in range(2):
                    at = which * LANES + row
                    value += weights[chip][:, at : at + 1] * got_ref[chip * 2 + core, which].astype(jnp.float32)
            acc[row, part, :] = value
    for head in range(QH):
        out_ref[:, head * HD : (head + 1) * HD] = acc[:, head, :].astype(jnp.bfloat16)


def whole(shape):
    return pl.BlockSpec(shape, lambda i, *_: (0,) * len(shape))


def per_device(prompt_states, kv_weight, image_owner, image_row, queries, cache, context_length):
    n = lax.axis_size("section")
    section = lax.axis_index("section")
    core = section % 2
    tokens, width = prompt_states.shape
    rows_dev, kv_width = kv_weight.shape
    columns_dev = kv_width // 2
    images = image_owner.shape[0]
    decode_rows = queries.shape[0]
    context = cache.shape[1]
    n_queries = 2 * images * GROUP

    cut = columns_dev // 2
    keep, give = pl.pallas_call(
        split_kernel,
        grid_spec=pltpu.PrefetchScalarGridSpec(
            num_scalar_prefetch=1,
            grid=(2,),
            in_specs=[
                pl.BlockSpec((rows_dev, cut), lambda i, core_ref: (0, 2 * i + core_ref[0])),
                pl.BlockSpec((rows_dev, cut), lambda i, core_ref: (0, 2 * i + 1 - core_ref[0])),
            ],
            out_specs=[pl.BlockSpec((rows_dev, cut), lambda i, core_ref: (0, i))] * 2,
        ),
        out_shape=[jax.ShapeDtypeStruct((rows_dev, columns_dev), jnp.bfloat16)] * 2,
        cost_estimate=pl.CostEstimate(flops=0, bytes_accessed=2**18, transcendentals=0),
        name="split",
    )(core.reshape(1), kv_weight, kv_weight)
    taken = swap_core(give)
    def swap_tokens(tied):
        return swap_core(lax.optimization_barrier((prompt_states, tied))[0])

    def square_sums(tied):
        states, _ = lax.optimization_barrier((prompt_states, tied))
        return pl.pallas_call(
            square_kernel,
            grid=(8,),
            in_specs=[pl.BlockSpec((tokens // 8, width), lambda i: (i, 0))],
            out_specs=pl.BlockSpec((tokens // 8, 1), lambda i: (i, 0)),
            out_shape=jax.ShapeDtypeStruct((tokens, 1), jnp.float32),
            cost_estimate=pl.CostEstimate(flops=0, bytes_accessed=2**18, transcendentals=0),
            compiler_params=pltpu.CompilerParams(vmem_limit_bytes=60 * 2**20),
            name="squares",
        )(pltpu.with_memory_space_constraint(states, pltpu.HBM))[:, 0]

    def swap_small(squares):
        places = jnp.concatenate([image_owner, image_row]).astype(jnp.float32)
        small = jnp.concatenate([squares, places])
        small = jnp.pad(small, (0, -small.shape[0] % (8 * HD))).reshape(-1, HD)
        got = swap_core(small).reshape(-1)
        factor = jnp.concatenate([squares, got[:tokens]])[:, None]
        at = tokens + images
        owners = jnp.concatenate([image_owner, got[tokens:at].astype(jnp.int32)])
        rows = jnp.concatenate([image_row, got[at : at + images].astype(jnp.int32)])
        return factor, owners, rows

    query_halves = queries.reshape(decode_rows, 2, HALF_QH * HD)
    keep_q = jnp.where(core == 0, query_halves[:, 0], query_halves[:, 1])
    give_q = jnp.where(core == 0, query_halves[:, 1], query_halves[:, 0])

    def place_images(all_q, owners, rows, chip_place):
        chip_of = jnp.sum(
            jnp.where(owners[:, None] // 2 == jnp.arange(n // 2)[None, :], chip_place[None, :], 0), axis=1
        )
        target = chip_of * (2 * decode_rows) + (owners % 2 ^ core) * decode_rows + rows
        pick = (target[:, None] == jnp.arange(n * decode_rows)[None, :]).astype(jnp.bfloat16)
        image_q = jnp.dot(pick, all_q, preferred_element_type=jnp.float32).astype(jnp.bfloat16)
        image_q = image_q.reshape(2 * images, HALF_KVH, GROUP, HD).transpose(1, 0, 2, 3)
        which = jnp.concatenate([jnp.full((images,), core), jnp.full((images,), 1 - core)]).astype(jnp.int32)
        return image_q.reshape(HALF_KVH, n_queries, HD), jnp.stack([owners, which, rows])

    def resident(length):
        step_rows = 2
        return pl.pallas_call(
            resident_kernel,
            grid_spec=pltpu.PrefetchScalarGridSpec(
                num_scalar_prefetch=1,
                grid=(decode_rows // step_rows,),
                in_specs=[
                    pl.BlockSpec((step_rows, QH, HD), lambda i, *_: (i, 0, 0)),
                    pl.BlockSpec((step_rows, context, kv_width), lambda i, *_: (i, 0, 0)),
                ],
                out_specs=[
                    pl.BlockSpec((step_rows, QH, HD), lambda i, *_: (i, 0, 0)),
                    whole((QH, HD)),
                    whole((QH, HD)),
                ],
            ),
            out_shape=[
                jax.ShapeDtypeStruct((decode_rows, QH, HD), jnp.float32),
                jax.ShapeDtypeStruct((QH, HD), jnp.float32),
                jax.ShapeDtypeStruct((QH, HD), jnp.float32),
            ],
            compiler_params=pltpu.CompilerParams(vmem_limit_bytes=60 * 2**20),
            cost_estimate=pl.CostEstimate(flops=0, bytes_accessed=2**18, transcendentals=0),
            name="resident",
        )(length, queries.reshape(decode_rows, QH, HD), cache)

    def product(other, blocks, base, count, pieces, carry, name, last=None):
        arrays, layout = [], []
        for index, piece in enumerate(pieces):
            place = index * rows_dev
            for array, start, rows in piece:
                at = [i for i, known in enumerate(arrays) if known is array]
                if not at:
                    arrays.append(array)
                    at = [len(arrays) - 1]
                layout.append((at[0], start, rows, place))
                place += rows
        steps = len(pieces) // count

        def token_spec(k):
            return pl.BlockSpec((tokens, rows_dev), lambda i, block_ref, *_: (0, block_ref[base + count * i + k]))

        anywhere = pl.BlockSpec(memory_space=pl.ANY)
        in_specs = [token_spec(k) for k in range(count)] * 2
        own_tokens = pltpu.with_memory_space_constraint(prompt_states, pltpu.HBM)
        other_tokens = pltpu.with_memory_space_constraint(other, pltpu.HBM)
        inputs = [own_tokens] * count + [other_tokens] * count
        scalars = [blocks]
        scratch = [pltpu.VMEM((len(pieces) * rows_dev, columns_dev), jnp.bfloat16)]
        total = (2 * tokens, columns_dev)
        body = functools.partial(first_kernel, layout, count)
        if carry is not None:
            body = functools.partial(next_kernel, layout, count)
            in_specs = in_specs + [anywhere]
            inputs = inputs + [carry]
            scratch = scratch + [pltpu.VMEM(total, jnp.float32)]
        out_specs, out_shape = whole(total), jax.ShapeDtypeStruct(total, jnp.float32)
        if last is not None:
            image_q, slot, factor = last
            body = functools.partial(last_kernel, layout, count, width)
            scalars = scalars + [slot]
            in_specs = in_specs + [whole((HALF_KVH, n_queries, HD)), whole((2 * tokens, 1))]
            inputs = inputs + [image_q, factor]
            out_specs = whole((n, 3, HALF_QH, HD))
            out_shape = jax.ShapeDtypeStruct((n, 3, HALF_QH, HD), jnp.bfloat16)
            scratch = scratch + [
                pltpu.VMEM(total, jnp.float32),
                pltpu.VMEM((2 * images, HALF_QH, HD), jnp.float32),
                pltpu.VMEM((2 * images, HALF_QH, HD), jnp.float32),
            ]
        return pl.pallas_call(
            body,
            grid_spec=pltpu.PrefetchScalarGridSpec(
                num_scalar_prefetch=len(scalars),
                grid=(steps,),
                in_specs=in_specs + [anywhere] * len(arrays),
                out_specs=out_specs,
                scratch_shapes=scratch + [pltpu.SemaphoreType.DMA((len(layout) + 1,))],
            ),
            out_shape=out_shape,
            compiler_params=pltpu.CompilerParams(vmem_limit_bytes=60 * 2**20),
            cost_estimate=pl.CostEstimate(flops=0, bytes_accessed=2**18, transcendentals=0),
            name=name,
        )(*scalars, *inputs, *arrays)

    if n == 16 and lax.axis_size("replica") == 2:
        table = block_table()
        blocks = jnp.array(table)[lax.axis_index("replica") * 16 + section]

        def starts(*arrays):
            return [[(array, 0, rows_dev)] for array in arrays]

        tie = lax.optimization_barrier

        def both(array):
            return [[(array, half, rows_dev)] for half in (0, rows_dev)]

        own_q = jnp.concatenate([keep_q, swap_core(give_q)], axis=0)
        behind_q, ahead_q, opposite_q = (along_ring(own_q, way) for way in (1, -1, 2))
        a_own_y = across_y(tie((keep, own_q))[0])
        source_a, source_b, behind_q, ahead_q, opposite_q = tie((keep, taken, behind_q, ahead_q, opposite_q))
        a_behind = along_ring(source_a)
        b_behind, b_own_y = along_ring(source_b), across_y(source_b)
        other = swap_tokens((taken, own_q))
        squares = square_sums(taken)

        source, squares, _ = tie((a_behind, squares, a_own_y))
        a_ahead, a_opposite, a_behind_y = across_replica(source), along_ring(source), across_y(source)
        source, squares, _ = tie((b_behind, squares, (b_own_y, a_ahead)))
        b_ahead, b_opposite, b_behind_y = across_replica(source), along_ring(source), across_y(source)
        ones = starts(keep, taken, a_behind, b_behind, a_own_y, b_own_y)
        total = product(other, blocks, 0, 2, ones, None, "rows_1")

        ring_q = jnp.concatenate([own_q, behind_q, ahead_q, opposite_q], axis=0)
        source_y, source, source_q, squares, total, _ = tie(
            (a_behind_y, a_opposite, ring_q, squares, total, b_ahead)
        )
        a_ahead_y, a_opposite_y = across_replica(source_y), across_y(source)
        all_q = jnp.concatenate([ring_q, across_y(source_q)], axis=0)
        source, squares, total, _ = tie((b_behind_y, squares, total, (b_opposite, a_ahead_y)))
        b_ahead_y, b_opposite_y = across_replica(source), along_ring(source)
        factor, owners, rows = swap_small(squares)
        image_q, slot = place_images(all_q, owners, rows, blocks[16:])
        twos = starts(a_ahead, b_ahead, a_opposite, b_opposite, a_behind_y, b_behind_y)
        total = product(other, blocks, 6, 2, twos, total, "rows_2")
        lasts = starts(a_ahead_y, a_opposite_y, b_opposite_y, b_ahead_y)
        slots = product(other, blocks, 12, 2, lasts, total, "rows_3", last=(image_q, slot, factor))
        length, slots = tie((context_length, slots))
        res_out, res_top, res_sum = resident(length)
    else:
        res_out, res_top, res_sum = resident(context_length)
        other = swap_tokens(taken)
        squares = square_sums(taken)
        factor, owners, rows = swap_small(squares)
        chip_q = jnp.concatenate([keep_q, swap_core(give_q)], axis=0)
        groups = [list(range(side, n, 2)) for side in range(2)]
        all_q = lax.all_gather(chip_q, "section", axis=0, tiled=True, axis_index_groups=groups)
        image_q, slot = place_images(all_q, owners, rows, jnp.arange(n // 2))
        a = gather_plain(keep)
        b = gather_plain(taken)
        chips = jnp.array([chip for chip, _, _ in a], jnp.int32)
        total = product(other, chips * 2 + core, 0, 2, [[(array, start, rows_dev)] for _, array, start in a], None, "rows_a")
        slots = product(
            other, chips * 2 + 1 - core, 0, 2, [[(array, start, rows_dev)] for _, array, start in b], total, "rows_b", last=(image_q, slot, factor)
        )
    got = lax.all_to_all(slots, "section", split_axis=0, concat_axis=0, tiled=True)

    return pl.pallas_call(
        combine_kernel,
        grid=(1,),
        in_specs=[
            whole((n, 3, HALF_QH, HD)),
            whole((decode_rows, QH, HD)),
            whole((QH, HD)),
            whole((QH, HD)),
        ],
        out_specs=whole((decode_rows, QH * HD)),
        scratch_shapes=[pltpu.VMEM((decode_rows, QH, HD), jnp.float32)],
        out_shape=jax.ShapeDtypeStruct((decode_rows, QH * HD), jnp.bfloat16),
        compiler_params=pltpu.CompilerParams(vmem_limit_bytes=60 * 2**20),
        name="combine",
    )(got, res_out, res_top, res_sum)


def solution(mesh):
    placed = (
        P(("replica", "section"), None),
        P("section", None),
        P(("replica", "section")),
        P(("replica", "section")),
        P(("replica", "section"), None),
        P(("replica", "section"), None, None),
        P(("replica", "section")),
    )
    return jax.shard_map(
        per_device,
        mesh=mesh,
        in_specs=placed,
        out_specs=P(("replica", "section"), None),
        check_vma=False,
    )
```

```python
import functools
import math

import jax
import jax.numpy as jnp
import numpy as np
from jax import lax
from jax.experimental import pallas as pl
from jax.experimental.pallas import tpu as pltpu
from jax.sharding import PartitionSpec as P

HD = 128
KVH = 4
QH = 32
IMG_TOK = 64
GROUP = QH // KVH
HALF_KVH = KVH // 2
HALF_QH = QH // 2
SCALE = 1.0 / math.sqrt(HD)
EPS = 1e-05

LANES = 64
N_KINDS = 7

masked_score = -1e30


def swap_core(x):
    n = lax.axis_size("section")
    return lax.ppermute(x, "section", [(i, i ^ 1) for i in range(n)])


def gather_plain(chunk):
    n = lax.axis_size("section")
    rows = chunk.shape[0]
    groups = [list(range(core, n, 2)) for core in range(2)]
    whole = lax.all_gather(chunk, "section", axis=0, tiled=True, axis_index_groups=groups)
    return [(chip, whole, chip * rows) for chip in range(n // 2)]


RING = [0, 1, 3, 2]


def along_ring(x, sign=1):
    perm = []
    for rep, way in ((0, sign), (1, -sign)):
        for p in range(4):
            for low in range(4):
                perm.append((rep * 16 + RING[p] * 4 + low, rep * 16 + RING[(p + way) % 4] * 4 + low))
    return lax.ppermute(x, ("replica", "section"), perm)


def across_y(x):
    return lax.ppermute(x, "section", [(i, i ^ 2) for i in range(16)])


def across_replica(x):
    return lax.ppermute(x, "replica", [(0, 1), (1, 0)])


STEPS = (("own", "behind", "own_y"), ("ahead", "opposite", "behind_y"), ("ahead_y", "opposite_y"))


def block_table():
    table = []
    for rep in range(2):
        for section in range(16):
            z, y, core = section // 4, section // 2 % 2, section % 2
            way = 1 - 2 * rep
            place = RING.index(z)
            ring = {"own": place, "behind": place - way, "ahead": place + way, "opposite": place + 2}

            def blocks(step, other):
                out = []
                for name in STEPS[step]:
                    chip = RING[ring[name.removesuffix("_y")] % 4] * 2 + (1 - y if name.endswith("_y") else y)
                    out.append(chip * 2 + (core ^ other))
                return out

            def both(step):
                return [block for pair in zip(blocks(step, 0), blocks(step, 1)) for block in pair]

            three = both(2)
            places = [0] * 8
            for i, name in enumerate(("own", "behind", "ahead", "opposite")):
                chip = RING[ring[name] % 4] * 2
                places[chip + y], places[chip + 1 - y] = i, 4 + i
            table.append(both(0) + both(1) + [three[0], three[2], three[3], three[1]] + places)
    return np.array(table, np.int32)


def square_kernel(states_ref, out_ref):
    total = None
    for i in range(0, states_ref.shape[1], HD):
        values = states_ref[:, i : i + HD].astype(jnp.float32)
        values = values * values
        total = values if total is None else total + values
    out_ref[...] = jnp.sum(total, axis=1, keepdims=True)


def split_kernel(core_ref, keep_in, give_in, keep_ref, give_ref):
    keep_ref[...] = keep_in[...]
    give_ref[...] = give_in[...]


def accumulate(layout, token_refs, piece_refs, weight, total, sems, carry_ref=None, carry=None):
    step = pl.program_id(0)
    rows = token_refs[0].shape[1]
    count = len(token_refs) // 2
    depth = count * rows
    copies = [
        pltpu.make_async_copy(
            piece_refs[which].at[pl.ds(start, size)], weight.at[pl.ds(place, size)], sems.at[i]
        )
        for i, (which, start, size, place) in enumerate(layout)
    ]
    carried = []
    if carry_ref is not None:
        carried = [pltpu.make_async_copy(carry_ref, carry, sems.at[len(layout)])]

    @pl.when(step == 0)
    def _():
        for copy in copies + carried:
            copy.start()

    for i in range(weight.shape[0] // depth):

        @pl.when(step == i)
        def _():
            for copy, (_, _, _, place) in zip(copies, layout):
                if place // depth == i:
                    copy.wait()

    states = jnp.concatenate(
        [
            jnp.concatenate([ref[...] for ref in token_refs[side * count : (side + 1) * count]], axis=1)
            for side in range(2)
        ],
        axis=0,
    )
    block = weight[pl.ds(pl.multiple_of(step * depth, depth), depth), :]
    product = jnp.dot(states, block, preferred_element_type=jnp.float32)

    @pl.when(step == 0)
    def _():
        total[...] = product

    @pl.when(step > 0)
    def _():
        total[...] += product

    if carry_ref is not None:

        @pl.when(step == pl.num_programs(0) - 1)
        def _():
            carried[0].wait()
            total[...] += carry[...]


def first_kernel(layout, count, block_ref, *refs):
    total, weight, sems = refs[-3:]
    accumulate(layout, refs[: 2 * count], refs[2 * count : -3], weight, total, sems)


def next_kernel(layout, count, block_ref, *refs):
    total, weight, carry, sems = refs[-4:]
    token_refs, (carry_ref, *piece_refs) = refs[: 2 * count], refs[2 * count : -4]
    accumulate(layout, token_refs, piece_refs, weight, total, sems, carry_ref, carry)


def parts_of(values, count):
    out = []
    for _ in range(count):
        part = values.astype(jnp.bfloat16).astype(jnp.float32)
        out.append(part)
        values = values - part
    return out


def last_kernel(layout, count, width, block_ref, slot_ref, *refs):
    token_refs, (carry_ref, query_ref, factor_ref, *piece_refs) = refs[: 2 * count], refs[2 * count : -7]
    slots_ref, weight, carry, total, summed, stats, sems = refs[-7:]
    images = query_ref.shape[1] // GROUP

    @pl.when(pl.program_id(0) == 0)
    def _():
        slots_ref[...] = jnp.zeros_like(slots_ref)

    accumulate(layout, token_refs, piece_refs, weight, total, sems, carry_ref, carry)

    @pl.when(pl.program_id(0) == pl.num_programs(0) - 1)
    def _():
        tokens = total.shape[0]
        queries = query_ref.shape[1]
        factor = lax.rsqrt(factor_ref[...] / width + EPS)
        image_of_query = lax.broadcasted_iota(jnp.int32, (queries, tokens), 0) // GROUP
        image_of_token = lax.broadcasted_iota(jnp.int32, (queries, tokens), 1) // IMG_TOK
        live = image_of_query == image_of_token
        lane = lax.broadcasted_iota(jnp.int32, (queries, HD), 1)
        for head in range(HALF_KVH):
            part = slice(head * GROUP, (head + 1) * GROUP)
            keys = (total[:, head * HD : (head + 1) * HD] * factor).astype(jnp.bfloat16)
            at = (HALF_KVH + head) * HD
            values = (total[:, at : at + HD] * factor).astype(jnp.bfloat16)
            scores = (
                lax.dot_general(
                    query_ref[head], keys, (((1,), (1,)), ((), ())), preferred_element_type=jnp.float32
                )
                * SCALE
            )
            scores = jnp.where(live, scores, masked_score)
            top = jnp.max(scores, axis=1, keepdims=True)
            weights = jnp.where(live, jnp.exp(scores - top), 0.0)
            total_weight = jnp.sum(weights, axis=1, keepdims=True)
            out = jnp.dot(weights.astype(jnp.bfloat16), values, preferred_element_type=jnp.float32)
            summed[:, part, :] = out.reshape(images, GROUP, HD)
            kinds = parts_of(top, 3) + parts_of(total_weight, 3) + [jnp.ones_like(top)]
            tile = jnp.zeros((queries, HD), jnp.float32)
            for kind, column in enumerate(kinds):
                tile = jnp.where(lane == kind * 8, column, tile)
            stats[:, part, :] = tile.reshape(images, GROUP, HD)
        for image in range(images):
            owner, which = slot_ref[0, image], slot_ref[1, image]
            slots_ref[owner, which] = summed[image].astype(jnp.bfloat16)
            tile = pltpu.roll(stats[image], which * LANES + slot_ref[2, image], 1)
            slots_ref[owner, 2] = slots_ref[owner, 2] + tile.astype(jnp.bfloat16)


def resident_kernel(length_ref, query_ref, cache_ref, out_ref, top_ref, sum_ref):
    step = pl.program_id(0)
    rows, context = cache_ref.shape[:2]
    place = lax.broadcasted_iota(jnp.int32, (QH, context), 1)
    lane = lax.broadcasted_iota(jnp.int32, (QH, HD), 1)

    @pl.when(step == 0)
    def _():
        top_ref[...] = jnp.zeros_like(top_ref)
        sum_ref[...] = jnp.zeros_like(sum_ref)

    parts = [slice(head * GROUP, (head + 1) * GROUP) for head in range(KVH)]
    scores = [
        jnp.concatenate(
            [
                lax.dot_general(
                    query_ref[row, part, :],
                    cache_ref[row, :, head * HD : (head + 1) * HD],
                    (((1,), (1,)), ((), ())),
                    preferred_element_type=jnp.float32,
                )
                for head, part in enumerate(parts)
            ],
            axis=0,
        )
        for row in range(rows)
    ]
    for row in range(rows):
        live = place < length_ref[step * rows + row]
        score = jnp.where(live, scores[row] * SCALE, masked_score)
        top = jnp.max(score, axis=1, keepdims=True)
        weights = jnp.where(live, jnp.exp(score - top), 0.0)
        mine = lane == step * rows + row
        top_ref[...] = jnp.where(mine, top, top_ref[...])
        sum_ref[...] = jnp.where(mine, jnp.sum(weights, axis=1, keepdims=True), sum_ref[...])
        weights = weights.astype(jnp.bfloat16)
        for head, part in enumerate(parts):
            at = (KVH + head) * HD
            out_ref[row, part, :] = jnp.dot(
                weights[part], cache_ref[row, :, at : at + HD], preferred_element_type=jnp.float32
            )


def combine_kernel(got_ref, res_out_ref, res_top_ref, res_sum_ref, out_ref, acc):
    chips = got_ref.shape[0] // 2
    rows = res_out_ref.shape[0]
    lane = lax.broadcasted_iota(jnp.int32, (HALF_QH, HD), 1)
    head_lane = (lane % LANES) < 8

    def moved(tile, by):
        return pltpu.roll(tile, HD - by, 1)

    for core in range(2):
        part = slice(core * HALF_QH, (core + 1) * HALF_QH)
        tops, sums, here = [], [], []
        for chip in range(chips):
            tile = got_ref[chip * 2 + core, 2].astype(jnp.float32)
            present = (moved(tile, 48) > 0.5) & head_lane
            tops.append(jnp.where(present, tile + moved(tile, 8) + moved(tile, 16), masked_score))
            sums.append(moved(tile, 24) + moved(tile, 32) + moved(tile, 40))
            here.append(present)
        row_top = functools.reduce(jnp.maximum, tops)
        row_top = jnp.maximum(row_top, pltpu.roll(row_top, LANES, 1))
        res_top = jnp.where(lane < 8, res_top_ref[part, :], masked_score)
        res_top = jnp.maximum(res_top, pltpu.roll(res_top, LANES, 1))
        row_top = jnp.maximum(row_top, res_top)
        weights = [jnp.where(a, jnp.exp(t - row_top), 0.0) for a, t in zip(here, tops)]
        joined = sum(w * s for w, s in zip(weights, sums))
        res_weight = jnp.exp(res_top - row_top)
        denominator = joined + pltpu.roll(joined, LANES, 1) + res_weight * res_sum_ref[part, :]
        scale = jnp.where(lane < 8, 1.0 / denominator, 0.0)
        scale = scale + pltpu.roll(scale, LANES, 1)
        res_share = res_weight * scale
        weights = [w * scale for w in weights]
        for row in range(rows):
            value = res_out_ref[row, part, :] * res_share[:, row : row + 1]
            for chip in range(chips):
                for which in range(2):
                    at = which * LANES + row
                    value += weights[chip][:, at : at + 1] * got_ref[chip * 2 + core, which].astype(jnp.float32)
            acc[row, part, :] = value
    for head in range(QH):
        out_ref[:, head * HD : (head + 1) * HD] = acc[:, head, :].astype(jnp.bfloat16)


def whole(shape):
    return pl.BlockSpec(shape, lambda i, *_: (0,) * len(shape))


def per_device(prompt_states, kv_weight, image_owner, image_row, queries, cache, context_length):
    n = lax.axis_size("section")
    section = lax.axis_index("section")
    core = section % 2
    tokens, width = prompt_states.shape
    rows_dev, kv_width = kv_weight.shape
    columns_dev = kv_width // 2
    images = image_owner.shape[0]
    decode_rows = queries.shape[0]
    context = cache.shape[1]
    n_queries = 2 * images * GROUP

    cut = columns_dev // 2
    keep, give = pl.pallas_call(
        split_kernel,
        grid_spec=pltpu.PrefetchScalarGridSpec(
            num_scalar_prefetch=1,
            grid=(2,),
            in_specs=[
                pl.BlockSpec((rows_dev, cut), lambda i, core_ref: (0, 2 * i + core_ref[0])),
                pl.BlockSpec((rows_dev, cut), lambda i, core_ref: (0, 2 * i + 1 - core_ref[0])),
            ],
            out_specs=[pl.BlockSpec((rows_dev, cut), lambda i, core_ref: (0, i))] * 2,
        ),
        out_shape=[jax.ShapeDtypeStruct((rows_dev, columns_dev), jnp.bfloat16)] * 2,
        cost_estimate=pl.CostEstimate(flops=0, bytes_accessed=2**18, transcendentals=0),
        name="split",
    )(core.reshape(1), kv_weight, kv_weight)
    taken = swap_core(give)
    def swap_tokens(tied):
        return swap_core(lax.optimization_barrier((prompt_states, tied))[0])

    def square_sums(tied):
        states, _ = lax.optimization_barrier((prompt_states, tied))
        return pl.pallas_call(
            square_kernel,
            grid=(8,),
            in_specs=[pl.BlockSpec((tokens // 8, width), lambda i: (i, 0))],
            out_specs=pl.BlockSpec((tokens // 8, 1), lambda i: (i, 0)),
            out_shape=jax.ShapeDtypeStruct((tokens, 1), jnp.float32),
            cost_estimate=pl.CostEstimate(flops=0, bytes_accessed=2**18, transcendentals=0),
            compiler_params=pltpu.CompilerParams(vmem_limit_bytes=60 * 2**20),
            name="squares",
        )(pltpu.with_memory_space_constraint(states, pltpu.HBM))[:, 0]

    def swap_small(squares):
        places = jnp.concatenate([image_owner, image_row]).astype(jnp.float32)
        small = jnp.concatenate([squares, places])
        small = jnp.pad(small, (0, -small.shape[0] % (8 * HD))).reshape(-1, HD)
        got = swap_core(small).reshape(-1)
        factor = jnp.concatenate([squares, got[:tokens]])[:, None]
        at = tokens + images
        owners = jnp.concatenate([image_owner, got[tokens:at].astype(jnp.int32)])
        rows = jnp.concatenate([image_row, got[at : at + images].astype(jnp.int32)])
        return factor, owners, rows

    query_halves = queries.reshape(decode_rows, 2, HALF_QH * HD)
    keep_q = jnp.where(core == 0, query_halves[:, 0], query_halves[:, 1])
    give_q = jnp.where(core == 0, query_halves[:, 1], query_halves[:, 0])

    def place_images(all_q, owners, rows, chip_place):
        chip_of = jnp.sum(
            jnp.where(owners[:, None] // 2 == jnp.arange(n // 2)[None, :], chip_place[None, :], 0), axis=1
        )
        target = chip_of * (2 * decode_rows) + (owners % 2 ^ core) * decode_rows + rows
        pick = (target[:, None] == jnp.arange(n * decode_rows)[None, :]).astype(jnp.bfloat16)
        image_q = jnp.dot(pick, all_q, preferred_element_type=jnp.float32).astype(jnp.bfloat16)
        image_q = image_q.reshape(2 * images, HALF_KVH, GROUP, HD).transpose(1, 0, 2, 3)
        which = jnp.concatenate([jnp.full((images,), core), jnp.full((images,), 1 - core)]).astype(jnp.int32)
        return image_q.reshape(HALF_KVH, n_queries, HD), jnp.stack([owners, which, rows])

    def resident(length):
        step_rows = 2
        return pl.pallas_call(
            resident_kernel,
            grid_spec=pltpu.PrefetchScalarGridSpec(
                num_scalar_prefetch=1,
                grid=(decode_rows // step_rows,),
                in_specs=[
                    pl.BlockSpec((step_rows, QH, HD), lambda i, *_: (i, 0, 0)),
                    pl.BlockSpec((step_rows, context, kv_width), lambda i, *_: (i, 0, 0)),
                ],
                out_specs=[
                    pl.BlockSpec((step_rows, QH, HD), lambda i, *_: (i, 0, 0)),
                    whole((QH, HD)),
                    whole((QH, HD)),
                ],
            ),
            out_shape=[
                jax.ShapeDtypeStruct((decode_rows, QH, HD), jnp.float32),
                jax.ShapeDtypeStruct((QH, HD), jnp.float32),
                jax.ShapeDtypeStruct((QH, HD), jnp.float32),
            ],
            compiler_params=pltpu.CompilerParams(vmem_limit_bytes=60 * 2**20),
            cost_estimate=pl.CostEstimate(flops=0, bytes_accessed=2**18, transcendentals=0),
            name="resident",
        )(length, queries.reshape(decode_rows, QH, HD), cache)

    def product(other, blocks, base, count, pieces, carry, name, last=None):
        arrays, layout = [], []
        for index, piece in enumerate(pieces):
            place = index * rows_dev
            for array, start, rows in piece:
                at = [i for i, known in enumerate(arrays) if known is array]
                if not at:
                    arrays.append(array)
                    at = [len(arrays) - 1]
                layout.append((at[0], start, rows, place))
                place += rows
        steps = len(pieces) // count

        def token_spec(k):
            return pl.BlockSpec((tokens, rows_dev), lambda i, block_ref, *_: (0, block_ref[base + count * i + k]))

        anywhere = pl.BlockSpec(memory_space=pl.ANY)
        in_specs = [token_spec(k) for k in range(count)] * 2
        own_tokens = pltpu.with_memory_space_constraint(prompt_states, pltpu.HBM)
        other_tokens = pltpu.with_memory_space_constraint(other, pltpu.HBM)
        inputs = [own_tokens] * count + [other_tokens] * count
        scalars = [blocks]
        scratch = [pltpu.VMEM((len(pieces) * rows_dev, columns_dev), jnp.bfloat16)]
        total = (2 * tokens, columns_dev)
        body = functools.partial(first_kernel, layout, count)
        if carry is not None:
            body = functools.partial(next_kernel, layout, count)
            in_specs = in_specs + [anywhere]
            inputs = inputs + [carry]
            scratch = scratch + [pltpu.VMEM(total, jnp.float32)]
        out_specs, out_shape = whole(total), jax.ShapeDtypeStruct(total, jnp.float32)
        if last is not None:
            image_q, slot, factor = last
            body = functools.partial(last_kernel, layout, count, width)
            scalars = scalars + [slot]
            in_specs = in_specs + [whole((HALF_KVH, n_queries, HD)), whole((2 * tokens, 1))]
            inputs = inputs + [image_q, factor]
            out_specs = whole((n, 3, HALF_QH, HD))
            out_shape = jax.ShapeDtypeStruct((n, 3, HALF_QH, HD), jnp.bfloat16)
            scratch = scratch + [
                pltpu.VMEM(total, jnp.float32),
                pltpu.VMEM((2 * images, HALF_QH, HD), jnp.float32),
                pltpu.VMEM((2 * images, HALF_QH, HD), jnp.float32),
            ]
        return pl.pallas_call(
            body,
            grid_spec=pltpu.PrefetchScalarGridSpec(
                num_scalar_prefetch=len(scalars),
                grid=(steps,),
                in_specs=in_specs + [anywhere] * len(arrays),
                out_specs=out_specs,
                scratch_shapes=scratch + [pltpu.SemaphoreType.DMA((len(layout) + 1,))],
            ),
            out_shape=out_shape,
            compiler_params=pltpu.CompilerParams(vmem_limit_bytes=60 * 2**20),
            cost_estimate=pl.CostEstimate(flops=0, bytes_accessed=2**18, transcendentals=0),
            name=name,
        )(*scalars, *inputs, *arrays)

    if n == 16 and lax.axis_size("replica") == 2:
        table = block_table()
        blocks = jnp.array(table)[lax.axis_index("replica") * 16 + section]

        def starts(*arrays):
            return [[(array, 0, rows_dev)] for array in arrays]

        tie = lax.optimization_barrier

        def both(array):
            return [[(array, half, rows_dev)] for half in (0, rows_dev)]

        own_q = jnp.concatenate([keep_q, swap_core(give_q)], axis=0)
        behind_q, ahead_q, opposite_q = (along_ring(own_q, way) for way in (1, -1, 2))
        a_own_y = across_y(tie((keep, own_q))[0])
        a_behind = along_ring(tie((keep, own_q))[0])
        source_b, behind_q, ahead_q, opposite_q = tie((taken, behind_q, ahead_q, opposite_q))
        b_behind, b_own_y = along_ring(source_b), across_y(source_b)
        other = swap_tokens((taken, own_q))
        squares = square_sums(a_behind)

        source, _ = tie((a_behind, a_own_y))
        a_ahead, a_opposite, a_behind_y = across_replica(source), along_ring(source), across_y(source)
        source, squares, _ = tie((b_behind, squares, (b_own_y, a_ahead)))
        b_ahead, b_opposite, b_behind_y = across_replica(source), along_ring(source), across_y(source)
        ones = starts(keep, taken, a_behind, b_behind, a_own_y, b_own_y)
        total = product(other, blocks, 0, 2, ones, None, "rows_1")

        ring_q = jnp.concatenate([own_q, behind_q, ahead_q, opposite_q], axis=0)
        source_y, source, source_q, squares, total, _ = tie(
            (a_behind_y, a_opposite, ring_q, squares, total, b_ahead)
        )
        a_ahead_y, a_opposite_y = across_replica(source_y), across_y(source)
        all_q = jnp.concatenate([ring_q, across_y(source_q)], axis=0)
        source, squares, total, _ = tie((b_behind_y, squares, total, (b_opposite, a_ahead_y)))
        b_ahead_y, b_opposite_y = across_replica(source), along_ring(source)
        factor, owners, rows = swap_small(squares)
        image_q, slot = place_images(all_q, owners, rows, blocks[16:])
        twos = starts(a_ahead, b_ahead, a_opposite, b_opposite, a_behind_y, b_behind_y)
        total = product(other, blocks, 6, 2, twos, total, "rows_2")
        lasts = starts(a_ahead_y, a_opposite_y, b_opposite_y, b_ahead_y)
        slots = product(other, blocks, 12, 2, lasts, total, "rows_3", last=(image_q, slot, factor))
        length, slots = tie((context_length, slots))
        res_out, res_top, res_sum = resident(length)
    else:
        res_out, res_top, res_sum = resident(context_length)
        other = swap_tokens(taken)
        squares = square_sums(taken)
        factor, owners, rows = swap_small(squares)
        chip_q = jnp.concatenate([keep_q, swap_core(give_q)], axis=0)
        groups = [list(range(side, n, 2)) for side in range(2)]
        all_q = lax.all_gather(chip_q, "section", axis=0, tiled=True, axis_index_groups=groups)
        image_q, slot = place_images(all_q, owners, rows, jnp.arange(n // 2))
        a = gather_plain(keep)
        b = gather_plain(taken)
        chips = jnp.array([chip for chip, _, _ in a], jnp.int32)
        total = product(other, chips * 2 + core, 0, 2, [[(array, start, rows_dev)] for _, array, start in a], None, "rows_a")
        slots = product(
            other, chips * 2 + 1 - core, 0, 2, [[(array, start, rows_dev)] for _, array, start in b], total, "rows_b", last=(image_q, slot, factor)
        )
    got = lax.all_to_all(slots, "section", split_axis=0, concat_axis=0, tiled=True)

    return pl.pallas_call(
        combine_kernel,
        grid=(1,),
        in_specs=[
            whole((n, 3, HALF_QH, HD)),
            whole((decode_rows, QH, HD)),
            whole((QH, HD)),
            whole((QH, HD)),
        ],
        out_specs=whole((decode_rows, QH * HD)),
        scratch_shapes=[pltpu.VMEM((decode_rows, QH, HD), jnp.float32)],
        out_shape=jax.ShapeDtypeStruct((decode_rows, QH * HD), jnp.bfloat16),
        compiler_params=pltpu.CompilerParams(vmem_limit_bytes=60 * 2**20),
        name="combine",
    )(got, res_out, res_top, res_sum)


def solution(mesh):
    placed = (
        P(("replica", "section"), None),
        P("section", None),
        P(("replica", "section")),
        P(("replica", "section")),
        P(("replica", "section"), None),
        P(("replica", "section"), None, None),
        P(("replica", "section")),
    )
    return jax.shard_map(
        per_device,
        mesh=mesh,
        in_specs=placed,
        out_specs=P(("replica", "section"), None),
        check_vma=False,
    )
```
